32 devices in a mesh: groups: 2 (over y), slab: 8 (over z, x), vec: 2 (over core).
Axes of the slice: x: 2, y: 2, z: 4, core: 2. Of those that a mesh axis runs over, the one named last changes fastest.
Arguments:
- vectors: bfloat16 [64, 64, 512], P(('groups', 'slab'), None, 'vec'), parts along dimension 0, may hold values from -18 to 18
- blocks: bfloat16 [32, 512, 512], P('groups', None, 'vec'), parts along dimension 0, may hold values from -2 to 4
- slab_blocks: int32 [64, 3], P(('groups', 'slab')), parts along dimension 0, may hold values from 0 to 15
- far_source: int32 [64, 4], P(('groups', 'slab')), parts along dimension 0, may hold values from 0 to 31, as said below
- far_block: int32 [64, 4], P(('groups', 'slab')), parts along dimension 0, may hold values from 0 to 15
- level_lower: bfloat16 [6, 64, 512, 512], P(None, ('groups', 'slab'), None, 'vec'), parts along dimension 1, may hold values from -0.125 to 0.125
- level_upper: bfloat16 [6, 64, 512, 512], P(None, ('groups', 'slab'), None, 'vec'), parts along dimension 1, may hold values from -0.125 to 0.125
- level_final: bfloat16 [64, 512, 512], P(('groups', 'slab'), None, 'vec'), parts along dimension 0, may hold values from -0.0625 to 0.0625
- shift_levels: float32 [16], P('groups'), parts along dimension 0, may hold values from 0.5 to 2.5
- shift_index: int32 [2], P('groups'), parts along dimension 0, may hold values from 0 to 7
Outputs:
- correction: bfloat16 [64, 64, 512], P(('groups', 'slab'), None, 'vec'), parts along dimension 0
- gram: float32 [256, 128], P('groups'), parts along dimension 0
- pencil: float32 [256, 128], P('groups'), parts along dimension 0
The draws below stay inside these ranges and needn't reach their ends.
There are 2 independent parts, one for each index of `groups`. The reference program is written for one: setup_inputs(seed, part) draws one part's arguments, and reference() takes and returns one part's arrays. A program takes and returns all parts, laid end to end along the dimension named above; each array names one. Nothing has to cross between parts.
Inputs may be any that keep to these rules, and one draw needn't show every extreme that they name: `far_source`: each of the 4 source slabs of slab t lies at most 4 slabs from t, and the first lies exactly 4 slabs away.
All inputs are finite; a program needn't handle non-finite values.
Results may differ from the reference program's by a relative error of at most 0.018.
Values may be sent and summed in bfloat16 or wider, within the bound.
No kernel may reach another device: no remote copies, remote signals or barrier semaphores. Data moves between devices by JAX's collectives and lax.ppermute only.
A program may use at most 128 MiB of HBM per device.

```python
import jax
import jax.numpy as jnp
from jax import lax

B = 512
K = 64
SLABS_DEV = 4
LEVELS = 6
FAR = 4
NBLK = 16
NSHIFT = 8
SLABS = 32


def draw_vectors(key, part):
    key = jax.random.fold_in(key, 5)
    position = jnp.arange(SLABS, dtype=jnp.float32) / max(SLABS - 1, 1)
    noise = jnp.clip(jax.random.normal(key, (SLABS, K, B), jnp.float32), -6.0, 6.0)
    factor = 1.0 + 2.0 * position
    return (noise * factor[:, None, None]).astype(jnp.bfloat16)


def draw_blocks(key, part):
    key = jax.random.fold_in(key, 11)
    first_key, second_key = jax.random.split(key)
    noise = jnp.clip(jax.random.normal(first_key, (NBLK, B, B), jnp.float32), -6.0, 6.0)
    energy = jax.random.uniform(second_key, (NBLK, B), jnp.float32, 0.5, 2.5)
    diagonal = (jnp.arange(B)[:, None] == jnp.arange(B)[None, :]).astype(jnp.float32)
    return (noise / B ** 0.5 + energy[:, :, None] * diagonal[None]).astype(jnp.bfloat16)


def draw_far_source(key, part):
    key = jax.random.fold_in(key, 7)
    slab_ids = jnp.arange(SLABS, dtype=jnp.int32)[:, None]
    offsets = jax.random.randint(key, (SLABS, FAR), -SLABS_DEV, SLABS_DEV + 1, dtype=jnp.int32)
    leading = jnp.where(slab_ids >= SLABS_DEV, -SLABS_DEV, SLABS_DEV).astype(jnp.int32)
    offsets = jnp.concatenate([leading, offsets[:, 1:]], 1)
    return jnp.clip(slab_ids + offsets, 0, SLABS - 1).astype(jnp.int32)


def draw_shift_levels(key, part):
    key = jax.random.fold_in(key, 13)
    order_key, jitter_key = jax.random.split(key)
    order = jax.random.permutation(order_key, NSHIFT).astype(jnp.float32)
    jitter = jax.random.uniform(jitter_key, (NSHIFT,), jnp.float32, 0.0, 0.1)
    return (0.5 + 0.25 * order + jitter).astype(jnp.float32)


def set_ends(values, own_key, low, top_value):
    shape = values.shape
    index_at = [jax.random.randint(jax.random.fold_in(own_key, axis), (), 0, shape[axis]) for axis in range(len(shape))]
    values = values.at[tuple(index_at)].set(low)
    longest = shape.index(max(shape))
    index_at[longest] = (index_at[longest] + 1) % shape[longest]
    return values.at[tuple(index_at)].set(top_value)


def steps_of(key, dims, cuts, smallest, high):
    gain, own = 1.0, jax.random.fold_in(key, 6)
    for dim, blocks in cuts:
        heights = jnp.exp(jax.random.uniform(jax.random.fold_in(own, dim), (blocks,), jnp.float32, smallest / len(cuts), high / len(cuts)))
        gain = gain * jnp.repeat(heights, dims[dim] // blocks).reshape([-1 if axis == dim else 1 for axis in range(len(dims))])
    return gain


def centred(stream_key, dims, spread, limit, pieces=(), kind=jnp.bfloat16):
    values = jax.random.normal(stream_key, dims, jnp.float32) * spread
    if len(pieces) > 0:
        values = steps_of(stream_key, dims, pieces, -0.22, 0.18) * values
    return jnp.clip(values, min=-limit, max=limit).astype(kind)


def setup_inputs(seed: int = 0, part: int = 0) -> dict:
    key_list = jax.random.split(jax.random.key(seed), 11)
    part_keys = jax.random.split(jax.random.fold_in(key_list[10], part), 11)
    vectors = draw_vectors(jax.random.fold_in(jax.random.fold_in(key_list[10], part), 71), part)
    blocks = draw_blocks(jax.random.fold_in(jax.random.fold_in(key_list[10], part), 71), part)
    slab_blocks = set_ends(jax.random.randint(part_keys[2], (SLABS, 3), 0, NBLK), jax.random.fold_in(part_keys[2], 1), 0, NBLK - 1).astype(jnp.int32)
    far_source = draw_far_source(jax.random.fold_in(jax.random.fold_in(key_list[10], part), 71), part)
    far_block = set_ends(jax.random.randint(part_keys[4], (SLABS, FAR), 0, NBLK), jax.random.fold_in(part_keys[4], 1), 0, NBLK - 1).astype(jnp.int32)
    level_lower = centred(part_keys[5], (LEVELS, SLABS, B, B), (4 * B) ** -0.5, 0.125, ((1, 8), (3, 2)))
    level_upper = centred(part_keys[6], (LEVELS, SLABS, B, B), (4 * B) ** -0.5, 0.125, ((1, 8), (3, 2)))
    level_final = centred(part_keys[7], (SLABS, B, B), (16 * B) ** -0.5, 0.0625, ((0, 8), (2, 2)))
    shift_levels = draw_shift_levels(jax.random.fold_in(jax.random.fold_in(key_list[10], part), 71), part)
    shift_index = jax.random.randint(part_keys[9], (1,), 0, NSHIFT).astype(jnp.int32)
    return dict(vectors=vectors, blocks=blocks, slab_blocks=slab_blocks, far_source=far_source, far_block=far_block, level_lower=level_lower, level_upper=level_upper, level_final=level_final, shift_levels=shift_levels, shift_index=shift_index)


def slabwise(left, right):
    return lax.map(lambda pair: jnp.dot(pair[0], pair[1], preferred_element_type=jnp.float32), (left, right))


def apply_operator(vectors, blocks, slab_blocks, far_source, far_block):
    padded = jnp.pad(vectors, ((SLABS_DEV, SLABS_DEV), (0, 0), (0, 0)))

    def one_slab(slab):
        block_ids = slab_blocks[slab]
        summed = jnp.zeros((K, B), jnp.float32)
        for offset_index in range(3):
            summed = summed + jnp.dot(padded[slab + SLABS_DEV - 1 + offset_index], blocks[block_ids[offset_index]], preferred_element_type=jnp.float32)
        for entry in range(FAR):
            summed = summed + jnp.dot(padded[far_source[slab, entry] + SLABS_DEV], blocks[far_block[slab, entry]], preferred_element_type=jnp.float32)
        return summed

    return lax.map(one_slab, jnp.arange(SLABS, dtype=jnp.int32)).astype(jnp.bfloat16)


def shifted(values, stride):
    if abs(stride) >= SLABS:
        return jnp.zeros_like(values)
    zeros = jnp.zeros((abs(stride),) + values.shape[1:], values.dtype)
    if stride > 0:
        return jnp.concatenate([zeros, values[:-stride]], 0)
    return jnp.concatenate([values[-stride:], zeros], 0)


def reference(vectors, blocks, slab_blocks, far_source, far_block, level_lower, level_upper, level_final, shift_levels, shift_index):
    rows_total = SLABS * B
    highest = lax.Precision.HIGHEST
    image = apply_operator(vectors, blocks, slab_blocks, far_source, far_block)
    quotient = jnp.einsum("skb,sjb->kj", vectors.astype(jnp.float32), image.astype(jnp.float32), precision=highest) / rows_total
    residual = (image.astype(jnp.float32) - jnp.einsum("kj,skb->sjb", quotient, vectors.astype(jnp.float32), precision=highest)).astype(jnp.bfloat16)
    for level_index in range(LEVELS):
        stride = 2 ** level_index
        update = slabwise(shifted(residual, stride), level_lower[level_index]) + slabwise(shifted(residual, -stride), level_upper[level_index])
        residual = (residual.astype(jnp.float32) - update).astype(jnp.bfloat16)
    correction = slabwise(residual, level_final).astype(jnp.bfloat16)
    corrected_image = apply_operator(correction, blocks, slab_blocks, far_source, far_block)
    basis = jnp.concatenate([vectors, correction], 1).astype(jnp.float32)
    images = jnp.concatenate([image, corrected_image], 1).astype(jnp.float32)
    gram = jnp.einsum("skb,sjb->kj", basis, basis, precision=highest) / rows_total
    pencil = jnp.einsum("skb,sjb->kj", basis, images, precision=highest) / rows_total - shift_levels[shift_index[0]] * gram
    return correction, gram, pencil
```

```python
import jax
import jax.numpy as jnp
from jax import lax
from jax.sharding import PartitionSpec as P


def padded(x, sides, width):
    for axis, dim in sides:
        size, length = (lax.axis_size(axis), x.shape[dim])
        up = [(i, (i + 1) % size) for i in range(size - 1)]
        down = [(j, i) for i, j in up]
        last = lax.slice_in_dim(x, length - width, length, axis=dim)
        first = lax.slice_in_dim(x, 0, width, axis=dim)
        before = lax.ppermute(last, axis, up)
        after = lax.ppermute(first, axis, down)
        x = jnp.concatenate([before, x, after], axis=dim)
    return x


def from_behind(block, axis, distance):
    devices = range(lax.axis_size(axis))
    route = [(i - distance, i) for i in devices if i - distance in devices]
    return lax.ppermute(block, axis, route)


def orbitals(operand):
    return lax.all_gather(operand, "vec", axis=2, tiled=True)


def rim(operand):
    return orbitals(padded(operand, (("slab", 0),), operand.shape[0]))


def move(operand, offset):
    return from_behind(operand, "slab", offset)


def halves_from(operand, stride):
    slab_count = operand.shape[0]
    if stride % slab_count == 0:
        return move(operand, stride // slab_count)
    if stride > 0:
        return move(operand[slab_count - stride :], 1)
    return move(operand[:-stride], -1)


def partners(residual, stride):
    slab_count = residual.shape[0]
    if stride >= slab_count * lax.axis_size("slab"):
        return None
    below, above = halves_from(residual, stride), halves_from(residual, -stride)
    if stride % slab_count == 0:
        rows = orbitals(jnp.concatenate([below, above], 0))
        return rows[:slab_count], rows[slab_count:]
    rows = orbitals(jnp.concatenate([below, residual, above], 0))
    return rows[:slab_count], rows[2 * stride :]


def total(part):
    slabs = lax.axis_size("slab")
    if slabs & (slabs - 1):
        return lax.psum(part, ("slab", "vec"))
    part = part + lax.ppermute(part, "vec", [(0, 1), (1, 0)])
    reach = 1
    while reach < slabs:
        part = part + lax.ppermute(part, "slab", [(i, i ^ reach) for i in range(slabs)])
        reach *= 2
    return part


def apply_operator(half_rows, blocks, slab_blocks, far_source, far_block):
    slab_count = half_rows.shape[0]
    extended = rim(half_rows)
    below_rows = extended[slab_count - 1 : 2 * slab_count - 1]
    own_rows = extended[slab_count : 2 * slab_count]
    above_rows = extended[slab_count + 1 : 2 * slab_count + 1]
    summed = jnp.einsum(
        "skb,sbc->skc", below_rows, blocks[slab_blocks[:, 0]], preferred_element_type=jnp.float32
    )
    summed = summed + jnp.einsum(
        "skb,sbc->skc", own_rows, blocks[slab_blocks[:, 1]], preferred_element_type=jnp.float32
    )
    summed = summed + jnp.einsum(
        "skb,sbc->skc", above_rows, blocks[slab_blocks[:, 2]], preferred_element_type=jnp.float32
    )
    first_slab = lax.axis_index("slab") * slab_count
    local_rows = far_source - first_slab + slab_count
    fetched = extended[local_rows]
    summed = summed + jnp.einsum(
        "sfkb,sfbc->skc", fetched, blocks[far_block], preferred_element_type=jnp.float32
    )
    return summed.astype(jnp.bfloat16)


def on_device(
    vectors,
    blocks,
    slab_blocks,
    far_source,
    far_block,
    level_lower,
    level_upper,
    level_final,
    shift_levels,
    shift_index,
):
    slab_count = vectors.shape[0]
    rows_total = slab_count * lax.axis_size("slab") * blocks.shape[1]
    highest = lax.Precision.HIGHEST
    image = apply_operator(vectors, blocks, slab_blocks, far_source, far_block)
    quotient_part = jnp.einsum("skb,sjb->kj", vectors, image, preferred_element_type=jnp.float32)
    quotient = total(quotient_part) / rows_total
    residual = (
        image.astype(jnp.float32)
        - jnp.einsum("kj,skb->sjb", quotient, vectors.astype(jnp.float32), precision=highest)
    ).astype(jnp.bfloat16)
    level_count = level_lower.shape[0]
    for level_index in range(level_count):
        stride = 2**level_index
        pair = partners(residual, stride)
        if pair is None:
            continue
        from_below, from_above = pair
        update = jnp.einsum(
            "skb,sbc->skc", from_below, level_lower[level_index], preferred_element_type=jnp.float32
        )
        update = update + jnp.einsum(
            "skb,sbc->skc", from_above, level_upper[level_index], preferred_element_type=jnp.float32
        )
        residual = (residual.astype(jnp.float32) - update).astype(jnp.bfloat16)
    correction = jnp.einsum(
        "skb,sbc->skc", orbitals(residual), level_final, preferred_element_type=jnp.float32
    ).astype(jnp.bfloat16)
    corrected_image = apply_operator(correction, blocks, slab_blocks, far_source, far_block)
    basis = jnp.concatenate([vectors, correction], 1)
    others = jnp.concatenate([vectors, correction, image, corrected_image], 1)
    part = jnp.einsum("skb,sjb->kj", basis, others, preferred_element_type=jnp.float32)
    both = total(part)
    width = basis.shape[1]
    gram_total, image_total = both[:, :width], both[:, width:]
    gram = gram_total / rows_total
    pencil = image_total / rows_total - shift_levels[shift_index[0]] * gram
    return (correction, gram, pencil)


def solution(mesh):
    in_specs = (
        P(("groups", "slab"), None, "vec"),
        P("groups", None, "vec"),
        P(("groups", "slab"), None),
        P(("groups", "slab"), None),
        P(("groups", "slab"), None),
        P(None, ("groups", "slab"), None, "vec"),
        P(None, ("groups", "slab"), None, "vec"),
        P(("groups", "slab"), None, "vec"),
        P("groups"),
        P("groups"),
    )
    out_specs = (P(("groups", "slab"), None, "vec"), P("groups", None), P("groups", None))
    return jax.shard_map(
        on_device, mesh=mesh, in_specs=in_specs, out_specs=out_specs, check_vma=False
    )
```

```python
import jax
import jax.numpy as jnp
from jax import lax
from jax.sharding import PartitionSpec as P


def padded(x, sides, width):
    for axis, dim in sides:
        size, length = (lax.axis_size(axis), x.shape[dim])
        up = [(i, (i + 1) % size) for i in range(size - 1)]
        down = [(j, i) for i, j in up]
        last = lax.slice_in_dim(x, length - width, length, axis=dim)
        first = lax.slice_in_dim(x, 0, width, axis=dim)
        before = lax.ppermute(last, axis, up)
        after = lax.ppermute(first, axis, down)
        x = jnp.concatenate([before, x, after], axis=dim)
    return x


def from_behind(block, axis, distance):
    devices = range(lax.axis_size(axis))
    route = [(i - distance, i) for i in devices if i - distance in devices]
    return lax.ppermute(block, axis, route)


def orbitals(operand):
    return lax.all_gather(operand, "vec", axis=2, tiled=True)


def rim(operand):
    return orbitals(padded(operand, (("slab", 0),), operand.shape[0]))


def move(operand, offset):
    return from_behind(operand, "slab", offset)


def halves_from(operand, stride):
    slab_count = operand.shape[0]
    if stride % slab_count == 0:
        return move(operand, stride // slab_count)
    if stride > 0:
        return move(operand[slab_count - stride :], 1)
    return move(operand[:-stride], -1)


def partners(residual, stride):
    slab_count = residual.shape[0]
    if stride >= slab_count * lax.axis_size("slab"):
        return None
    below, above = halves_from(residual, stride), halves_from(residual, -stride)
    if stride % slab_count == 0:
        rows = orbitals(jnp.concatenate([below, above], 0))
        return rows[:slab_count], rows[slab_count:]
    rows = orbitals(jnp.concatenate([below, residual, above], 0))
    return rows[:slab_count], rows[2 * stride :]


def exchanged(chunks):
    return lax.all_to_all(chunks, ("slab", "vec"), split_axis=0, concat_axis=0, tiled=True)


def total_at_once(part):
    count = lax.axis_size("slab") * lax.axis_size("vec")
    rows, cols = part.shape
    return exchanged(jnp.tile(part, (count, 1))).reshape(count, rows, cols).sum(0)


def total(part):
    count = lax.axis_size("slab") * lax.axis_size("vec")
    rows, cols = part.shape
    share = exchanged(part.reshape(count, -1, 128)).sum(0, keepdims=True)
    return exchanged(jnp.tile(share, (count, 1, 1))).reshape(rows, cols)


def apply_operator(half_rows, blocks, slab_blocks, far_source, far_block):
    slab_count = half_rows.shape[0]
    extended = rim(half_rows)
    below_rows = extended[slab_count - 1 : 2 * slab_count - 1]
    own_rows = extended[slab_count : 2 * slab_count]
    above_rows = extended[slab_count + 1 : 2 * slab_count + 1]
    summed = jnp.einsum(
        "skb,sbc->skc", below_rows, blocks[slab_blocks[:, 0]], preferred_element_type=jnp.float32
    )
    summed = summed + jnp.einsum(
        "skb,sbc->skc", own_rows, blocks[slab_blocks[:, 1]], preferred_element_type=jnp.float32
    )
    summed = summed + jnp.einsum(
        "skb,sbc->skc", above_rows, blocks[slab_blocks[:, 2]], preferred_element_type=jnp.float32
    )
    first_slab = lax.axis_index("slab") * slab_count
    local_rows = far_source - first_slab + slab_count
    fetched = extended[local_rows]
    summed = summed + jnp.einsum(
        "sfkb,sfbc->skc", fetched, blocks[far_block], preferred_element_type=jnp.float32
    )
    return summed.astype(jnp.bfloat16)


def on_device(
    vectors,
    blocks,
    slab_blocks,
    far_source,
    far_block,
    level_lower,
    level_upper,
    level_final,
    shift_levels,
    shift_index,
):
    slab_count = vectors.shape[0]
    rows_total = slab_count * lax.axis_size("slab") * blocks.shape[1]
    highest = lax.Precision.HIGHEST
    image = apply_operator(vectors, blocks, slab_blocks, far_source, far_block)
    quotient_part = jnp.einsum("skb,sjb->kj", vectors, image, preferred_element_type=jnp.float32)
    quotient = total_at_once(quotient_part) / rows_total
    residual = (
        image.astype(jnp.float32)
        - jnp.einsum("kj,skb->sjb", quotient, vectors.astype(jnp.float32), precision=highest)
    ).astype(jnp.bfloat16)
    level_count = level_lower.shape[0]
    for level_index in range(level_count):
        stride = 2**level_index
        pair = partners(residual, stride)
        if pair is None:
            continue
        from_below, from_above = pair
        update = jnp.einsum(
            "skb,sbc->skc", from_below, level_lower[level_index], preferred_element_type=jnp.float32
        )
        update = update + jnp.einsum(
            "skb,sbc->skc", from_above, level_upper[level_index], preferred_element_type=jnp.float32
        )
        residual = (residual.astype(jnp.float32) - update).astype(jnp.bfloat16)
    correction = jnp.einsum(
        "skb,sbc->skc", orbitals(residual), level_final, preferred_element_type=jnp.float32
    ).astype(jnp.bfloat16)
    corrected_image = apply_operator(correction, blocks, slab_blocks, far_source, far_block)
    basis = jnp.concatenate([vectors, correction], 1)
    others = jnp.concatenate([vectors, correction, image, corrected_image], 1)
    part = jnp.einsum("skb,sjb->kj", basis, others, preferred_element_type=jnp.float32)
    both = total(part)
    width = basis.shape[1]
    gram_total, image_total = both[:, :width], both[:, width:]
    gram = gram_total / rows_total
    pencil = image_total / rows_total - shift_levels[shift_index[0]] * gram
    return (correction, gram, pencil)


def solution(mesh):
    in_specs = (
        P(("groups", "slab"), None, "vec"),
        P("groups", None, "vec"),
        P(("groups", "slab"), None),
        P(("groups", "slab"), None),
        P(("groups", "slab"), None),
        P(None, ("groups", "slab"), None, "vec"),
        P(None, ("groups", "slab"), None, "vec"),
        P(("groups", "slab"), None, "vec"),
        P("groups"),
        P("groups"),
    )
    out_specs = (P(("groups", "slab"), None, "vec"), P("groups", None), P("groups", None))
    return jax.shard_map(
        on_device, mesh=mesh, in_specs=in_specs, out_specs=out_specs, check_vma=False
    )
```

```python
import functools

import jax
import jax.numpy as jnp
from jax import lax
from jax.experimental import pallas as pl
from jax.experimental.pallas import tpu as pltpu
from jax.sharding import PartitionSpec as P

f32, bf16 = jnp.float32, jnp.bfloat16
CHAIN = ("slab", "vec")
ANY = pl.BlockSpec(memory_space=pl.ANY)
VMEM = pl.BlockSpec(memory_space=pltpu.VMEM)
SMEM = pl.BlockSpec(memory_space=pltpu.SMEM)
SWAP = [(0, 1), (1, 0)]
MIB = 1024 * 1024


def kernel_call(body, out_shape, in_specs, scratch=(), vmem=16 * MIB, flops=0, size=0):
    return pl.pallas_call(
        body,
        out_shape=out_shape,
        in_specs=in_specs,
        out_specs=jax.tree.map(lambda _: VMEM, out_shape),
        scratch_shapes=list(scratch),
        compiler_params=pltpu.CompilerParams(vmem_limit_bytes=vmem),
        cost_estimate=pl.CostEstimate(flops=flops, bytes_accessed=size, transcendentals=0),
    )


def struct(shape, dtype=bf16):
    return jax.ShapeDtypeStruct(shape, dtype)


def dot(rows, matrix):
    return jnp.dot(rows, matrix, preferred_element_type=f32)


def dot_t(left, right):
    return lax.dot_general(left, right, (((1,), (1,)), ((), ())), preferred_element_type=f32)


def columns(index, width):
    return pl.ds(pl.multiple_of(index * width, width), width)


def pack_body(levels, place, lower, upper, final, packed, sem):
    count = packed.shape[1]
    theirs = pl.ds((1 - place[0]) * count, count)
    copies = []
    for level in range(levels):
        for side, ref in enumerate((lower, upper)):
            copies.append((ref.at[level, theirs], 2 * level + side))
    copies.append((final.at[theirs], 2 * levels))
    copies = [pltpu.make_async_copy(src, packed.at[k], sem.at[k]) for src, k in copies]
    for copy in copies:
        copy.start()
    for copy in copies:
        copy.wait()


def pack(place, lower, upper, final, levels):
    _, slabs, rows, half = lower.shape
    return pl.pallas_call(
        functools.partial(pack_body, levels),
        out_shape=struct((2 * levels + 1, slabs // 2, rows, half)),
        in_specs=[SMEM, ANY, ANY, ANY],
        out_specs=ANY,
        scratch_shapes=[pltpu.SemaphoreType.DMA((2 * levels + 1,))],
        compiler_params=pltpu.CompilerParams(vmem_limit_bytes=2 * MIB),
    )(place, lower, upper, final)


def image_body(place, table, extended, vectors, blocks, keep, send, quotient, image):
    slabs, _, half = vectors.shape
    reach = table.shape[1] // 2
    part = jnp.zeros(quotient.shape, f32)
    for slab in range(slabs):
        summed = None
        for entry in range(reach):
            rows = extended[table[slab, entry] + (slab + slabs)]
            term = dot(rows, blocks[table[slab, reach + entry]])
            summed = term if summed is None else summed + term
        rounded = summed.astype(bf16)
        image[slab] = rounded
        part = part + dot_t(vectors[slab], rounded)
    quotient[...] = part
    mine = slabs // 2
    keep[...] = image[pl.ds(place[0] * mine, mine)]
    send[...] = image[pl.ds((1 - place[0]) * mine, mine)]


def image_halves(place, table, extended, vectors, blocks):
    slabs, rows, half = vectors.shape
    part = struct((slabs // 2, rows, half))
    return kernel_call(
        image_body,
        (part, part, struct((rows, rows), f32)),
        [SMEM, SMEM, VMEM, VMEM, VMEM],
        [pltpu.VMEM((slabs, rows, half), bf16)],
    )(place, table, extended, vectors, blocks)


def weight_copies(level, place, lower, upper, packed, weights, sem):
    count = weights.shape[2]
    mine = pl.ds(place[0] * count, count)
    return [
        [
            pltpu.make_async_copy(ref.at[level, mine], weights.at[side, 0], sem.at[side, 0]),
            pltpu.make_async_copy(packed.at[2 * level + side], weights.at[side, 1], sem.at[side, 1]),
        ]
        for side, ref in enumerate((lower, upper))
    ]


def level_rows(place, part, side_rows, own, weights, out):
    half = weights.shape[-1]
    cols = columns(jnp.where(part == 0, place[0], 1 - place[0]), half)
    for slab in range(own.shape[0]):
        summed = None
        for side, rows in side_rows:
            term = dot(rows[slab], weights[side, part, slab])
            summed = term if summed is None else summed + term
        out[slab, :, cols] = (own[slab, :, cols].astype(f32) - summed).astype(bf16)


def level_body(level, place, own, below, above, lower, upper, packed, out, weights, sem):
    copies = weight_copies(level, place, lower, upper, packed, weights, sem)
    for part in range(2):
        for side in range(2):
            copies[side][part].start()
    for part in range(2):
        for side in range(2):
            copies[side][part].wait()
        level_rows(place, part, ((0, below), (1, above)), own, weights, out)


def reduced(level, place, own, below, above, lower, upper, packed):
    slabs, _, width = own.shape
    half = lower.shape[-1]
    return kernel_call(
        functools.partial(level_body, level),
        struct(own.shape),
        [SMEM, VMEM, VMEM, VMEM, ANY, ANY, ANY],
        [pltpu.VMEM((2, 2, slabs, width, half), bf16), pltpu.SemaphoreType.DMA((2, 2))],
    )(place, own, below, above, lower, upper, packed)


def last_body(level, place, own, other, lower, upper, final, packed, whole, keep, send, weights, rows, sem):
    count = own.shape[0]
    half = keep.shape[-1]
    mine = pl.ds(place[0] * count, count)
    below = place[1]

    def fetch(ref):
        return pltpu.make_async_copy(ref.at[level, mine], weights.at[0, 0], sem.at[0])

    pl.when(below == 1)(lambda: fetch(lower).start())
    pl.when(below == 0)(lambda: fetch(upper).start())
    copies = [
        fetch(lower),
        pltpu.make_async_copy(packed.at[2 * level + 1 - below], weights.at[0, 1], sem.at[1]),
        pltpu.make_async_copy(final.at[mine], weights.at[1, 0], sem.at[2]),
        pltpu.make_async_copy(packed.at[packed.shape[0] - 1], weights.at[1, 1], sem.at[3]),
    ]
    for copy in copies[1:]:
        copy.start()
    for part in range(2):
        copies[part].wait()
        level_rows(place, part, ((0, other),), own, weights, rows)
    for part, target in enumerate((keep, send)):
        copies[2 + part].wait()
        cols = columns(jnp.where(part == 0, place[0], 1 - place[0]), half)
        for slab in range(count):
            result = dot(rows[slab], weights[1, part, slab]).astype(bf16)
            target[slab] = result
            whole[slab, :, cols] = result


def last_reduced(level, place, own, other, lower, upper, final, packed):
    slabs, rows, width = own.shape
    half = lower.shape[-1]
    part = struct((slabs, rows, half))
    return kernel_call(
        functools.partial(last_body, level),
        (struct(own.shape), part, part),
        [SMEM, VMEM, VMEM, ANY, ANY, ANY, ANY],
        [
            pltpu.VMEM((2, 2, slabs, width, half), bf16),
            pltpu.VMEM(own.shape, bf16),
            pltpu.SemaphoreType.DMA((4,)),
        ],
    )(place, own, other, lower, upper, final, packed)


def final_body(place, own, final, packed, whole, keep, send, weights, sem):
    count = own.shape[0]
    half = keep.shape[-1]
    mine = pl.ds(place[0] * count, count)
    copies = [
        pltpu.make_async_copy(final.at[mine], weights.at[0], sem.at[0]),
        pltpu.make_async_copy(packed.at[packed.shape[0] - 1], weights.at[1], sem.at[1]),
    ]
    for copy in copies:
        copy.start()
    for part, target in enumerate((keep, send)):
        copies[part].wait()
        cols = columns(jnp.where(part == 0, place[0], 1 - place[0]), half)
        for slab in range(count):
            result = dot(own[slab], weights[part, slab]).astype(bf16)
            target[slab] = result
            whole[slab, :, cols] = result


def corrected(place, own, final, packed):
    slabs, rows, width = own.shape
    half = final.shape[-1]
    part = struct((slabs, rows, half))
    return kernel_call(
        final_body,
        (struct(own.shape), part, part),
        [SMEM, VMEM, ANY, ANY],
        [pltpu.VMEM((2, slabs, width, half), bf16), pltpu.SemaphoreType.DMA((2,))],
    )(place, own, final, packed)


def pencil_body(place, table, extended, image, window, blocks, others, out, summed):
    slabs = window.shape[0]
    own = image.shape[0]
    below = slabs - own
    half = blocks.shape[-1]
    rows = image.shape[1]
    reach = table.shape[1] // 2
    first = place[0] * own
    mine, theirs = columns(place[0], half), columns(1 - place[0], half)
    summed[...] = jnp.zeros(summed.shape, f32)

    @pl.loop(0, slabs * reach)
    def _(pair):
        target = lax.div(pair, reach)
        entry = pair - target * reach
        source = target + table[first + target, entry]
        inside = jnp.logical_and(source >= 0, source < slabs)
        held = jnp.logical_or(target >= below, source >= below)

        @pl.when(jnp.logical_and(inside, held))
        def _():
            block = table[first + target, reach + entry]
            vectors = window[source]
            summed[target, :, mine] += dot(vectors, blocks[block])
            summed[target, :, theirs] += dot(vectors, others[block])

    pencil = jnp.zeros((2 * rows, rows), f32)
    overlap = jnp.zeros((2 * rows, rows), f32)
    mixed = jnp.zeros((rows, rows), f32)
    old = jnp.zeros((rows, rows), f32)
    for slab in range(slabs):
        vectors, correction = extended[first + slab], window[slab]
        basis = jnp.concatenate([vectors, correction], 0)
        pencil = pencil + dot_t(basis, summed[slab].astype(bf16))
        if slab >= below:
            overlap = overlap + dot_t(basis, correction)
            mixed = mixed + dot_t(correction, image[slab - below])
            old = old + dot_t(vectors, vectors)
    out[0 : 2 * rows, 0:rows] = pencil
    out[0 : 2 * rows, rows : 2 * rows] = overlap
    out[2 * rows : 3 * rows, 0:rows] = mixed
    out[2 * rows : 3 * rows, rows : 2 * rows] = old


def pencil_parts(place, table, extended, image, window, blocks, others):
    rows = image.shape[1]
    return kernel_call(
        pencil_body,
        struct((3 * rows, 2 * rows), f32),
        [SMEM, SMEM, VMEM, VMEM, VMEM, VMEM, VMEM],
        [pltpu.VMEM(window.shape, f32)],
        vmem=24 * MIB,
    )(place, table, extended, image, window, blocks, others)


def swapped(operand):
    return lax.ppermute(operand, "vec", SWAP)


def along(operand, axis, distance):
    count = lax.axis_size("slab") * (2 if axis == CHAIN else 1)
    route = [(i, i + distance) for i in range(count) if 0 <= i + distance < count]
    return lax.ppermute(operand, axis, route)


def slab_total(part):
    slabs = lax.axis_size("slab")
    reach = 1
    while reach < slabs:
        part = part + lax.ppermute(part, "slab", [(i, i ^ reach) for i in range(slabs)])
        reach *= 2
    return part


def on_device(
    vectors,
    blocks,
    slab_blocks,
    far_source,
    far_block,
    level_lower,
    level_upper,
    level_final,
    shift_levels,
    shift_index,
):
    slab_count, rows, half = vectors.shape
    own_count = slab_count // 2
    slabs = lax.axis_size("slab")
    chain = 2 * slabs
    width = blocks.shape[1]
    rows_total = slab_count * slabs * width
    levels = [l for l in range(level_lower.shape[0]) if 2**l < slab_count * slabs]
    slab, core = lax.axis_index("slab"), lax.axis_index("vec")
    link = 2 * slab + core
    pair_distance = 2 ** levels[-1] // own_count
    one_partner = 2 * pair_distance >= chain
    place = jnp.stack([core, (link >= pair_distance).astype(jnp.int32)]).astype(jnp.int32)

    halo = jnp.concatenate([along(vectors, "slab", 1), vectors, along(vectors, "slab", -1)], 0)
    extended = lax.all_gather(halo, "vec", axis=2, tiled=True)
    slab_ids = slab * slab_count + jnp.arange(slab_count, dtype=jnp.int32)[:, None]
    near = jnp.broadcast_to(jnp.arange(-1, 2, dtype=jnp.int32), (slab_count, 3))
    table = jnp.concatenate([near, far_source - slab_ids, slab_blocks, far_block], 1)
    tables = jnp.concatenate([along(table, "slab", 1), table], 0)

    packed = swapped(pack(place, level_lower, level_upper, level_final, len(levels)))
    others = swapped(blocks)
    weights = (level_lower, level_upper, packed)

    keep, send, quotient = image_halves(place, table, extended, vectors, blocks)
    received = swapped(send)
    quotient = slab_total(quotient + swapped(quotient)) / rows_total
    image = jnp.where(core == 0, jnp.concatenate([keep, received], 2), jnp.concatenate([received, keep], 2))

    def held(offset):
        return lax.dynamic_slice_in_dim(extended, slab_count + own_count * core + offset, own_count)

    below = jnp.concatenate([along(image[own_count - 1 :], CHAIN, 1), image[: own_count - 1]], 0)
    above = jnp.concatenate([image[1:], along(image[:1], CHAIN, -1)], 0)
    both = [jnp.concatenate([a, held(o)], 1) for a, o in ((image, 0), (below, -1), (above, 1))]
    both = reduced(0, place, *both, *weights)
    both = reduced(1, place, both, along(both, CHAIN, 1), along(both, CHAIN, -1), *weights)
    shift = jnp.einsum(
        "kj,skb->sjb", quotient, both[:, rows:].astype(f32), precision=lax.Precision.HIGHEST
    )
    residual = (both[:, :rows].astype(f32) - shift).astype(bf16)
    for level in levels[2:]:
        distance = 2**level // own_count
        if level == levels[-1] and one_partner:
            route = [(i, i + distance) for i in range(chain - distance)]
            other = lax.ppermute(residual, CHAIN, route + [(j, i) for i, j in route])
            correction, keep, send = last_reduced(
                level, place, residual, other, level_lower, level_upper, level_final, packed
            )
        else:
            below, above = along(residual, CHAIN, distance), along(residual, CHAIN, -distance)
            residual = reduced(level, place, residual, below, above, *weights)
    if not one_partner:
        correction, keep, send = corrected(place, residual, level_final, packed)

    window = jnp.concatenate([along(correction, CHAIN, 2), along(correction, CHAIN, 1), correction], 0)
    received = swapped(send)
    result = jnp.where(core == 0, jnp.concatenate([keep, received], 0), jnp.concatenate([received, keep], 0))
    part = pencil_parts(place, tables, extended, image, window, blocks, others)
    sums = slab_total(part + swapped(part)) / rows_total
    top, bottom = sums[: 2 * rows], sums[2 * rows :]
    old, mixed, overlap = bottom[:, rows:], bottom[:, :rows], top[:, rows:]
    gram = jnp.concatenate([jnp.concatenate([old, overlap[:rows].T], 0), overlap], 1)
    projected = jnp.concatenate([jnp.concatenate([quotient, mixed], 0), top[:, :rows]], 1)
    pencil = projected - shift_levels[shift_index[0]] * gram
    return (result, gram, pencil)


def solution(mesh):
    in_specs = (
        P(("groups", "slab"), None, "vec"),
        P("groups", None, "vec"),
        P(("groups", "slab"), None),
        P(("groups", "slab"), None),
        P(("groups", "slab"), None),
        P(None, ("groups", "slab"), None, "vec"),
        P(None, ("groups", "slab"), None, "vec"),
        P(("groups", "slab"), None, "vec"),
        P("groups"),
        P("groups"),
    )
    out_specs = (P(("groups", "slab"), None, "vec"), P("groups", None), P("groups", None))
    return jax.shard_map(
        on_device, mesh=mesh, in_specs=in_specs, out_specs=out_specs, check_vma=False
    )
```

```python
import functools

import jax
import jax.numpy as jnp
from jax import lax
from jax.experimental import pallas as pl
from jax.experimental.pallas import tpu as pltpu
from jax.sharding import PartitionSpec as P

f32, bf16 = jnp.float32, jnp.bfloat16
CHAIN = ("slab", "vec")
ANY = pl.BlockSpec(memory_space=pl.ANY)
VMEM = pl.BlockSpec(memory_space=pltpu.VMEM)
SMEM = pl.BlockSpec(memory_space=pltpu.SMEM)
SWAP = [(0, 1), (1, 0)]
MIB = 1024 * 1024


def kernel_call(body, out_shape, in_specs, scratch=(), vmem=16 * MIB, flops=0, size=0):
    return pl.pallas_call(
        body,
        out_shape=out_shape,
        in_specs=in_specs,
        out_specs=jax.tree.map(lambda _: VMEM, out_shape),
        scratch_shapes=list(scratch),
        compiler_params=pltpu.CompilerParams(vmem_limit_bytes=vmem),
        cost_estimate=pl.CostEstimate(flops=flops, bytes_accessed=size, transcendentals=0),
    )


def struct(shape, dtype=bf16):
    return jax.ShapeDtypeStruct(shape, dtype)


def dot(rows, matrix):
    return jnp.dot(rows, matrix, preferred_element_type=f32)


def dot_t(left, right):
    return lax.dot_general(left, right, (((1,), (1,)), ((), ())), preferred_element_type=f32)


def columns(index, width):
    return pl.ds(pl.multiple_of(index * width, width), width)


def in_vmem(operand):
    return pltpu.with_memory_space_constraint(operand, pltpu.VMEM)


def in_hbm(operand):
    return pltpu.with_memory_space_constraint(operand, pltpu.HBM)


def fetch_body(levels, other, place, lower, upper, final, *rest):
    blocks = rest[0] if len(rest) == 4 else None
    fetched, sem = rest[-2 if blocks is None else -3], rest[-1]
    count = fetched.shape[1]
    which = 1 - place[0] if other else place[0]
    slabs = pl.ds(which * count, count)
    pairs = []
    for level in range(levels):
        for ref in (lower, upper):
            pairs.append((ref.at[level, slabs], fetched.at[len(pairs)]))
    pairs.append((final.at[slabs], fetched.at[len(pairs)]))
    if blocks is not None:
        pairs.insert(0, (blocks, rest[-2]))
    copies = [pltpu.make_async_copy(*pair, sem.at[k]) for k, pair in enumerate(pairs)]
    for copy in copies:
        copy.start()
    for copy in copies:
        copy.wait()


def fetch(place, lower, upper, final, levels, blocks=None):
    _, slabs, rows, half = lower.shape
    shape = (2 * levels + 1, slabs // 2, rows, half)
    operands = [in_hbm(x) for x in (lower, upper, final)]
    out_shape = [pltpu.VMEM(shape, bf16)]
    size = 2 * 2 * (2 * levels + 1) * (slabs // 2) * rows * half
    if blocks is not None:
        operands.append(in_hbm(blocks))
        out_shape.append(pltpu.VMEM(blocks.shape, bf16))
        size += 2 * 2 * blocks.size
    return pl.pallas_call(
        functools.partial(fetch_body, levels, blocks is None),
        out_shape=out_shape,
        in_specs=[SMEM] + [ANY] * len(operands),
        out_specs=[ANY] * len(out_shape),
        scratch_shapes=[pltpu.SemaphoreType.DMA((2 * levels + 2,))],
        compiler_params=pltpu.CompilerParams(vmem_limit_bytes=2 * MIB),
        cost_estimate=pl.CostEstimate(flops=0, bytes_accessed=size, transcendentals=0),
    )(place, *operands)


def image_body(place, table, extended, vectors, blocks, keep, send, quotient, image):
    slabs, _, half = vectors.shape
    reach = table.shape[1] // 2
    part = jnp.zeros(quotient.shape, f32)
    for slab in range(slabs):
        summed = None
        for entry in range(reach):
            rows = extended[table[slab, entry] + (slab + slabs)]
            term = dot(rows, blocks[table[slab, reach + entry]])
            summed = term if summed is None else summed + term
        rounded = summed.astype(bf16)
        image[slab] = rounded
        part = part + dot_t(vectors[slab], rounded)
    quotient[...] = part
    mine = slabs // 2
    keep[...] = image[pl.ds(place[0] * mine, mine)]
    send[...] = image[pl.ds((1 - place[0]) * mine, mine)]


def image_halves(place, table, extended, vectors, blocks):
    slabs, rows, half = vectors.shape
    part = struct((slabs // 2, rows, half))
    return kernel_call(
        image_body,
        (part, part, struct((rows, rows), f32)),
        [SMEM, SMEM, VMEM, VMEM, VMEM],
        [pltpu.VMEM((slabs, rows, half), bf16)],
        flops=14 * slabs * rows * 2 * half * half,
        size=2 * blocks.size,
    )(place, table, extended, vectors, blocks)


def both_parts(place, mine, packed):
    half = mine.shape[-1]
    return (columns(place[0], half), mine), (columns(1 - place[0], half), packed)


def first_vectors_body(place, extended, mine, packed, out):
    count = out.shape[0]
    first = extended.shape[0] // 3 + count * place[0]
    for cols, weights in both_parts(place, mine, packed):
        for slab in range(count):
            own = first + slab
            summed = dot(extended[own - 1], weights[0, slab]) + dot(extended[own + 1], weights[1, slab])
            out[slab, :, cols] = (extended[own, :, cols].astype(f32) - summed).astype(bf16)


def first_body(place, image, inner, outer, vectors, quotient, mine, packed, out):
    count = image.shape[0]
    odd = place[0] == 1
    below = [jnp.where(odd, inner[0], outer[0])] + [image[slab] for slab in range(count - 1)]
    above = [image[slab] for slab in range(1, count)] + [jnp.where(odd, outer[0], inner[0])]
    high = quotient[...].astype(bf16)
    low = (quotient[...] - high.astype(f32)).astype(bf16)
    factors = (high.T, low.T)
    for cols, weights in both_parts(place, mine, packed):
        for slab in range(count):
            summed = dot(below[slab], weights[0, slab]) + dot(above[slab], weights[1, slab])
            for factor in factors:
                summed = summed + dot(factor, vectors[slab, :, cols])
            out[slab, :, cols] = (image[slab, :, cols].astype(f32) - summed).astype(bf16)


def reduce_rows(level, place, own, partners, mine, packed, out):
    bit = place[1 + level]
    for cols, weights in both_parts(place, mine, packed):
        for slab in range(own.shape[0]):
            summed = None
            for side, rows in zip((1 - bit, bit), partners):
                term = dot(rows[slab], weights[2 * level + side, slab])
                summed = term if summed is None else summed + term
            out[slab, :, cols] = (own[slab, :, cols].astype(f32) - summed).astype(bf16)


def level_body(level, place, own, *rest):
    *partners, mine, packed, out = rest
    reduce_rows(level, place, own, partners, mine, packed, out)


def product(place, rows, mine, packed, whole, parts):
    last = mine.shape[0] - 1
    for (cols, weights), target in zip(both_parts(place, mine, packed), parts):
        for slab in range(whole.shape[0]):
            result = dot(rows[slab], weights[last, slab]).astype(bf16)
            target[slab] = result
            whole[slab, :, cols] = result


def last_body(level, place, own, *rest):
    *partners, mine, packed, whole, keep, send, rows = rest
    reduce_rows(level, place, own, partners, mine, packed, rows)
    product(place, rows, mine, packed, whole, (keep, send))


def level_flops(operand, products):
    return 2 * products * operand.size * operand.shape[-1]


def add_pairs(table, row, entries, position, inside, window, blocks, others, place, summed, slot):
    half = blocks.shape[-1]
    mine, theirs = columns(place[0], half), columns(1 - place[0], half)
    for entry in range(entries):
        source = position + table[row, entry]

        @pl.when(inside(source))
        def _():
            block = table[row, entries + entry]
            vectors = window(source)
            summed[slot, :, mine] += dot(vectors, blocks[block])
            summed[slot, :, theirs] += dot(vectors, others[block])


def own_pairs_body(place, table, extended, image, correction, blocks, others, summed, out):
    own, rows, _ = image.shape
    reach = table.shape[1] // 2
    below = extended.shape[0] // 3
    first = place[0] * own
    summed[...] = jnp.zeros(summed.shape, f32)
    for slab in range(own):
        add_pairs(
            table, first + below + slab, reach, slab,
            lambda source: jnp.logical_and(source >= 0, source < own),
            lambda source: correction[source], blocks, others, place, summed, slab,
        )
    overlap = jnp.zeros((2 * rows, rows), f32)
    mixed = jnp.zeros((rows, rows), f32)
    old = jnp.zeros((rows, rows), f32)
    for slab in range(own):
        vectors, fixed = extended[first + below + slab], correction[slab]
        overlap = overlap + dot_t(jnp.concatenate([vectors, fixed], 0), fixed)
        mixed = mixed + dot_t(fixed, image[slab])
        old = old + dot_t(vectors, vectors)
    out[0 : 2 * rows, 0:rows] = jnp.zeros((2 * rows, rows), f32)
    out[0 : 2 * rows, rows : 2 * rows] = overlap
    out[2 * rows : 3 * rows, 0:rows] = mixed
    out[2 * rows : 3 * rows, rows : 2 * rows] = old


def cross_pairs_body(place, table, extended, correction, near, far, blocks, others, begun, part, out, window, summed):
    own, rows, _ = correction.shape
    reach = table.shape[1] // 2
    below = window.shape[0] - own
    half = blocks.shape[-1]
    first = place[0] * own
    mine, theirs = columns(place[0], half), columns(1 - place[0], half)
    window[0:own] = far[...]
    window[own : 2 * own] = near[...]
    window[below : below + own] = correction[...]
    summed[0:below] = jnp.zeros((below,) + summed.shape[1:], f32)
    summed[below : below + own] = begun[...]

    @pl.loop(0, (below + own) * reach)
    def _(pair):
        target = lax.div(pair, reach)
        entry = pair - target * reach
        source = target + table[first + target, entry]
        inside = jnp.logical_and(source >= 0, source < below + own)

        @pl.when(jnp.logical_and(inside, (target >= below) != (source >= below)))
        def _():
            block = table[first + target, reach + entry]
            vectors = window[source]
            summed[target, :, mine] += dot(vectors, blocks[block])
            summed[target, :, theirs] += dot(vectors, others[block])

    pencil = jnp.zeros((2 * rows, rows), f32)
    for slab in range(below + own):
        basis = jnp.concatenate([extended[first + slab], window[slab]], 0)
        pencil = pencil + dot_t(basis, summed[slab].astype(bf16))
    out[...] = part[...]
    out[0 : 2 * rows, 0:rows] = pencil


def pencil_parts(place, table, extended, image, correction, near, far, blocks, others):
    own, rows, width = image.shape
    flops = level_flops(image, 7)
    begun, part = kernel_call(
        own_pairs_body,
        (struct(image.shape, f32), struct((3 * rows, 2 * rows), f32)),
        [SMEM, SMEM] + [VMEM] * 5,
        flops=flops,
        vmem=20 * MIB,
    )(place, table, extended, image, correction, blocks, others)
    return kernel_call(
        cross_pairs_body,
        struct(part.shape, f32),
        [SMEM, SMEM] + [VMEM] * 8,
        [pltpu.VMEM((3 * own, rows, width), bf16), pltpu.VMEM((3 * own, rows, width), f32)],
        flops=flops,
        vmem=20 * MIB,
    )(place, table, extended, correction, near, far, blocks, others, begun, part)


def assemble_body(scale, levels, index, quotient, first, second, gram, pencil):
    rows = quotient.shape[0]
    shift = levels[index[0]]
    sums = (first[...] + second[...]) * scale
    overlap = sums[: 2 * rows, rows:]
    old, mixed = sums[2 * rows :, rows:], sums[2 * rows :, :rows]
    left = jnp.concatenate([old, overlap[:rows].T], 0)
    whole = jnp.concatenate([left, overlap], 1)
    gram[...] = whole
    projected = jnp.concatenate([jnp.concatenate([quotient[...], mixed], 0), sums[: 2 * rows, :rows]], 1)
    pencil[...] = projected - shift * whole


def swapped(operand):
    return lax.ppermute(operand, "vec", SWAP)


def along(operand, axis, distance):
    count = lax.axis_size("slab") * (2 if axis == CHAIN else 1)
    route = [(i, i + distance) for i in range(count) if 0 <= i + distance < count]
    return lax.ppermute(operand, axis, route)


def pair_routes(distance):
    chain = 2 * lax.axis_size("slab")
    routes = []
    for bit in range(2):
        ups = [(i, i + distance) for i in range(chain - distance) if i // distance % 2 == bit]
        routes.append(ups + [(j, i) for i, j in ups])
    return [route for route in routes if route]


def shared_out(part, reach, radix):
    slabs = lax.axis_size("slab")
    split = radix // 2
    core = lax.axis_index("vec")
    received = []
    for offset in range(split):
        route = []
        for i in range(slabs):
            if offset:
                route.append((2 * i, 2 * (i ^ (offset * reach))))
            route.append((2 * i + 1, 2 * (i ^ ((offset + split) * reach)) + 1))
        received.append(lax.ppermute(part, CHAIN, route))
    received[0] = jnp.where(core == 0, part, received[0])
    while len(received) > 1:
        received = [a + b for a, b in zip(received[::2], received[1::2])]
    return received[0]


def on_device(
    vectors,
    blocks,
    slab_blocks,
    far_source,
    far_block,
    level_lower,
    level_upper,
    level_final,
    shift_levels,
    shift_index,
):
    slab_count, rows, half = vectors.shape
    own_count = slab_count // 2
    slabs = lax.axis_size("slab")
    chain = 2 * slabs
    width = blocks.shape[1]
    rows_total = slab_count * slabs * width
    levels = [l for l in range(level_lower.shape[0]) if 2**l < slab_count * slabs]
    slab, core = lax.axis_index("slab"), lax.axis_index("vec")
    link = 2 * slab + core
    steps = [max(2**l // own_count, 1) for l in levels]
    place = jnp.stack([core] + [link // step % 2 for step in steps]).astype(jnp.int32)

    below, above = along(vectors, "slab", 1), along(vectors, "slab", -1)
    slab_ids = slab * slab_count + jnp.arange(slab_count, dtype=jnp.int32)[:, None]
    near = jnp.broadcast_to(jnp.arange(-1, 2, dtype=jnp.int32), (slab_count, 3))
    table = jnp.concatenate([near, far_source - slab_ids, slab_blocks, far_block], 1)
    tables = jnp.concatenate([along(table, "slab", 1), table], 0)

    (theirs,) = fetch(place, level_lower, level_upper, level_final, len(levels))
    packed = swapped(theirs)
    mine, held_blocks = fetch(place, level_lower, level_upper, level_final, len(levels), blocks)
    others = swapped(blocks)
    mine, packed, held_blocks, others = (in_vmem(x) for x in (mine, packed, held_blocks, others))

    halo = jnp.concatenate([below, vectors, above], 0)
    halo, tables = lax.optimization_barrier((halo, tables))
    extended = lax.all_gather(halo, "vec", axis=2, tiled=True)

    keep, send, quotient = image_halves(place, table, extended, vectors, held_blocks)
    received, quotient = swapped(send), quotient + swapped(quotient)
    image = jnp.where(core == 0, jnp.concatenate([keep, received], 2), jnp.concatenate([received, keep], 2))

    reach = 1
    while reach < slabs:
        radix = min(8, slabs // reach)
        share = shared_out(quotient, reach, radix)
        quotient = share + swapped(share)
        reach *= radix
    quotient = quotient / rows_total

    vectors_1 = kernel_call(
        first_vectors_body,
        struct(image.shape),
        [SMEM] + [VMEM] * 3,
        flops=level_flops(image, 2),
    )(place, extended, mine, packed)
    inner_route, outer_route = pair_routes(1)
    inner = swapped(lax.dynamic_slice_in_dim(image, (own_count - 1) * (1 - core), 1))
    outer = lax.ppermute(lax.dynamic_slice_in_dim(image, (own_count - 1) * core, 1), CHAIN, outer_route)
    residual = kernel_call(
        first_body,
        struct(image.shape),
        [SMEM] + [VMEM] * 7,
        flops=level_flops(image, 2),
    )(place, image, inner, outer, vectors_1, quotient, mine, packed)
    for level, step in zip(levels[1:], steps[1:]):
        partners = [lax.ppermute(residual, CHAIN, route) for route in reversed(pair_routes(step))][::-1]
        inputs = [SMEM] + [VMEM] * (3 + len(partners))
        if level != levels[-1]:
            residual = kernel_call(
                functools.partial(level_body, level),
                struct(residual.shape),
                inputs,
                flops=level_flops(residual, 2),
            )(place, residual, *partners, mine, packed)
    part = struct((own_count, rows, half))
    correction, keep, send = kernel_call(
        functools.partial(last_body, levels[-1]),
        (struct(residual.shape), part, part),
        inputs,
        [pltpu.VMEM(residual.shape, bf16)],
        flops=level_flops(residual, 2),
    )(place, residual, *partners, mine, packed)

    far, near = along(correction, CHAIN, 2), along(correction, CHAIN, 1)
    part = pencil_parts(place, tables, extended, image, correction, near, far, held_blocks, others)
    received = swapped(send)
    result = jnp.where(core == 0, jnp.concatenate([keep, received], 0), jnp.concatenate([received, keep], 0))

    part = part + swapped(part)
    radix = min(4, slabs)
    part = shared_out(part, 1, radix)
    reach = radix
    while reach < slabs:
        part = part + lax.ppermute(part, "slab", [(i, i ^ reach) for i in range(slabs)])
        reach *= 2
    square = struct((2 * rows, 2 * rows), f32)
    gram, pencil = kernel_call(
        functools.partial(assemble_body, 1.0 / rows_total),
        (square, square),
        [SMEM, SMEM] + [VMEM] * 3,
    )(shift_levels, shift_index, quotient, part, swapped(part))
    return (result, gram, pencil)


def solution(mesh):
    in_specs = (
        P(("groups", "slab"), None, "vec"),
        P("groups", None, "vec"),
        P(("groups", "slab"), None),
        P(("groups", "slab"), None),
        P(("groups", "slab"), None),
        P(None, ("groups", "slab"), None, "vec"),
        P(None, ("groups", "slab"), None, "vec"),
        P(("groups", "slab"), None, "vec"),
        P("groups"),
        P("groups"),
    )
    out_specs = (P(("groups", "slab"), None, "vec"), P("groups", None), P("groups", None))
    return jax.shard_map(
        on_device, mesh=mesh, in_specs=in_specs, out_specs=out_specs, check_vma=False
    )
```

```python
import functools

import jax
import jax.numpy as jnp
from jax import lax
from jax.experimental import pallas as pl
from jax.experimental.pallas import tpu as pltpu
from jax.sharding import PartitionSpec as P

f32, bf16 = jnp.float32, jnp.bfloat16
CHAIN = ("slab", "vec")
ANY = pl.BlockSpec(memory_space=pl.ANY)
VMEM = pl.BlockSpec(memory_space=pltpu.VMEM)
SMEM = pl.BlockSpec(memory_space=pltpu.SMEM)
SWAP = [(0, 1), (1, 0)]
MIB = 1024 * 1024


def kernel_call(body, out_shape, in_specs, scratch=(), vmem=16 * MIB, flops=0, size=0):
    return pl.pallas_call(
        body,
        out_shape=out_shape,
        in_specs=in_specs,
        out_specs=jax.tree.map(lambda _: VMEM, out_shape),
        scratch_shapes=list(scratch),
        compiler_params=pltpu.CompilerParams(vmem_limit_bytes=vmem),
        cost_estimate=pl.CostEstimate(flops=flops, bytes_accessed=size, transcendentals=0),
    )


def struct(shape, dtype=bf16):
    return jax.ShapeDtypeStruct(shape, dtype)


def dot(rows, matrix):
    return jnp.dot(rows, matrix, preferred_element_type=f32)


def dot_t(left, right):
    return lax.dot_general(left, right, (((1,), (1,)), ((), ())), preferred_element_type=f32)


def columns(index, width):
    return pl.ds(pl.multiple_of(index * width, width), width)


def in_vmem(operand):
    return pltpu.with_memory_space_constraint(operand, pltpu.VMEM)


def in_hbm(operand):
    return pltpu.with_memory_space_constraint(operand, pltpu.HBM)


def weight_copies(level, place, sources, weights, sem):
    count = weights.shape[2]
    slabs = pl.ds(place[0] * count, count)
    copies = []
    for side in range(2):
        for part in range(2):
            source = sources[2 * side + part].at[level, slabs]
            copies.append(pltpu.make_async_copy(source, weights.at[side, part], sem.at[side, part]))
    return copies


def run(copies):
    for copy in copies:
        copy.start()
    for copy in copies:
        copy.wait()


def load_body(level, place, token, *rest):
    *sources, weights, sem = rest
    run(weight_copies(level, place, sources, weights, sem))


def load_last_body(level, place, token, *rest):
    *sources, final, final_other, weights, sem = rest
    count = weights.shape[2]
    slabs = pl.ds(place[0] * count, count)
    above = place[1 + level] == 0

    def copy(source, side, part):
        return pltpu.make_async_copy(source, weights.at[side, part], sem.at[side, part])

    for part in range(2):
        pl.when(above)(lambda: copy(sources[2 + part].at[level, slabs], 0, part).start())
        pl.when(jnp.logical_not(above))(lambda: copy(sources[part].at[level, slabs], 0, part).start())
    finals = [copy(ref.at[slabs], 1, part) for part, ref in enumerate((final, final_other))]
    for each in finals:
        each.start()
    for part in range(2):
        copy(sources[part].at[level, slabs], 0, part).wait()
    for each in finals:
        each.wait()


def load(body, place, token, sources):
    _, slabs, rows, half = sources[0].shape
    shape = (2, 2, slabs // 2, rows, half)
    return pl.pallas_call(
        body,
        out_shape=pltpu.VMEM(shape, bf16),
        in_specs=[SMEM] + [ANY] * (1 + len(sources)),
        out_specs=VMEM,
        scratch_shapes=[pltpu.SemaphoreType.DMA((2, 2))],
        compiler_params=pltpu.CompilerParams(vmem_limit_bytes=4 * MIB),
        cost_estimate=pl.CostEstimate(flops=0, bytes_accessed=8 * slabs * rows * half, transcendentals=0),
    )(place, token, *[in_hbm(x) for x in sources])


def load_whole_body(place, token, *rest):
    count = len(rest) // 2
    sources, targets, sem = rest[:count], rest[count:-1], rest[-1]
    run([pltpu.make_async_copy(*pair, sem.at[k]) for k, pair in enumerate(zip(sources, targets))])


def load_whole(place, token, arrays):
    return pl.pallas_call(
        load_whole_body,
        out_shape=[pltpu.VMEM(x.shape, x.dtype) for x in arrays],
        in_specs=[SMEM] + [ANY] * (1 + len(arrays)),
        out_specs=[VMEM] * len(arrays),
        scratch_shapes=[pltpu.SemaphoreType.DMA((len(arrays),))],
        compiler_params=pltpu.CompilerParams(vmem_limit_bytes=12 * MIB),
        cost_estimate=pl.CostEstimate(
            flops=0, bytes_accessed=sum(2 * x.size for x in arrays), transcendentals=0
        ),
    )(place, token, *[in_hbm(x) for x in arrays])


def image_body(place, table, extended, vectors, blocks, keep, send, quotient, image):
    slabs, _, half = vectors.shape
    reach = table.shape[1] // 2
    part = jnp.zeros(quotient.shape, f32)
    for slab in range(slabs):
        summed = None
        for entry in range(reach):
            rows = extended[table[slab, entry] + (slab + slabs)]
            term = dot(rows, blocks[table[slab, reach + entry]])
            summed = term if summed is None else summed + term
        rounded = summed.astype(bf16)
        image[slab] = rounded
        part = part + dot_t(vectors[slab], rounded)
    quotient[...] = part
    mine = slabs // 2
    keep[...] = image[pl.ds(place[0] * mine, mine)]
    send[...] = image[pl.ds((1 - place[0]) * mine, mine)]


def image_halves(place, table, extended, vectors, blocks):
    slabs, rows, half = vectors.shape
    part = struct((slabs // 2, rows, half))
    return kernel_call(
        image_body,
        (part, part, struct((rows, rows), f32)),
        [SMEM, SMEM, VMEM, VMEM, VMEM],
        [pltpu.VMEM((slabs, rows, half), bf16)],
        flops=14 * slabs * rows * 2 * half * half,
        size=2 * blocks.size,
    )(place, table, extended, vectors, blocks)


def both_parts(place, half):
    return columns(place[0], half), columns(1 - place[0], half)


def first_vectors_body(place, token, extended, *rest):
    *sources, out, weights, sem = rest
    count, half = out.shape[0], weights.shape[-1]
    first = extended.shape[0] // 3 + count * place[0]
    copies = weight_copies(0, place, sources, weights, sem)
    for copy in copies:
        copy.start()
    for part, cols in enumerate(both_parts(place, half)):
        copies[part].wait()
        copies[2 + part].wait()
        for slab in range(count):
            own = first + slab
            summed = dot(extended[own - 1], weights[0, part, slab])
            summed = summed + dot(extended[own + 1], weights[1, part, slab])
            out[slab, :, cols] = (extended[own, :, cols].astype(f32) - summed).astype(bf16)


def first_body(place, image, inner, outer, vectors, quotient, *rest):
    *sources, out, weights, sem = rest
    count, half = out.shape[0], weights.shape[-1]
    copies = weight_copies(0, place, sources, weights, sem)
    for copy in copies:
        copy.start()
    odd = place[0] == 1
    below = [jnp.where(odd, inner[0], outer[0])] + [image[slab] for slab in range(count - 1)]
    above = [image[slab] for slab in range(1, count)] + [jnp.where(odd, outer[0], inner[0])]
    high = quotient[...].astype(bf16)
    low = (quotient[...] - high.astype(f32)).astype(bf16)
    factors = (high.T, low.T)
    for part, cols in enumerate(both_parts(place, half)):
        copies[part].wait()
        copies[2 + part].wait()
        for slab in range(count):
            summed = dot(below[slab], weights[0, part, slab]) + dot(above[slab], weights[1, part, slab])
            for factor in factors:
                summed = summed + dot(factor, vectors[slab, :, cols])
            out[slab, :, cols] = (image[slab, :, cols].astype(f32) - summed).astype(bf16)


def reduce_rows(place, own, partners, sides, weights, out):
    for part, cols in enumerate(both_parts(place, weights.shape[-1])):
        for slab in range(own.shape[0]):
            summed = None
            for side, rows in zip(sides, partners):
                term = dot(rows[slab], weights[side, part, slab])
                summed = term if summed is None else summed + term
            out[slab, :, cols] = (own[slab, :, cols].astype(f32) - summed).astype(bf16)


def second_body(place, own, inner, outer, weights, out):
    reduce_rows(place, own, (inner, outer), (1 - place[0], place[0]), weights, out)


def level_body(place, own, below, above, weights, out):
    reduce_rows(place, own, (below, above), (0, 1), weights, out)


def product(place, rows, weights, whole, targets):
    for part, cols in enumerate(both_parts(place, weights.shape[-1])):
        for slab in range(whole.shape[0]):
            result = dot(rows[slab], weights[part, slab]).astype(bf16)
            targets[part][slab] = result
            whole[slab, :, cols] = result


def last_body(place, own, other, weights, whole, keep, send, rows):
    reduce_rows(place, own, (other,), (0,), weights, rows)
    product(place, rows, weights.at[1], whole, (keep, send))


def final_body(place, own, final, final_other, whole, keep, send, weights, sem):
    count = own.shape[0]
    slabs = pl.ds(place[0] * count, count)
    run([
        pltpu.make_async_copy(ref.at[slabs], weights.at[part], sem.at[part])
        for part, ref in enumerate((final, final_other))
    ])
    product(place, own, weights, whole, (keep, send))


def level_flops(operand, products):
    return 2 * products * operand.size * operand.shape[-1]


def add_pairs(table, row, entries, position, inside, window, blocks, others, place, summed, slot):
    half = blocks.shape[-1]
    mine, theirs = columns(place[0], half), columns(1 - place[0], half)
    for entry in range(entries):
        source = position + table[row, entry]

        @pl.when(inside(source))
        def _():
            block = table[row, entries + entry]
            vectors = window(source)
            summed[slot, :, mine] += dot(vectors, blocks[block])
            summed[slot, :, theirs] += dot(vectors, others[block])


def own_pairs_body(place, table, extended, image, correction, blocks, others, summed, out):
    own, rows, _ = image.shape
    reach = table.shape[1] // 2
    below = extended.shape[0] // 3
    first = place[0] * own
    summed[...] = jnp.zeros(summed.shape, f32)
    for slab in range(own):
        add_pairs(
            table, first + below + slab, reach, slab,
            lambda source: jnp.logical_and(source >= 0, source < own),
            lambda source: correction[source], blocks, others, place, summed, slab,
        )
    overlap = jnp.zeros((2 * rows, rows), f32)
    mixed = jnp.zeros((rows, rows), f32)
    old = jnp.zeros((rows, rows), f32)
    for slab in range(own):
        vectors, fixed = extended[first + below + slab], correction[slab]
        overlap = overlap + dot_t(jnp.concatenate([vectors, fixed], 0), fixed)
        mixed = mixed + dot_t(fixed, image[slab])
        old = old + dot_t(vectors, vectors)
    out[0 : 2 * rows, 0:rows] = jnp.zeros((2 * rows, rows), f32)
    out[0 : 2 * rows, rows : 2 * rows] = overlap
    out[2 * rows : 3 * rows, 0:rows] = mixed
    out[2 * rows : 3 * rows, rows : 2 * rows] = old


def cross_pairs_body(place, table, extended, correction, near, far, blocks, others, begun, part, out, window, summed):
    own, rows, _ = correction.shape
    reach = table.shape[1] // 2
    below = window.shape[0] - own
    half = blocks.shape[-1]
    first = place[0] * own
    mine, theirs = columns(place[0], half), columns(1 - place[0], half)
    window[0:own] = far[...]
    window[own : 2 * own] = near[...]
    window[below : below + own] = correction[...]
    summed[0:below] = jnp.zeros((below,) + summed.shape[1:], f32)
    summed[below : below + own] = begun[...]

    @pl.loop(0, (below + own) * reach)
    def _(pair):
        target = lax.div(pair, reach)
        entry = pair - target * reach
        source = target + table[first + target, entry]
        inside = jnp.logical_and(source >= 0, source < below + own)

        @pl.when(jnp.logical_and(inside, (target >= below) != (source >= below)))
        def _():
            block = table[first + target, reach + entry]
            vectors = window[source]
            summed[target, :, mine] += dot(vectors, blocks[block])
            summed[target, :, theirs] += dot(vectors, others[block])

    pencil = jnp.zeros((2 * rows, rows), f32)
    for slab in range(below + own):
        basis = jnp.concatenate([extended[first + slab], window[slab]], 0)
        pencil = pencil + dot_t(basis, summed[slab].astype(bf16))
    out[...] = part[...]
    out[0 : 2 * rows, 0:rows] = pencil


def pencil_parts(place, table, extended, image, correction, near, far, blocks, others):
    own, rows, width = image.shape
    flops = level_flops(image, 7)
    begun, part = kernel_call(
        own_pairs_body,
        (struct(image.shape, f32), struct((3 * rows, 2 * rows), f32)),
        [SMEM, SMEM] + [VMEM] * 5,
        flops=flops,
        vmem=20 * MIB,
    )(place, table, extended, image, correction, blocks, others)
    return kernel_call(
        cross_pairs_body,
        struct(part.shape, f32),
        [SMEM, SMEM] + [VMEM] * 8,
        [pltpu.VMEM((3 * own, rows, width), bf16), pltpu.VMEM((3 * own, rows, width), f32)],
        flops=flops,
        vmem=20 * MIB,
    )(place, table, extended, correction, near, far, blocks, others, begun, part)


def assemble_body(scale, levels, index, quotient, first, second, gram, pencil):
    rows = quotient.shape[0]
    shift = levels[index[0]]
    sums = (first[...] + second[...]) * scale
    overlap = sums[: 2 * rows, rows:]
    old, mixed = sums[2 * rows :, rows:], sums[2 * rows :, :rows]
    left = jnp.concatenate([old, overlap[:rows].T], 0)
    whole = jnp.concatenate([left, overlap], 1)
    gram[...] = whole
    projected = jnp.concatenate([jnp.concatenate([quotient[...], mixed], 0), sums[: 2 * rows, :rows]], 1)
    pencil[...] = projected - shift * whole


def swapped(operand):
    return lax.ppermute(operand, "vec", SWAP)


def along(operand, axis, distance):
    count = lax.axis_size("slab") * (2 if axis == CHAIN else 1)
    route = [(i, i + distance) for i in range(count) if 0 <= i + distance < count]
    return lax.ppermute(operand, axis, route)


def pair_routes(distance):
    chain = 2 * lax.axis_size("slab")
    routes = []
    for bit in range(2):
        ups = [(i, i + distance) for i in range(chain - distance) if i // distance % 2 == bit]
        routes.append(ups + [(j, i) for i, j in ups])
    return [route for route in routes if route]


def shared_out(part, reach, radix):
    slabs = lax.axis_size("slab")
    split = radix // 2
    core = lax.axis_index("vec")
    received = []
    for offset in range(split):
        route = []
        for i in range(slabs):
            if offset:
                route.append((2 * i, 2 * (i ^ (offset * reach))))
            route.append((2 * i + 1, 2 * (i ^ ((offset + split) * reach)) + 1))
        received.append(lax.ppermute(part, CHAIN, route))
    received[0] = jnp.where(core == 0, part, received[0])
    while len(received) > 1:
        received = [a + b for a, b in zip(received[::2], received[1::2])]
    return received[0]


def on_device(
    vectors,
    blocks,
    slab_blocks,
    far_source,
    far_block,
    level_lower,
    level_upper,
    level_final,
    shift_levels,
    shift_index,
):
    slab_count, rows, half = vectors.shape
    own_count = slab_count // 2
    slabs = lax.axis_size("slab")
    chain = 2 * slabs
    width = blocks.shape[1]
    rows_total = slab_count * slabs * width
    levels = [l for l in range(level_lower.shape[0]) if 2**l < slab_count * slabs]
    slab, core = lax.axis_index("slab"), lax.axis_index("vec")
    link = 2 * slab + core
    steps = [max(2**l // own_count, 1) for l in levels]
    place = jnp.stack([core] + [link // step % 2 for step in steps]).astype(jnp.int32)

    slab_ids = slab * slab_count + jnp.arange(slab_count, dtype=jnp.int32)[:, None]
    near = jnp.broadcast_to(jnp.arange(-1, 2, dtype=jnp.int32), (slab_count, 3))
    table = jnp.concatenate([near, far_source - slab_ids, slab_blocks, far_block], 1)
    flat = vectors.reshape(slab_count * rows, half)
    note = jnp.pad(table.astype(bf16), ((0, 16 - slab_count), (0, half - table.shape[1])))
    above = along(vectors, "slab", -1)
    lifted = along(jnp.concatenate([flat, note], 0), "slab", 1)
    below = lifted[: slab_count * rows].reshape(vectors.shape)
    lower_table = lifted[slab_count * rows :][:slab_count, : table.shape[1]].astype(jnp.int32)
    tables = jnp.concatenate([lower_table, table], 0)

    weights = (level_lower, swapped(level_lower), level_upper, swapped(level_upper))
    (held_blocks,) = load_whole(place, place, [blocks])
    extended = lax.all_gather(jnp.concatenate([below, vectors, above], 0), "vec", axis=2, tiled=True)
    keep, send, quotient = image_halves(place, table, extended, vectors, in_vmem(held_blocks))
    received, quotient = swapped(send), quotient + swapped(quotient)
    image = jnp.where(core == 0, jnp.concatenate([keep, received], 2), jnp.concatenate([received, keep], 2))
    image, quotient = lax.optimization_barrier((image, quotient))

    inner_route, outer_route = pair_routes(1)
    outer = lax.ppermute(lax.dynamic_slice_in_dim(image, (own_count - 1) * core, 1), CHAIN, outer_route)
    inner = swapped(lax.dynamic_slice_in_dim(image, (own_count - 1) * (1 - core), 1))
    reach = 1
    while reach < slabs:
        radix = min(8, slabs // reach)
        share = shared_out(quotient, reach, radix)
        quotient = share + swapped(share)
        reach *= radix
    quotient = quotient / rows_total

    buffers = [pltpu.VMEM((2, 2, own_count, width, half), bf16), pltpu.SemaphoreType.DMA((2, 2))]
    held_weights = [in_hbm(x) for x in weights]
    vectors_1 = kernel_call(
        first_vectors_body,
        struct(image.shape),
        [SMEM, ANY, VMEM] + [ANY] * 4,
        buffers,
        flops=level_flops(image, 2),
        size=8 * own_count * width * half,
    )(place, image, extended, *held_weights)
    residual = kernel_call(
        first_body,
        struct(image.shape),
        [SMEM] + [VMEM] * 5 + [ANY] * 4,
        buffers,
        flops=level_flops(image, 2),
        size=8 * own_count * width * half,
    )(place, image, inner, outer, vectors_1, quotient, *held_weights)

    finals = (level_final, swapped(level_final))
    others = swapped(blocks)
    part = struct((own_count, rows, half))
    ends = (struct(residual.shape), part, part)
    one_partner = chain == 2 * steps[-1]
    for level, step in zip(levels[1:], steps[1:]):
        last = level == levels[-1]
        if last:
            held_blocks, others = load_whole(place, residual, [blocks, others])
        if last and one_partner:
            matrices = load(functools.partial(load_last_body, level), place, residual, weights + finals)
            (route,) = pair_routes(step)
            other = lax.ppermute(residual, CHAIN, route)
            correction, keep, send = kernel_call(
                last_body,
                ends,
                [SMEM] + [VMEM] * 3,
                [pltpu.VMEM(residual.shape, bf16)],
                flops=level_flops(residual, 2),
            )(place, residual, other, in_vmem(matrices))
            break
        matrices = load(functools.partial(load_body, level), place, residual, weights)
        if step == 1:
            partners = [lax.ppermute(residual, CHAIN, outer_route), swapped(residual)][::-1]
        else:
            partners = [along(residual, CHAIN, step), along(residual, CHAIN, -step)]
        residual = kernel_call(
            second_body if step == 1 else level_body,
            struct(residual.shape),
            [SMEM] + [VMEM] * 4,
            flops=level_flops(residual, 2),
        )(place, residual, *partners, in_vmem(matrices))
    if not one_partner:
        correction, keep, send = kernel_call(
            final_body,
            ends,
            [SMEM, VMEM, ANY, ANY],
            [pltpu.VMEM((2, own_count, width, half), bf16), pltpu.SemaphoreType.DMA((2,))],
            flops=level_flops(residual, 1),
        )(place, residual, *[in_hbm(x) for x in finals])
    held_blocks, others = in_vmem(held_blocks), in_vmem(others)

    far, near = along(correction, CHAIN, 2), along(correction, CHAIN, 1)
    part = pencil_parts(place, tables, extended, image, correction, near, far, held_blocks, others)
    received = swapped(send)
    result = jnp.where(core == 0, jnp.concatenate([keep, received], 0), jnp.concatenate([received, keep], 0))

    part = part + swapped(part)
    radix = min(4, slabs)
    part = shared_out(part, 1, radix)
    reach = radix
    while reach < slabs:
        part = part + lax.ppermute(part, "slab", [(i, i ^ reach) for i in range(slabs)])
        reach *= 2
    square = struct((2 * rows, 2 * rows), f32)
    gram, pencil = kernel_call(
        functools.partial(assemble_body, 1.0 / rows_total),
        (square, square),
        [SMEM, SMEM] + [VMEM] * 3,
    )(shift_levels, shift_index, quotient, part, swapped(part))
    return (result, gram, pencil)


def solution(mesh):
    in_specs = (
        P(("groups", "slab"), None, "vec"),
        P("groups", None, "vec"),
        P(("groups", "slab"), None),
        P(("groups", "slab"), None),
        P(("groups", "slab"), None),
        P(None, ("groups", "slab"), None, "vec"),
        P(None, ("groups", "slab"), None, "vec"),
        P(("groups", "slab"), None, "vec"),
        P("groups"),
        P("groups"),
    )
    out_specs = (P(("groups", "slab"), None, "vec"), P("groups", None), P("groups", None))
    return jax.shard_map(
        on_device, mesh=mesh, in_specs=in_specs, out_specs=out_specs, check_vma=False
    )
```

```python
import functools

import jax
import jax.numpy as jnp
from jax import lax
from jax.experimental import pallas as pl
from jax.experimental.pallas import tpu as pltpu
from jax.sharding import PartitionSpec as P

f32, bf16 = jnp.float32, jnp.bfloat16
CHAIN = ("slab", "vec")
ANY = pl.BlockSpec(memory_space=pl.ANY)
VMEM = pl.BlockSpec(memory_space=pltpu.VMEM)
SMEM = pl.BlockSpec(memory_space=pltpu.SMEM)
SWAP = [(0, 1), (1, 0)]
MIB = 1024 * 1024


def kernel_call(body, out_shape, in_specs, scratch=(), vmem=16 * MIB, flops=0, size=0):
    return pl.pallas_call(
        body,
        out_shape=out_shape,
        in_specs=in_specs,
        out_specs=jax.tree.map(lambda _: VMEM, out_shape),
        scratch_shapes=list(scratch),
        compiler_params=pltpu.CompilerParams(vmem_limit_bytes=vmem),
        cost_estimate=pl.CostEstimate(flops=flops, bytes_accessed=size, transcendentals=0),
    )


def struct(shape, dtype=bf16):
    return jax.ShapeDtypeStruct(shape, dtype)


def dot(rows, matrix):
    return jnp.dot(rows, matrix, preferred_element_type=f32)


def dot_t(left, right):
    return lax.dot_general(left, right, (((1,), (1,)), ((), ())), preferred_element_type=f32)


def columns(index, width):
    return pl.ds(pl.multiple_of(index * width, width), width)


def in_vmem(operand):
    return pltpu.with_memory_space_constraint(operand, pltpu.VMEM)


def in_hbm(operand):
    return pltpu.with_memory_space_constraint(operand, pltpu.HBM)


def weight_copies(level, place, sources, weights, sem):
    count = weights.shape[2]
    slabs = pl.ds(place[0] * count, count)
    copies = []
    for side in range(2):
        for part in range(2):
            source = sources[2 * side + part].at[level, slabs]
            copies.append(pltpu.make_async_copy(source, weights.at[side, part], sem.at[side, part]))
    return copies


def run(copies):
    for copy in copies:
        copy.start()
    for copy in copies:
        copy.wait()


def load_body(level, place, token, *rest):
    *sources, weights, sem = rest
    run(weight_copies(level, place, sources, weights, sem))


def load_last_body(level, place, token, *rest):
    *sources, final, final_other, weights, sem = rest
    count = weights.shape[2]
    slabs = pl.ds(place[0] * count, count)
    above = place[1 + level] == 0

    def copy(source, side, part):
        return pltpu.make_async_copy(source, weights.at[side, part], sem.at[side, part])

    for part in range(2):
        pl.when(above)(lambda: copy(sources[2 + part].at[level, slabs], 0, part).start())
        pl.when(jnp.logical_not(above))(lambda: copy(sources[part].at[level, slabs], 0, part).start())
    finals = [copy(ref.at[slabs], 1, part) for part, ref in enumerate((final, final_other))]
    for each in finals:
        each.start()
    for part in range(2):
        copy(sources[part].at[level, slabs], 0, part).wait()
    for each in finals:
        each.wait()


def load(body, place, token, sources):
    _, slabs, rows, half = sources[0].shape
    shape = (2, 2, slabs // 2, rows, half)
    return pl.pallas_call(
        body,
        out_shape=pltpu.VMEM(shape, bf16),
        in_specs=[SMEM] + [ANY] * (1 + len(sources)),
        out_specs=VMEM,
        scratch_shapes=[pltpu.SemaphoreType.DMA((2, 2))],
        compiler_params=pltpu.CompilerParams(vmem_limit_bytes=4 * MIB),
        cost_estimate=pl.CostEstimate(flops=0, bytes_accessed=8 * slabs * rows * half, transcendentals=0),
    )(place, token, *[in_hbm(x) for x in sources])


def load_whole_body(place, token, *rest):
    count = len(rest) // 2
    sources, targets, sem = rest[:count], rest[count:-1], rest[-1]
    run([pltpu.make_async_copy(*pair, sem.at[k]) for k, pair in enumerate(zip(sources, targets))])


def load_whole(place, token, arrays):
    return pl.pallas_call(
        load_whole_body,
        out_shape=[pltpu.VMEM(x.shape, x.dtype) for x in arrays],
        in_specs=[SMEM] + [ANY] * (1 + len(arrays)),
        out_specs=[VMEM] * len(arrays),
        scratch_shapes=[pltpu.SemaphoreType.DMA((len(arrays),))],
        compiler_params=pltpu.CompilerParams(vmem_limit_bytes=12 * MIB),
        cost_estimate=pl.CostEstimate(
            flops=0, bytes_accessed=sum(2 * x.size for x in arrays), transcendentals=0
        ),
    )(place, token, *[in_hbm(x) for x in arrays])


def image_body(place, table, extended, vectors, blocks, keep, send, moments, image):
    slabs, count, _ = vectors.shape
    reach = table.shape[1] // 2
    quotient, old = jnp.zeros((count, count), f32), jnp.zeros((count, count), f32)
    for slab in range(slabs):
        summed = None
        for entry in range(reach):
            rows = extended[table[slab, entry] + (slab + slabs)]
            term = dot(rows, blocks[table[slab, reach + entry]])
            summed = term if summed is None else summed + term
        rounded = summed.astype(bf16)
        image[slab] = rounded
        quotient = quotient + dot_t(vectors[slab], rounded)
        old = old + dot_t(vectors[slab], vectors[slab])
    moments[:, 0:count] = quotient
    moments[:, count : 2 * count] = old
    mine = slabs // 2
    keep[...] = image[pl.ds(place[0] * mine, mine)]
    send[...] = image[pl.ds((1 - place[0]) * mine, mine)]


def image_halves(place, table, extended, vectors, blocks):
    slabs, rows, half = vectors.shape
    part = struct((slabs // 2, rows, half))
    return kernel_call(
        image_body,
        (part, part, struct((rows, 2 * rows), f32)),
        [SMEM, SMEM, VMEM, VMEM, VMEM],
        [pltpu.VMEM((slabs, rows, half), bf16)],
        flops=14 * slabs * rows * 2 * half * half,
        size=2 * blocks.size,
    )(place, table, extended, vectors, blocks)


def both_parts(place, half):
    return columns(place[0], half), columns(1 - place[0], half)


def first_vectors_body(place, extended, weights, out):
    count, half = out.shape[0], weights.shape[-1]
    first = extended.shape[0] // 3 + count * place[0]
    for part, cols in enumerate(both_parts(place, half)):
        for slab in range(count):
            own = first + slab
            summed = dot(extended[own - 1], weights[0, part, slab])
            summed = summed + dot(extended[own + 1], weights[1, part, slab])
            out[slab, :, cols] = (extended[own, :, cols].astype(f32) - summed).astype(bf16)


def first_body(place, image, inner, outer, vectors, weights, out):
    count, rows, _ = image.shape
    half = weights.shape[-1]
    odd = place[0] == 1
    below = [jnp.where(odd, inner[0], outer[0])] + [image[slab] for slab in range(count - 1)]
    above = [image[slab] for slab in range(1, count)] + [jnp.where(odd, outer[0], inner[0])]
    for slab in range(count):
        out[slab, rows : 2 * rows] = vectors[slab]
    for part, cols in enumerate(both_parts(place, half)):
        for slab in range(count):
            summed = dot(below[slab], weights[0, part, slab]) + dot(above[slab], weights[1, part, slab])
            out[slab, 0:rows, cols] = (image[slab, :, cols].astype(f32) - summed).astype(bf16)


def reduce_rows(place, own, partners, sides, weights, out):
    for part, cols in enumerate(both_parts(place, weights.shape[-1])):
        for slab in range(own.shape[0]):
            summed = None
            for side, rows in zip(sides, partners):
                term = dot(rows[slab], weights[side, part, slab])
                summed = term if summed is None else summed + term
            out[slab, :, cols] = (own[slab, :, cols].astype(f32) - summed).astype(bf16)


def second_body(place, own, inner, outer, weights, moments, out):
    count, rows, _ = out.shape
    high = moments[:, 0:rows].astype(bf16)
    low = (moments[:, 0:rows] - high.astype(f32)).astype(bf16)
    factors = (high.T, low.T)
    for part, cols in enumerate(both_parts(place, weights.shape[-1])):
        for slab in range(count):
            summed = dot(inner[slab], weights[1 - place[0], part, slab])
            summed = summed + dot(outer[slab], weights[place[0], part, slab])
            both = own[slab, :, cols].astype(f32) - summed
            image, vectors = both[:rows], both[rows:].astype(bf16)
            for factor in factors:
                image = image - dot(factor, vectors)
            out[slab, :, cols] = image.astype(bf16)


def level_body(place, own, below, above, weights, out):
    reduce_rows(place, own, (below, above), (0, 1), weights, out)


def product(place, rows, weights, whole, targets):
    for part, cols in enumerate(both_parts(place, weights.shape[-1])):
        for slab in range(whole.shape[0]):
            result = dot(rows[slab], weights[part, slab]).astype(bf16)
            targets[part][slab] = result
            whole[slab, :, cols] = result


def last_body(place, own, other, weights, whole, keep, send, rows):
    reduce_rows(place, own, (other,), (0,), weights, rows)
    product(place, rows, weights.at[1], whole, (keep, send))


def final_body(place, own, final, final_other, whole, keep, send, weights, sem):
    count = own.shape[0]
    slabs = pl.ds(place[0] * count, count)
    run([
        pltpu.make_async_copy(ref.at[slabs], weights.at[part], sem.at[part])
        for part, ref in enumerate((final, final_other))
    ])
    product(place, own, weights, whole, (keep, send))


def level_flops(operand, products):
    return 2 * products * operand.size * operand.shape[-1]


def add_pairs(table, row, entries, position, inside, window, blocks, others, place, summed, slot):
    half = blocks.shape[-1]
    mine, theirs = columns(place[0], half), columns(1 - place[0], half)
    for entry in range(entries):
        source = position + table[row, entry]

        @pl.when(inside(source))
        def _():
            block = table[row, entries + entry]
            vectors = window(source)
            summed[slot, :, mine] += dot(vectors, blocks[block])
            summed[slot, :, theirs] += dot(vectors, others[block])


def own_pairs_body(place, table, levels, index, extended, image, correction, blocks, others, summed, out, shift):
    own, rows, _ = image.shape
    reach = table.shape[1] // 2
    below = extended.shape[0] // 3
    first = place[0] * own
    shift[...] = jnp.full(shift.shape, levels[index[0]], f32)
    summed[...] = jnp.zeros(summed.shape, f32)
    for slab in range(own):
        add_pairs(
            table, first + below + slab, reach, slab,
            lambda source: jnp.logical_and(source >= 0, source < own),
            lambda source: correction[source], blocks, others, place, summed, slab,
        )
    overlap = jnp.zeros((2 * rows, rows), f32)
    mixed = jnp.zeros((rows, rows), f32)
    for slab in range(own):
        vectors, fixed = extended[first + below + slab], correction[slab]
        overlap = overlap + dot_t(jnp.concatenate([vectors, fixed], 0), fixed)
        mixed = mixed + dot_t(fixed, image[slab])
    out[0 : 2 * rows, 0:rows] = jnp.zeros((2 * rows, rows), f32)
    out[0 : 2 * rows, rows : 2 * rows] = overlap
    out[2 * rows :, 0:rows] = mixed[: rows // 2]
    out[2 * rows :, rows : 2 * rows] = mixed[rows // 2 :]


def cross_pairs_body(
    place, table, extended, correction, near, far, blocks, others, begun, part, keep, send, window, summed, out
):
    own, rows, _ = correction.shape
    reach = table.shape[1] // 2
    below = window.shape[0] - own
    half = blocks.shape[-1]
    first = place[0] * own
    mine, theirs = columns(place[0], half), columns(1 - place[0], half)
    window[0:own] = far[...]
    window[own : 2 * own] = near[...]
    window[below : below + own] = correction[...]
    summed[0:below] = jnp.zeros((below,) + summed.shape[1:], f32)
    summed[below : below + own] = begun[...]

    @pl.loop(0, (below + own) * reach)
    def _(pair):
        target = lax.div(pair, reach)
        entry = pair - target * reach
        source = target + table[first + target, entry]
        inside = jnp.logical_and(source >= 0, source < below + own)

        @pl.when(jnp.logical_and(inside, (target >= below) != (source >= below)))
        def _():
            block = table[first + target, reach + entry]
            vectors = window[source]
            summed[target, :, mine] += dot(vectors, blocks[block])
            summed[target, :, theirs] += dot(vectors, others[block])

    pencil = jnp.zeros((2 * rows, rows), f32)
    for slab in range(below + own):
        basis = jnp.concatenate([extended[first + slab], window[slab]], 0)
        pencil = pencil + dot_t(basis, summed[slab].astype(bf16))
    out[...] = part[...]
    out[0 : 2 * rows, 0:rows] = pencil
    keep[...] = out[row_half(place[0], keep)]
    send[...] = out[row_half(1 - place[0], keep)]


def row_half(index, part):
    return pl.ds(pl.multiple_of(index * part.shape[0], 8), part.shape[0])


def assemble_body(scale, place, shift, moments, first, second, gram, pencil, whole):
    rows = moments.shape[0]
    whole[row_half(place[0], first)] = first[...] * scale
    whole[row_half(1 - place[0], first)] = second[...] * scale
    top, bottom = whole[0 : 2 * rows], whole[2 * rows :]
    overlap = top[:, rows:]
    mixed = jnp.concatenate([bottom[:, :rows], bottom[:, rows:]], 0)
    left = jnp.concatenate([moments[:, rows:], overlap[:rows].T], 0)
    product = jnp.concatenate([left, overlap], 1)
    gram[...] = product
    projected = jnp.concatenate([jnp.concatenate([moments[:, :rows], mixed], 0), top[:, :rows]], 1)
    pencil[...] = projected - shift[0:1] * product


def swapped(operand):
    return lax.ppermute(operand, "vec", SWAP)


def along(operand, axis, distance):
    count = lax.axis_size("slab") * (2 if axis == CHAIN else 1)
    route = [(i, i + distance) for i in range(count) if 0 <= i + distance < count]
    return lax.ppermute(operand, axis, route)


def pair_routes(distance):
    chain = 2 * lax.axis_size("slab")
    routes = []
    for bit in range(2):
        ups = [(i, i + distance) for i in range(chain - distance) if i // distance % 2 == bit]
        routes.append(ups + [(j, i) for i, j in ups])
    return [route for route in routes if route]


def summed_up(parts):
    while len(parts) > 1:
        parts = [a + b for a, b in zip(parts[::2], parts[1::2])]
    return parts[0]


def shared_out(part, reach, radix):
    slabs = lax.axis_size("slab")
    split = radix // 2
    received = []
    for offset in range(split):
        route = []
        for i in range(slabs):
            if offset:
                route.append((2 * i, 2 * (i ^ (offset * reach))))
            route.append((2 * i + 1, 2 * (i ^ ((offset + split) * reach)) + 1))
        received.append(lax.ppermute(part, CHAIN, route))
    received[0] = jnp.where(lax.axis_index("vec") == 0, part, received[0])
    return summed_up(received)


def slab_total(part):
    slabs = lax.axis_size("slab")
    reach = 1
    while reach < slabs:
        radix = min(4, slabs // reach)
        routes = [[(i, i ^ (offset * reach)) for i in range(slabs)] for offset in range(1, radix)]
        part = summed_up([part] + [lax.ppermute(part, "slab", route) for route in routes])
        reach *= radix
    return part


def on_device(
    vectors,
    blocks,
    slab_blocks,
    far_source,
    far_block,
    level_lower,
    level_upper,
    level_final,
    shift_levels,
    shift_index,
):
    slab_count, rows, half = vectors.shape
    own_count = slab_count // 2
    slabs = lax.axis_size("slab")
    chain = 2 * slabs
    width = blocks.shape[1]
    rows_total = slab_count * slabs * width
    levels = [l for l in range(level_lower.shape[0]) if 2**l < slab_count * slabs]
    slab, core = lax.axis_index("slab"), lax.axis_index("vec")
    link = 2 * slab + core
    steps = [max(2**l // own_count, 1) for l in levels]
    place = jnp.stack([core] + [link // step % 2 for step in steps]).astype(jnp.int32)

    weights = (level_lower, swapped(level_lower), level_upper, swapped(level_upper))
    below, above = along(vectors, "slab", 1), along(vectors, "slab", -1)
    slab_ids = slab * slab_count + jnp.arange(slab_count, dtype=jnp.int32)[:, None]
    near = jnp.broadcast_to(jnp.arange(-1, 2, dtype=jnp.int32), (slab_count, 3))
    table = jnp.concatenate([near, far_source - slab_ids, slab_blocks, far_block], 1)
    (held_blocks,) = load_whole(place, place, [blocks])
    extended = lax.all_gather(jnp.concatenate([below, vectors, above], 0), "vec", axis=2, tiled=True)
    keep, send, moments = image_halves(place, table, extended, vectors, in_vmem(held_blocks))
    received, moments = swapped(send), moments + swapped(moments)
    image = jnp.where(core == 0, jnp.concatenate([keep, received], 2), jnp.concatenate([received, keep], 2))
    image, moments = lax.optimization_barrier((image, moments))

    inner_route, outer_route = pair_routes(1)
    outer = lax.ppermute(lax.dynamic_slice_in_dim(image, (own_count - 1) * core, 1), CHAIN, outer_route)
    inner = swapped(lax.dynamic_slice_in_dim(image, (own_count - 1) * (1 - core), 1))
    reach = 1
    while reach < slabs:
        radix = min(8, slabs // reach)
        share = shared_out(moments, reach, radix)
        moments = share + swapped(share)
        reach *= radix
    moments = moments / rows_total

    matrices = in_vmem(load(functools.partial(load_body, 0), place, image, weights))
    vectors_1 = kernel_call(
        first_vectors_body,
        struct(image.shape),
        [SMEM] + [VMEM] * 2,
        flops=level_flops(image, 2),
    )(place, extended, matrices)
    both = kernel_call(
        first_body,
        struct((own_count, 2 * rows, width)),
        [SMEM] + [VMEM] * 5,
        flops=level_flops(image, 2),
    )(place, image, inner, outer, vectors_1, matrices)
    matrices = in_vmem(load(functools.partial(load_body, 1), place, both, weights))
    outer, inner = lax.ppermute(both, CHAIN, outer_route), swapped(both)
    residual = kernel_call(
        second_body,
        struct(image.shape),
        [SMEM] + [VMEM] * 5,
        flops=level_flops(both, 2),
    )(place, both, inner, outer, matrices, moments)

    late_blocks, late_final, residual = lax.optimization_barrier((blocks, level_final, residual))
    finals = (level_final, swapped(late_final))
    others = swapped(late_blocks)
    part = struct((own_count, rows, half))
    ends = (struct(residual.shape), part, part)
    one_partner = chain == 2 * steps[-1]
    for level, step in zip(levels[2:], steps[2:]):
        last = level == levels[-1]
        if last:
            held_blocks, others = load_whole(place, residual, [blocks, others])
        if last and one_partner:
            matrices = load(functools.partial(load_last_body, level), place, residual, weights + finals)
            (route,) = pair_routes(step)
            other = lax.ppermute(residual, CHAIN, route)
            other, held_blocks, others = lax.optimization_barrier((other, held_blocks, others))
            correction, keep, send = kernel_call(
                last_body,
                ends,
                [SMEM] + [VMEM] * 3,
                [pltpu.VMEM(residual.shape, bf16)],
                flops=level_flops(residual, 2),
            )(place, residual, other, in_vmem(matrices))
            break
        matrices = load(functools.partial(load_body, level), place, residual, weights)
        partners = [along(residual, CHAIN, step), along(residual, CHAIN, -step)]
        if level == levels[-2]:
            matrices, note = lax.optimization_barrier((matrices, table))
            lower_table = along(note, "slab", 1)
            partners, lower_table = lax.optimization_barrier((partners, lower_table))
        residual = kernel_call(
            level_body,
            struct(residual.shape),
            [SMEM] + [VMEM] * 4,
            flops=level_flops(residual, 2),
        )(place, residual, *partners, in_vmem(matrices))
    if not one_partner:
        correction, keep, send = kernel_call(
            final_body,
            ends,
            [SMEM, VMEM, ANY, ANY],
            [pltpu.VMEM((2, own_count, width, half), bf16), pltpu.SemaphoreType.DMA((2,))],
            flops=level_flops(residual, 1),
        )(place, residual, *[in_hbm(x) for x in finals])
    held_blocks, others = in_vmem(held_blocks), in_vmem(others)

    far, near = along(correction, CHAIN, 2), along(correction, CHAIN, 1)
    received = swapped(send)
    result = jnp.where(core == 0, jnp.concatenate([keep, received], 0), jnp.concatenate([received, keep], 0))
    far, near, result = lax.optimization_barrier((far, near, result))
    tables = jnp.concatenate([lower_table, table], 0)
    flops = level_flops(image, 7)
    sums = (5 * rows // 2, 2 * rows)
    begun, part, shift = kernel_call(
        own_pairs_body,
        (struct(image.shape, f32), struct(sums, f32), struct((8, 2 * rows), f32)),
        [SMEM] * 4 + [VMEM] * 5,
        flops=flops,
    )(place, tables, shift_levels, shift_index, extended, image, correction, held_blocks, others)
    share = struct((sums[0] // 2, sums[1]), f32)
    keep, send = kernel_call(
        cross_pairs_body,
        (share, share),
        [SMEM] * 2 + [VMEM] * 8,
        [
            pltpu.VMEM((3 * own_count, rows, width), bf16),
            pltpu.VMEM((3 * own_count, rows, width), f32),
            pltpu.VMEM(sums, f32),
        ],
        flops=flops,
    )(place, tables, extended, correction, near, far, held_blocks, others, begun, part)
    share = slab_total(keep + swapped(send))
    square = struct((2 * rows, 2 * rows), f32)
    gram, pencil = kernel_call(
        functools.partial(assemble_body, 1.0 / rows_total),
        (square, square),
        [SMEM] + [VMEM] * 4,
        [pltpu.VMEM(sums, f32)],
    )(place, shift, moments, share, swapped(share))
    return (result, gram, pencil)


def solution(mesh):
    in_specs = (
        P(("groups", "slab"), None, "vec"),
        P("groups", None, "vec"),
        P(("groups", "slab"), None),
        P(("groups", "slab"), None),
        P(("groups", "slab"), None),
        P(None, ("groups", "slab"), None, "vec"),
        P(None, ("groups", "slab"), None, "vec"),
        P(("groups", "slab"), None, "vec"),
        P("groups"),
        P("groups"),
    )
    out_specs = (P(("groups", "slab"), None, "vec"), P("groups", None), P("groups", None))
    return jax.shard_map(
        on_device, mesh=mesh, in_specs=in_specs, out_specs=out_specs, check_vma=False
    )
```

```python
import functools

import jax
import jax.numpy as jnp
from jax import lax
from jax.experimental import pallas as pl
from jax.experimental.pallas import tpu as pltpu
from jax.sharding import PartitionSpec as P

f32, bf16 = jnp.float32, jnp.bfloat16
CHAIN = ("slab", "vec")
ANY = pl.BlockSpec(memory_space=pl.ANY)
VMEM = pl.BlockSpec(memory_space=pltpu.VMEM)
SMEM = pl.BlockSpec(memory_space=pltpu.SMEM)
SWAP = [(0, 1), (1, 0)]
MIB = 1024 * 1024


def kernel_call(body, out_shape, in_specs, scratch=(), vmem=16 * MIB, flops=0, size=0):
    return pl.pallas_call(
        body,
        out_shape=out_shape,
        in_specs=in_specs,
        out_specs=jax.tree.map(lambda _: VMEM, out_shape),
        scratch_shapes=list(scratch),
        compiler_params=pltpu.CompilerParams(vmem_limit_bytes=vmem),
        cost_estimate=pl.CostEstimate(flops=flops, bytes_accessed=size, transcendentals=0),
    )


def struct(shape, dtype=bf16):
    return jax.ShapeDtypeStruct(shape, dtype)


def dot(rows, matrix):
    return jnp.dot(rows, matrix, preferred_element_type=f32)


def dot_t(left, right):
    return lax.dot_general(left, right, (((1,), (1,)), ((), ())), preferred_element_type=f32)


def columns(index, width):
    return pl.ds(pl.multiple_of(index * width, width), width)


def in_vmem(operand):
    return pltpu.with_memory_space_constraint(operand, pltpu.VMEM)


def in_hbm(operand):
    return pltpu.with_memory_space_constraint(operand, pltpu.HBM)


def run(copies):
    for copy in copies:
        copy.start()
    for copy in copies:
        copy.wait()


def pack_body(levels, place, token, *rest):
    *sources, sem = rest
    outs = sources[len(sources) - (2 if levels[0] == 0 else 1) :]
    lower, upper = sources[:2]
    count = outs[0].shape[1]
    copies = []
    for out, core in zip(outs, (1 - place[0], place[0])):
        slabs = pl.ds(core * count, count)
        parts = [ref.at[level, slabs] for level in levels for ref in (lower, upper)]
        if levels[0] != 0:
            parts.append(sources[2].at[slabs])
        for k, part in enumerate(parts):
            copies.append(pltpu.make_async_copy(part, out.at[k], sem.at[len(copies)]))
    run(copies)


def pack(levels, place, token, lower, upper, final=None):
    _, slabs, rows, half = lower.shape
    count = 2 * len(levels) + (0 if final is None else 1)
    shape = struct((count, slabs // 2, rows, half))
    outs = [shape] if final is not None else [shape, shape]
    operands = [in_hbm(x) for x in (lower, upper, final) if x is not None]
    return pl.pallas_call(
        functools.partial(pack_body, levels),
        out_shape=outs,
        in_specs=[SMEM] + [ANY] * (1 + len(operands)),
        out_specs=[VMEM] * len(outs),
        scratch_shapes=[pltpu.SemaphoreType.DMA((len(outs) * count,))],
        compiler_params=pltpu.CompilerParams(vmem_limit_bytes=6 * MIB),
        cost_estimate=pl.CostEstimate(
            flops=0, bytes_accessed=2 * len(outs) * count * slabs * rows * half // 2, transcendentals=0
        ),
    )(place, token, *operands)


def load_body(level, first, place, token, lower, upper, packed, weights, sem):
    count = weights.shape[2]
    slabs = pl.ds(place[0] * count, count)
    copies = []
    for side, ref in enumerate((lower, upper)):
        sources = (ref.at[level, slabs], packed.at[2 * (level - first) + side])
        for part, source in enumerate(sources):
            copies.append(pltpu.make_async_copy(source, weights.at[side, part], sem.at[side, part]))
    run(copies)


def load_last_body(level, first, place, token, lower, upper, packed, final, weights, sem):
    count = weights.shape[2]
    slabs = pl.ds(place[0] * count, count)
    above = 1 - place[1 + level]

    def copy(source, side, part):
        return pltpu.make_async_copy(source, weights.at[side, part], sem.at[side, part])

    pl.when(above == 1)(lambda: copy(upper.at[level, slabs], 0, 0).start())
    pl.when(above == 0)(lambda: copy(lower.at[level, slabs], 0, 0).start())
    others = [
        copy(packed.at[2 * (level - first) + above], 0, 1),
        copy(final.at[slabs], 1, 0),
        copy(packed.at[packed.shape[0] - 1], 1, 1),
    ]
    for each in others:
        each.start()
    copy(lower.at[level, slabs], 0, 0).wait()
    for each in others:
        each.wait()


def load(body, place, token, lower, upper, packed, *finals):
    _, slabs, rows, half = lower.shape
    shape = (2, 2, slabs // 2, rows, half)
    operands = [in_hbm(lower), in_hbm(upper), packed] + [in_hbm(x) for x in finals]
    return pl.pallas_call(
        body,
        out_shape=pltpu.VMEM(shape, bf16),
        in_specs=[SMEM] + [ANY] * (1 + len(operands)),
        out_specs=VMEM,
        scratch_shapes=[pltpu.SemaphoreType.DMA((2, 2))],
        compiler_params=pltpu.CompilerParams(vmem_limit_bytes=4 * MIB),
        cost_estimate=pl.CostEstimate(flops=0, bytes_accessed=8 * slabs * rows * half, transcendentals=0),
    )(place, token, *operands)


def load_whole_body(place, token, source, target, sem):
    run([pltpu.make_async_copy(source, target, sem.at[0])])


def load_whole(place, token, array):
    return pl.pallas_call(
        load_whole_body,
        out_shape=pltpu.VMEM(array.shape, array.dtype),
        in_specs=[SMEM, ANY, ANY],
        out_specs=VMEM,
        scratch_shapes=[pltpu.SemaphoreType.DMA((1,))],
        compiler_params=pltpu.CompilerParams(vmem_limit_bytes=6 * MIB),
        cost_estimate=pl.CostEstimate(flops=0, bytes_accessed=2 * array.size, transcendentals=0),
    )(place, token, in_hbm(array))


def image_body(place, table, extended, vectors, blocks, keep, send, moments, image):
    slabs, count, _ = vectors.shape
    reach = table.shape[1] // 2
    quotient, old = jnp.zeros((count, count), f32), jnp.zeros((count, count), f32)
    for slab in range(slabs):
        summed = None
        for entry in range(reach):
            rows = extended[table[slab, entry] + (slab + slabs)]
            term = dot(rows, blocks[table[slab, reach + entry]])
            summed = term if summed is None else summed + term
        rounded = summed.astype(bf16)
        image[slab] = rounded
        quotient = quotient + dot_t(vectors[slab], rounded)
        old = old + dot_t(vectors[slab], vectors[slab])
    moments[:, 0:count] = quotient
    moments[:, count : 2 * count] = old
    mine = slabs // 2
    keep[...] = image[pl.ds(place[0] * mine, mine)]
    send[...] = image[pl.ds((1 - place[0]) * mine, mine)]


def image_halves(place, table, extended, vectors, blocks):
    slabs, rows, half = vectors.shape
    part = struct((slabs // 2, rows, half))
    return kernel_call(
        image_body,
        (part, part, struct((rows, 2 * rows), f32)),
        [SMEM, SMEM, VMEM, VMEM, VMEM],
        [pltpu.VMEM((slabs, rows, half), bf16)],
        flops=14 * slabs * rows * 2 * half * half,
        size=2 * blocks.size,
    )(place, table, extended, vectors, blocks)


def both_parts(place, half):
    return columns(place[0], half), columns(1 - place[0], half)


def first_vectors_body(place, extended, mine, packed, out):
    count, half = out.shape[0], mine.shape[-1]
    first = extended.shape[0] // 3 + count * place[0]
    for weights, cols in zip((mine, packed), both_parts(place, half)):
        for slab in range(count):
            own = first + slab
            summed = dot(extended[own - 1], weights[0, slab])
            summed = summed + dot(extended[own + 1], weights[1, slab])
            out[slab, :, cols] = (extended[own, :, cols].astype(f32) - summed).astype(bf16)


def first_body(place, image, inner, outer, vectors, mine, packed, out):
    count, rows, _ = image.shape
    half = mine.shape[-1]
    odd = place[0] == 1
    below = [jnp.where(odd, inner[0], outer[0])] + [image[slab] for slab in range(count - 1)]
    above = [image[slab] for slab in range(1, count)] + [jnp.where(odd, outer[0], inner[0])]
    for slab in range(count):
        out[slab, rows : 2 * rows] = vectors[slab]
    for weights, cols in zip((mine, packed), both_parts(place, half)):
        for slab in range(count):
            summed = dot(below[slab], weights[0, slab]) + dot(above[slab], weights[1, slab])
            out[slab, 0:rows, cols] = (image[slab, :, cols].astype(f32) - summed).astype(bf16)


def reduce_rows(place, own, partners, sides, weights, out):
    for part, cols in enumerate(both_parts(place, weights.shape[-1])):
        for slab in range(own.shape[0]):
            summed = None
            for side, rows in zip(sides, partners):
                term = dot(rows[slab], weights[side, part, slab])
                summed = term if summed is None else summed + term
            out[slab, :, cols] = (own[slab, :, cols].astype(f32) - summed).astype(bf16)


def second_body(place, own, inner, outer, mine, packed, moments, note, out, lifted):
    count, rows, _ = out.shape
    lifted[count * rows :] = note[...]
    high = moments[:, 0:rows].astype(bf16)
    low = (moments[:, 0:rows] - high.astype(f32)).astype(bf16)
    factors = (high.T, low.T)
    for weights, cols in zip((mine, packed), both_parts(place, mine.shape[-1])):
        for slab in range(count):
            summed = dot(inner[slab], weights[2 + 1 - place[0], slab])
            summed = summed + dot(outer[slab], weights[2 + place[0], slab])
            both = own[slab, :, cols].astype(f32) - summed
            image, vectors = both[:rows], both[rows:].astype(bf16)
            for factor in factors:
                image = image - dot(factor, vectors)
            out[slab, :, cols] = image.astype(bf16)
            lifted[slab * rows : (slab + 1) * rows, cols] = image.astype(bf16)


def level_body(place, own, below, above, weights, out):
    reduce_rows(place, own, (below, above), (0, 1), weights, out)


def third_body(place, own, lifted, above, weights, out):
    count, rows, _ = own.shape
    below = [lifted[slab * rows : (slab + 1) * rows] for slab in range(count)]
    reduce_rows(place, own, (below, above), (0, 1), weights, out)


def product(place, rows, weights, whole, targets):
    for part, cols in enumerate(both_parts(place, weights.shape[-1])):
        for slab in range(whole.shape[0]):
            result = dot(rows[slab], weights[part, slab]).astype(bf16)
            targets[part][slab] = result
            whole[slab, :, cols] = result


def last_body(place, own, other, weights, whole, keep, send, rows):
    reduce_rows(place, own, (other,), (0,), weights, rows)
    product(place, rows, weights.at[1], whole, (keep, send))


def final_body(place, own, final, packed, whole, keep, send, weights, sem):
    count = own.shape[0]
    sources = (final.at[pl.ds(place[0] * count, count)], packed.at[packed.shape[0] - 1])
    run([
        pltpu.make_async_copy(source, weights.at[part], sem.at[part])
        for part, source in enumerate(sources)
    ])
    product(place, own, weights, whole, (keep, send))


def level_flops(operand, products):
    return 2 * products * operand.size * operand.shape[-1]


def add_pairs(table, row, entries, position, inside, window, blocks, others, place, summed, slot):
    half = blocks.shape[-1]
    mine, theirs = columns(place[0], half), columns(1 - place[0], half)
    for entry in range(entries):
        source = position + table[row, entry]

        @pl.when(inside(source))
        def _():
            block = table[row, entries + entry]
            vectors = window(source)
            summed[slot, :, mine] += dot(vectors, blocks[block])
            summed[slot, :, theirs] += dot(vectors, others[block])


def own_pairs_body(place, table, levels, index, extended, image, correction, blocks, others, summed, out, shift):
    own, rows, _ = image.shape
    reach = table.shape[1] // 2
    below = extended.shape[0] // 3
    first = place[0] * own
    shift[...] = jnp.full(shift.shape, levels[index[0]], f32)
    summed[...] = jnp.zeros(summed.shape, f32)
    for slab in range(own):
        add_pairs(
            table, first + below + slab, reach, slab,
            lambda source: jnp.logical_and(source >= 0, source < own),
            lambda source: correction[source], blocks, others, place, summed, slab,
        )
    overlap = jnp.zeros((2 * rows, rows), f32)
    mixed = jnp.zeros((rows, rows), f32)
    for slab in range(own):
        vectors, fixed = extended[first + below + slab], correction[slab]
        overlap = overlap + dot_t(jnp.concatenate([vectors, fixed], 0), fixed)
        mixed = mixed + dot_t(fixed, image[slab])
    out[0 : 2 * rows, 0:rows] = jnp.zeros((2 * rows, rows), f32)
    out[0 : 2 * rows, rows : 2 * rows] = overlap
    out[2 * rows :, 0:rows] = mixed[: rows // 2]
    out[2 * rows :, rows : 2 * rows] = mixed[rows // 2 :]


def cross_pairs_body(
    place, table, extended, correction, near, far, blocks, others, begun, part, keep, send, window, summed, out
):
    own, rows, _ = correction.shape
    reach = table.shape[1] // 2
    below = window.shape[0] - own
    half = blocks.shape[-1]
    first = place[0] * own
    mine, theirs = columns(place[0], half), columns(1 - place[0], half)
    window[0:own] = far[...]
    window[own : 2 * own] = near[...]
    window[below : below + own] = correction[...]
    summed[0:below] = jnp.zeros((below,) + summed.shape[1:], f32)
    summed[below : below + own] = begun[...]

    @pl.loop(0, (below + own) * reach)
    def _(pair):
        target = lax.div(pair, reach)
        entry = pair - target * reach
        source = target + table[first + target, entry]
        inside = jnp.logical_and(source >= 0, source < below + own)

        @pl.when(jnp.logical_and(inside, (target >= below) != (source >= below)))
        def _():
            block = table[first + target, reach + entry]
            vectors = window[source]
            summed[target, :, mine] += dot(vectors, blocks[block])
            summed[target, :, theirs] += dot(vectors, others[block])

    pencil = jnp.zeros((2 * rows, rows), f32)
    for slab in range(below + own):
        basis = jnp.concatenate([extended[first + slab], window[slab]], 0)
        pencil = pencil + dot_t(basis, summed[slab].astype(bf16))
    out[...] = part[...]
    out[0 : 2 * rows, 0:rows] = pencil
    keep[...] = out[row_half(place[0], keep)]
    send[...] = out[row_half(1 - place[0], keep)]


def row_half(index, part):
    return pl.ds(pl.multiple_of(index * part.shape[0], 8), part.shape[0])


def assemble_body(scale, place, shift, moments, first, second, gram, pencil, whole):
    rows = moments.shape[0]
    whole[row_half(place[0], first)] = first[...] * scale
    whole[row_half(1 - place[0], first)] = second[...] * scale
    top, bottom = whole[0 : 2 * rows], whole[2 * rows :]
    overlap = top[:, rows:]
    mixed = jnp.concatenate([bottom[:, :rows], bottom[:, rows:]], 0)
    left = jnp.concatenate([moments[:, rows:], overlap[:rows].T], 0)
    product = jnp.concatenate([left, overlap], 1)
    gram[...] = product
    projected = jnp.concatenate([jnp.concatenate([moments[:, :rows], mixed], 0), top[:, :rows]], 1)
    pencil[...] = projected - shift[0:1] * product


def swapped(operand):
    return lax.ppermute(operand, "vec", SWAP)


def along(operand, axis, distance):
    count = lax.axis_size("slab") * (2 if axis == CHAIN else 1)
    route = [(i, i + distance) for i in range(count) if 0 <= i + distance < count]
    return lax.ppermute(operand, axis, route)


def pair_routes(distance):
    chain = 2 * lax.axis_size("slab")
    routes = []
    for bit in range(2):
        ups = [(i, i + distance) for i in range(chain - distance) if i // distance % 2 == bit]
        routes.append(ups + [(j, i) for i, j in ups])
    return [route for route in routes if route]


def summed_up(parts):
    while len(parts) > 1:
        parts = [a + b for a, b in zip(parts[::2], parts[1::2])]
    return parts[0]


def shared_out(part, reach, radix):
    slabs = lax.axis_size("slab")
    split = radix // 2
    received = []
    for offset in range(split):
        route = []
        for i in range(slabs):
            if offset:
                route.append((2 * i, 2 * (i ^ (offset * reach))))
            route.append((2 * i + 1, 2 * (i ^ ((offset + split) * reach)) + 1))
        received.append(lax.ppermute(part, CHAIN, route))
    received[0] = jnp.where(lax.axis_index("vec") == 0, part, received[0])
    return summed_up(received)


def slab_total(part):
    slabs = lax.axis_size("slab")
    reach = 1
    while reach < slabs:
        radix = min(4, slabs // reach)
        routes = [[(i, i ^ (offset * reach)) for i in range(slabs)] for offset in range(1, radix)]
        part = summed_up([part] + [lax.ppermute(part, "slab", route) for route in routes])
        reach *= radix
    return part


def on_device(
    vectors,
    blocks,
    slab_blocks,
    far_source,
    far_block,
    level_lower,
    level_upper,
    level_final,
    shift_levels,
    shift_index,
):
    slab_count, rows, half = vectors.shape
    own_count = slab_count // 2
    slabs = lax.axis_size("slab")
    chain = 2 * slabs
    width = blocks.shape[1]
    rows_total = slab_count * slabs * width
    levels = [l for l in range(level_lower.shape[0]) if 2**l < slab_count * slabs]
    slab, core = lax.axis_index("slab"), lax.axis_index("vec")
    link = 2 * slab + core
    steps = [max(2**l // own_count, 1) for l in levels]
    place = jnp.stack([core] + [link // step % 2 for step in steps]).astype(jnp.int32)

    below, above = along(vectors, "slab", 1), along(vectors, "slab", -1)
    slab_ids = slab * slab_count + jnp.arange(slab_count, dtype=jnp.int32)[:, None]
    near = jnp.broadcast_to(jnp.arange(-1, 2, dtype=jnp.int32), (slab_count, 3))
    table = jnp.concatenate([near, far_source - slab_ids, slab_blocks, far_block], 1)
    note = jnp.pad(table.astype(bf16), ((0, 16 - slab_count), (0, width - table.shape[1])))
    held_blocks = load_whole(place, place, blocks)
    theirs, mine = pack(levels[:2], place, held_blocks, level_lower, level_upper)
    extended = lax.all_gather(jnp.concatenate([below, vectors, above], 0), "vec", axis=2, tiled=True)
    theirs, extended = lax.optimization_barrier((theirs, extended))
    packed, mine = in_vmem(swapped(theirs)), in_vmem(mine)
    keep, send, moments = image_halves(place, table, extended, vectors, in_vmem(held_blocks))
    received, moments = swapped(send), moments + swapped(moments)
    image = jnp.where(core == 0, jnp.concatenate([keep, received], 2), jnp.concatenate([received, keep], 2))
    image, moments = lax.optimization_barrier((image, moments))

    inner_route, outer_route = pair_routes(1)
    outer = lax.ppermute(lax.dynamic_slice_in_dim(image, (own_count - 1) * core, 1), CHAIN, outer_route)
    inner = swapped(lax.dynamic_slice_in_dim(image, (own_count - 1) * (1 - core), 1))
    reach = 1
    while True:
        radix = min(8, slabs // reach)
        share = shared_out(moments, reach, radix)
        reach *= radix
        if reach >= slabs:
            break
        moments = share + swapped(share)

    vectors_1 = kernel_call(
        first_vectors_body,
        struct(image.shape),
        [SMEM] + [VMEM] * 3,
        flops=level_flops(image, 2),
    )(place, extended, mine, packed)
    both = kernel_call(
        first_body,
        struct((own_count, 2 * rows, width)),
        [SMEM] + [VMEM] * 6,
        flops=level_flops(image, 2),
    )(place, image, inner, outer, vectors_1, mine, packed)
    both, share = lax.optimization_barrier((both, share))
    outer, inner = lax.ppermute(both, CHAIN, outer_route), swapped(both)
    moments = (share + swapped(share)) / rows_total
    (theirs,) = pack(levels[2:], place, both, level_lower, level_upper, level_final)
    theirs, inner, outer, moments = lax.optimization_barrier((theirs, inner, outer, moments))
    residual, lifted = kernel_call(
        second_body,
        (struct(image.shape), struct((own_count * rows + 16, width))),
        [SMEM] + [VMEM] * 7,
        flops=level_flops(both, 2),
    )(place, both, inner, outer, mine, packed, moments, note)

    packed = swapped(theirs)
    part = struct((own_count, rows, half))
    ends = (struct(residual.shape), part, part)
    one_partner = chain == 2 * steps[-1]
    for level, step in zip(levels[2:], steps[2:]):
        last = level == levels[-1]
        if last:
            held_blocks = load_whole(place, residual, blocks)
        if last and one_partner:
            body = functools.partial(load_last_body, level, 2)
            matrices = load(body, place, residual, level_lower, level_upper, packed, level_final)
            (route,) = pair_routes(step)
            other = lax.ppermute(residual, CHAIN, route)
            other, held_blocks = lax.optimization_barrier((other, held_blocks))
            correction, keep, send = kernel_call(
                last_body,
                ends,
                [SMEM] + [VMEM] * 3,
                [pltpu.VMEM(residual.shape, bf16)],
                flops=level_flops(residual, 2),
            )(place, residual, other, in_vmem(matrices))
            break
        body = functools.partial(load_body, level, 2)
        matrices = load(body, place, residual, level_lower, level_upper, packed)
        below, above = along(residual if level > 2 else lifted, CHAIN, step), along(residual, CHAIN, -step)
        if level == 2:
            count = own_count * rows
            lower_table = below[count : count + slab_count, : table.shape[1]].astype(jnp.int32)
        residual = kernel_call(
            level_body if level > 2 else third_body,
            struct(residual.shape),
            [SMEM] + [VMEM] * 4,
            flops=level_flops(residual, 2),
        )(place, residual, below, above, in_vmem(matrices))
        if level == 2:
            late_blocks, residual = lax.optimization_barrier((blocks, residual))
            others = swapped(late_blocks)
    if not one_partner:
        correction, keep, send = kernel_call(
            final_body,
            ends,
            [SMEM, VMEM, ANY, ANY],
            [pltpu.VMEM((2, own_count, width, half), bf16), pltpu.SemaphoreType.DMA((2,))],
            flops=level_flops(residual, 1),
        )(place, residual, in_hbm(level_final), packed)
    held_blocks, others = in_vmem(held_blocks), in_vmem(others)

    far, near = along(correction, CHAIN, 2), along(correction, CHAIN, 1)
    received = swapped(send)
    result = jnp.where(core == 0, jnp.concatenate([keep, received], 0), jnp.concatenate([received, keep], 0))
    tables = jnp.concatenate([lower_table, table], 0)
    flops = level_flops(image, 7)
    sums = (5 * rows // 2, 2 * rows)
    begun, part, shift = kernel_call(
        own_pairs_body,
        (struct(image.shape, f32), struct(sums, f32), struct((8, 2 * rows), f32)),
        [SMEM] * 4 + [VMEM] * 5,
        flops=flops,
    )(place, tables, shift_levels, shift_index, extended, image, correction, held_blocks, others)
    share = struct((sums[0] // 2, sums[1]), f32)
    keep, send = kernel_call(
        cross_pairs_body,
        (share, share),
        [SMEM] * 2 + [VMEM] * 8,
        [
            pltpu.VMEM((3 * own_count, rows, width), bf16),
            pltpu.VMEM((3 * own_count, rows, width), f32),
            pltpu.VMEM(sums, f32),
        ],
        flops=flops,
    )(place, tables, extended, correction, near, far, held_blocks, others, begun, part)
    share = slab_total(keep + swapped(send))
    square = struct((2 * rows, 2 * rows), f32)
    gram, pencil = kernel_call(
        functools.partial(assemble_body, 1.0 / rows_total),
        (square, square),
        [SMEM] + [VMEM] * 4,
        [pltpu.VMEM(sums, f32)],
    )(place, shift, moments, share, swapped(share))
    return (result, gram, pencil)


def solution(mesh):
    in_specs = (
        P(("groups", "slab"), None, "vec"),
        P("groups", None, "vec"),
        P(("groups", "slab"), None),
        P(("groups", "slab"), None),
        P(("groups", "slab"), None),
        P(None, ("groups", "slab"), None, "vec"),
        P(None, ("groups", "slab"), None, "vec"),
        P(("groups", "slab"), None, "vec"),
        P("groups"),
        P("groups"),
    )
    out_specs = (P(("groups", "slab"), None, "vec"), P("groups", None), P("groups", None))
    return jax.shard_map(
        on_device, mesh=mesh, in_specs=in_specs, out_specs=out_specs, check_vma=False
    )
```

```python
import functools

import jax
import jax.numpy as jnp
from jax import lax
from jax.experimental import pallas as pl
from jax.experimental.pallas import tpu as pltpu
from jax.sharding import PartitionSpec as P

f32, bf16 = jnp.float32, jnp.bfloat16
CHAIN = ("slab", "vec")
ANY = pl.BlockSpec(memory_space=pl.ANY)
VMEM = pl.BlockSpec(memory_space=pltpu.VMEM)
SMEM = pl.BlockSpec(memory_space=pltpu.SMEM)
SWAP = [(0, 1), (1, 0)]
MIB = 1024 * 1024


def kernel_call(body, out_shape, in_specs, scratch=(), vmem=16 * MIB, flops=0, size=0):
    return pl.pallas_call(
        body,
        out_shape=out_shape,
        in_specs=in_specs,
        out_specs=jax.tree.map(lambda _: VMEM, out_shape),
        scratch_shapes=list(scratch),
        compiler_params=pltpu.CompilerParams(vmem_limit_bytes=vmem),
        cost_estimate=pl.CostEstimate(flops=flops, bytes_accessed=size, transcendentals=0),
    )


def struct(shape, dtype=bf16):
    return jax.ShapeDtypeStruct(shape, dtype)


def dot(rows, matrix):
    return jnp.dot(rows, matrix, preferred_element_type=f32)


def dot_t(left, right):
    return lax.dot_general(left, right, (((1,), (1,)), ((), ())), preferred_element_type=f32)


def columns(index, width):
    return pl.ds(pl.multiple_of(index * width, width), width)


def in_vmem(operand):
    return pltpu.with_memory_space_constraint(operand, pltpu.VMEM)


def in_hbm(operand):
    return pltpu.with_memory_space_constraint(operand, pltpu.HBM)


def run(copies):
    for copy in copies:
        copy.start()
    for copy in copies:
        copy.wait()


def pack_body(levels, place, token, lower, upper, *rest):
    *final, out, sem = rest
    count = out.shape[1]
    slabs = pl.ds((1 - place[0]) * count, count)
    parts = [ref.at[level, slabs] for level in levels for ref in (lower, upper)]
    parts += [ref.at[slabs] for ref in final]
    run([pltpu.make_async_copy(part, out.at[k], sem.at[k]) for k, part in enumerate(parts)])


def pack(levels, place, token, *operands):
    _, slabs, rows, half = operands[0].shape
    count = 2 * len(levels) + len(operands) - 2
    out = struct((count, slabs // 2, rows, half))
    return pl.pallas_call(
        functools.partial(pack_body, levels),
        out_shape=out,
        in_specs=[SMEM] + [ANY] * (1 + len(operands)),
        out_specs=VMEM,
        scratch_shapes=[pltpu.SemaphoreType.DMA((count,))],
        compiler_params=pltpu.CompilerParams(vmem_limit_bytes=6 * MIB),
        cost_estimate=pl.CostEstimate(flops=0, bytes_accessed=2 * out.size, transcendentals=0),
    )(place, token, *[in_hbm(x) for x in operands])


def load_body(level, first, place, token, lower, upper, packed, weights, sem):
    count = weights.shape[2]
    slabs = pl.ds(place[0] * count, count)
    copies = []
    for side, ref in enumerate((lower, upper)):
        sources = (ref.at[level, slabs], packed.at[2 * (level - first) + side])
        for part, source in enumerate(sources):
            copies.append(pltpu.make_async_copy(source, weights.at[side, part], sem.at[side, part]))
    run(copies)


def load_last_body(level, first, place, token, lower, upper, packed, final, weights, sem):
    count = weights.shape[2]
    slabs = pl.ds(place[0] * count, count)
    above = 1 - place[1 + level]

    def copy(source, side, part):
        return pltpu.make_async_copy(source, weights.at[side, part], sem.at[side, part])

    pl.when(above == 1)(lambda: copy(upper.at[level, slabs], 0, 0).start())
    pl.when(above == 0)(lambda: copy(lower.at[level, slabs], 0, 0).start())
    others = [
        copy(packed.at[2 * (level - first) + above], 0, 1),
        copy(final.at[slabs], 1, 0),
        copy(packed.at[packed.shape[0] - 1], 1, 1),
    ]
    for each in others:
        each.start()
    copy(lower.at[level, slabs], 0, 0).wait()
    for each in others:
        each.wait()


def load(body, place, token, lower, upper, packed, *finals):
    _, slabs, rows, half = lower.shape
    shape = (2, 2, slabs // 2, rows, half)
    operands = [in_hbm(lower), in_hbm(upper), packed] + [in_hbm(x) for x in finals]
    return pl.pallas_call(
        body,
        out_shape=pltpu.VMEM(shape, bf16),
        in_specs=[SMEM] + [ANY] * (1 + len(operands)),
        out_specs=VMEM,
        scratch_shapes=[pltpu.SemaphoreType.DMA((2, 2))],
        compiler_params=pltpu.CompilerParams(vmem_limit_bytes=4 * MIB),
        cost_estimate=pl.CostEstimate(flops=0, bytes_accessed=8 * slabs * rows * half, transcendentals=0),
    )(place, token, *operands)


def load_whole_body(place, token, source, target, sem):
    run([pltpu.make_async_copy(source, target, sem.at[0])])


def load_whole(place, token, array):
    return pl.pallas_call(
        load_whole_body,
        out_shape=pltpu.VMEM(array.shape, array.dtype),
        in_specs=[SMEM, ANY, ANY],
        out_specs=VMEM,
        scratch_shapes=[pltpu.SemaphoreType.DMA((1,))],
        compiler_params=pltpu.CompilerParams(vmem_limit_bytes=6 * MIB),
        cost_estimate=pl.CostEstimate(flops=0, bytes_accessed=2 * array.size, transcendentals=0),
    )(place, token, in_hbm(array))


def image_body(place, table, extended, vectors, blocks, keep, send, moments, image):
    slabs, count, _ = vectors.shape
    reach = table.shape[1] // 2
    quotient, old = jnp.zeros((count, count), f32), jnp.zeros((count, count), f32)
    for slab in range(slabs):
        summed = None
        for entry in range(reach):
            rows = extended[table[slab, entry] + (slab + slabs)]
            term = dot(rows, blocks[table[slab, reach + entry]])
            summed = term if summed is None else summed + term
        rounded = summed.astype(bf16)
        image[slab] = rounded
        quotient = quotient + dot_t(vectors[slab], rounded)
        old = old + dot_t(vectors[slab], vectors[slab])
    moments[:, 0:count] = quotient
    moments[:, count : 2 * count] = old
    mine = slabs // 2
    keep[...] = image[pl.ds(place[0] * mine, mine)]
    send[...] = image[pl.ds((1 - place[0]) * mine, mine)]


def image_halves(place, table, extended, vectors, blocks):
    slabs, rows, half = vectors.shape
    part = struct((slabs // 2, rows, half))
    return kernel_call(
        image_body,
        (part, part, struct((rows, 2 * rows), f32)),
        [SMEM, SMEM, VMEM, VMEM, VMEM],
        [pltpu.VMEM((slabs, rows, half), bf16)],
        flops=14 * slabs * rows * 2 * half * half,
        size=2 * blocks.size,
    )(place, table, extended, vectors, blocks)


def both_parts(place, half):
    return columns(place[0], half), columns(1 - place[0], half)


def first_vectors_body(place, extended, weights, out):
    count, half = out.shape[0], weights.shape[-1]
    first = extended.shape[0] // 3 + count * place[0]
    for part, cols in enumerate(both_parts(place, half)):
        for slab in range(count):
            own = first + slab
            summed = dot(extended[own - 1], weights[0, part, slab])
            summed = summed + dot(extended[own + 1], weights[1, part, slab])
            out[slab, :, cols] = (extended[own, :, cols].astype(f32) - summed).astype(bf16)


def first_body(place, image, inner, outer, vectors, weights, out):
    count, rows, _ = image.shape
    half = weights.shape[-1]
    odd = place[0] == 1
    below = [jnp.where(odd, inner[0], outer[0])] + [image[slab] for slab in range(count - 1)]
    above = [image[slab] for slab in range(1, count)] + [jnp.where(odd, outer[0], inner[0])]
    for slab in range(count):
        out[slab, rows : 2 * rows] = vectors[slab]
    for part, cols in enumerate(both_parts(place, half)):
        for slab in range(count):
            summed = dot(below[slab], weights[0, part, slab]) + dot(above[slab], weights[1, part, slab])
            out[slab, 0:rows, cols] = (image[slab, :, cols].astype(f32) - summed).astype(bf16)


def reduce_rows(place, own, partners, sides, weights, out):
    for part, cols in enumerate(both_parts(place, weights.shape[-1])):
        for slab in range(own.shape[0]):
            summed = None
            for side, rows in zip(sides, partners):
                term = dot(rows[slab], weights[side, part, slab])
                summed = term if summed is None else summed + term
            out[slab, :, cols] = (own[slab, :, cols].astype(f32) - summed).astype(bf16)


def second_body(place, own, inner, outer, weights, moments, note, out, lifted):
    count, rows, _ = out.shape
    lifted[count * rows :] = note[...]
    high = moments[:, 0:rows].astype(bf16)
    low = (moments[:, 0:rows] - high.astype(f32)).astype(bf16)
    factors = (high.T, low.T)
    for part, cols in enumerate(both_parts(place, weights.shape[-1])):
        for slab in range(count):
            summed = dot(inner[slab], weights[1 - place[0], part, slab])
            summed = summed + dot(outer[slab], weights[place[0], part, slab])
            both = own[slab, :, cols].astype(f32) - summed
            image, vectors = both[:rows], both[rows:].astype(bf16)
            for factor in factors:
                image = image - dot(factor, vectors)
            out[slab, :, cols] = image.astype(bf16)
            lifted[slab * rows : (slab + 1) * rows, cols] = image.astype(bf16)


def level_body(place, own, below, above, weights, out):
    reduce_rows(place, own, (below, above), (0, 1), weights, out)


def third_body(place, own, lifted, above, weights, out):
    count, rows, _ = own.shape
    below = [lifted[slab * rows : (slab + 1) * rows] for slab in range(count)]
    reduce_rows(place, own, (below, above), (0, 1), weights, out)


def product(place, rows, weights, whole, targets):
    for part, cols in enumerate(both_parts(place, weights.shape[-1])):
        for slab in range(whole.shape[0]):
            result = dot(rows[slab], weights[part, slab]).astype(bf16)
            targets[part][slab] = result
            whole[slab, :, cols] = result


def last_body(place, own, other, weights, whole, keep, send, rows):
    reduce_rows(place, own, (other,), (0,), weights, rows)
    product(place, rows, weights.at[1], whole, (keep, send))


def final_body(place, own, final, packed, whole, keep, send, weights, sem):
    count = own.shape[0]
    sources = (final.at[pl.ds(place[0] * count, count)], packed.at[packed.shape[0] - 1])
    run([
        pltpu.make_async_copy(source, weights.at[part], sem.at[part])
        for part, source in enumerate(sources)
    ])
    product(place, own, weights, whole, (keep, send))


def level_flops(operand, products):
    return 2 * products * operand.size * operand.shape[-1]


def add_pairs(table, row, entries, position, inside, window, blocks, others, place, summed, slot):
    half = blocks.shape[-1]
    mine, theirs = columns(place[0], half), columns(1 - place[0], half)
    for entry in range(entries):
        source = position + table[row, entry]

        @pl.when(inside(source))
        def _():
            block = table[row, entries + entry]
            vectors = window(source)
            summed[slot, :, mine] += dot(vectors, blocks[block])
            summed[slot, :, theirs] += dot(vectors, others[block])


def own_pairs_body(place, table, levels, index, extended, image, correction, blocks, others, summed, out, shift):
    own, rows, _ = image.shape
    reach = table.shape[1] // 2
    below = extended.shape[0] // 3
    first = place[0] * own
    shift[...] = jnp.full(shift.shape, levels[index[0]], f32)
    summed[...] = jnp.zeros(summed.shape, f32)
    for slab in range(own):
        add_pairs(
            table, first + below + slab, reach, slab,
            lambda source: jnp.logical_and(source >= 0, source < own),
            lambda source: correction[source], blocks, others, place, summed, slab,
        )
    overlap = jnp.zeros((2 * rows, rows), f32)
    mixed = jnp.zeros((rows, rows), f32)
    for slab in range(own):
        vectors, fixed = extended[first + below + slab], correction[slab]
        overlap = overlap + dot_t(jnp.concatenate([vectors, fixed], 0), fixed)
        mixed = mixed + dot_t(fixed, image[slab])
    out[0 : 2 * rows, 0:rows] = jnp.zeros((2 * rows, rows), f32)
    out[0 : 2 * rows, rows : 2 * rows] = overlap
    out[2 * rows :, 0:rows] = mixed[: rows // 2]
    out[2 * rows :, rows : 2 * rows] = mixed[rows // 2 :]


def cross_pairs_body(
    place, table, extended, correction, near, far, blocks, others, begun, part, keep, send, window, summed, out
):
    own, rows, _ = correction.shape
    reach = table.shape[1] // 2
    below = window.shape[0] - own
    half = blocks.shape[-1]
    first = place[0] * own
    mine, theirs = columns(place[0], half), columns(1 - place[0], half)
    window[0:own] = far[...]
    window[own : 2 * own] = near[...]
    window[below : below + own] = correction[...]
    summed[0:below] = jnp.zeros((below,) + summed.shape[1:], f32)
    summed[below : below + own] = begun[...]

    @pl.loop(0, (below + own) * reach)
    def _(pair):
        target = lax.div(pair, reach)
        entry = pair - target * reach
        source = target + table[first + target, entry]
        inside = jnp.logical_and(source >= 0, source < below + own)

        @pl.when(jnp.logical_and(inside, (target >= below) != (source >= below)))
        def _():
            block = table[first + target, reach + entry]
            vectors = window[source]
            summed[target, :, mine] += dot(vectors, blocks[block])
            summed[target, :, theirs] += dot(vectors, others[block])

    pencil = jnp.zeros((2 * rows, rows), f32)
    for slab in range(below + own):
        basis = jnp.concatenate([extended[first + slab], window[slab]], 0)
        pencil = pencil + dot_t(basis, summed[slab].astype(bf16))
    out[...] = part[...]
    out[0 : 2 * rows, 0:rows] = pencil
    keep[...] = out[row_half(place[0], keep)]
    send[...] = out[row_half(1 - place[0], keep)]


def row_half(index, part):
    return pl.ds(pl.multiple_of(index * part.shape[0], 8), part.shape[0])


def assemble_body(scale, place, shift, moments, first, second, gram, pencil, whole):
    rows = moments.shape[0]
    whole[row_half(place[0], first)] = first[...] * scale
    whole[row_half(1 - place[0], first)] = second[...] * scale
    top, bottom = whole[0 : 2 * rows], whole[2 * rows :]
    overlap = top[:, rows:]
    mixed = jnp.concatenate([bottom[:, :rows], bottom[:, rows:]], 0)
    left = jnp.concatenate([moments[:, rows:], overlap[:rows].T], 0)
    product = jnp.concatenate([left, overlap], 1)
    gram[...] = product
    projected = jnp.concatenate([jnp.concatenate([moments[:, :rows], mixed], 0), top[:, :rows]], 1)
    pencil[...] = projected - shift[0:1] * product


def swapped(operand):
    return lax.ppermute(operand, "vec", SWAP)


def along(operand, axis, distance):
    count = lax.axis_size("slab") * (2 if axis == CHAIN else 1)
    route = [(i, i + distance) for i in range(count) if 0 <= i + distance < count]
    return lax.ppermute(operand, axis, route)


def pair_routes(distance):
    chain = 2 * lax.axis_size("slab")
    routes = []
    for bit in range(2):
        ups = [(i, i + distance) for i in range(chain - distance) if i // distance % 2 == bit]
        routes.append(ups + [(j, i) for i, j in ups])
    return [route for route in routes if route]


def summed_up(parts):
    while len(parts) > 1:
        parts = [a + b for a, b in zip(parts[::2], parts[1::2])]
    return parts[0]


def slab_total(part):
    slabs = lax.axis_size("slab")
    reach = 1
    while reach < slabs:
        radix = min(4, slabs // reach)
        routes = [[(i, i ^ (offset * reach)) for i in range(slabs)] for offset in range(1, radix)]
        part = summed_up([part] + [lax.ppermute(part, "slab", route) for route in routes])
        reach *= radix
    return part


def on_device(
    vectors,
    blocks,
    slab_blocks,
    far_source,
    far_block,
    level_lower,
    level_upper,
    level_final,
    shift_levels,
    shift_index,
):
    slab_count, rows, half = vectors.shape
    own_count = slab_count // 2
    slabs = lax.axis_size("slab")
    chain = 2 * slabs
    width = blocks.shape[1]
    rows_total = slab_count * slabs * width
    levels = [l for l in range(level_lower.shape[0]) if 2**l < slab_count * slabs]
    slab, core = lax.axis_index("slab"), lax.axis_index("vec")
    link = 2 * slab + core
    steps = [max(2**l // own_count, 1) for l in levels]
    place = jnp.stack([core] + [link // step % 2 for step in steps]).astype(jnp.int32)

    below, above = along(vectors, "slab", 1), along(vectors, "slab", -1)
    slab_ids = slab * slab_count + jnp.arange(slab_count, dtype=jnp.int32)[:, None]
    near = jnp.broadcast_to(jnp.arange(-1, 2, dtype=jnp.int32), (slab_count, 3))
    table = jnp.concatenate([near, far_source - slab_ids, slab_blocks, far_block], 1)
    note = jnp.pad(table.astype(bf16), ((0, 16 - slab_count), (0, width - table.shape[1])))
    held_blocks = load_whole(place, place, blocks)
    theirs = pack(levels[:3], place, held_blocks, level_lower, level_upper)
    extended = lax.all_gather(jnp.concatenate([below, vectors, above], 0), "vec", axis=2, tiled=True)
    theirs, extended = lax.optimization_barrier((theirs, extended))
    keep, send, moments = image_halves(place, table, extended, vectors, in_vmem(held_blocks))
    received, moments = swapped(send), moments + swapped(moments)
    image = jnp.where(core == 0, jnp.concatenate([keep, received], 2), jnp.concatenate([received, keep], 2))
    image, moments, theirs = lax.optimization_barrier((image, moments, theirs))
    packed = swapped(theirs)

    inner_route, outer_route = pair_routes(1)
    outer = lax.ppermute(lax.dynamic_slice_in_dim(image, (own_count - 1) * core, 1), CHAIN, outer_route)
    inner = swapped(lax.dynamic_slice_in_dim(image, (own_count - 1) * (1 - core), 1))
    flips = [[(i, i ^ 2**bit) for i in range(slabs)] for bit in range((slabs - 1).bit_length())]
    received = lax.ppermute(moments, "slab", flips[0])
    body = functools.partial(load_body, 0, 0)
    matrices = in_vmem(load(body, place, image, level_lower, level_upper, packed))
    vectors_1 = kernel_call(
        first_vectors_body,
        struct(image.shape),
        [SMEM] + [VMEM] * 2,
        flops=level_flops(image, 2),
    )(place, extended, matrices)
    both = kernel_call(
        first_body,
        struct((own_count, 2 * rows, width)),
        [SMEM] + [VMEM] * 5,
        flops=level_flops(image, 2),
    )(place, image, inner, outer, vectors_1, matrices)
    both, received = lax.optimization_barrier((both, received))
    outer, inner = lax.ppermute(both, CHAIN, outer_route), swapped(both)
    for flip in flips[1:]:
        moments = moments + received
        received = lax.ppermute(moments, "slab", flip)
    moments = (moments + received) / rows_total
    body = functools.partial(load_body, 1, 0)
    matrices = in_vmem(load(body, place, both, level_lower, level_upper, packed))
    residual, lifted = kernel_call(
        second_body,
        (struct(image.shape), struct((own_count * rows + 16, width))),
        [SMEM] + [VMEM] * 6,
        flops=level_flops(both, 2),
    )(place, both, inner, outer, matrices, moments, note)

    part = struct((own_count, rows, half))
    ends = (struct(residual.shape), part, part)
    one_partner = chain == 2 * steps[-1]
    for level, step in zip(levels[2:], steps[2:]):
        last = level == levels[-1]
        if last:
            held_blocks = load_whole(place, residual, blocks)
        if last and one_partner:
            body = functools.partial(load_last_body, level, 3)
            matrices = load(body, place, residual, level_lower, level_upper, packed, level_final)
            (route,) = pair_routes(step)
            other = lax.ppermute(residual, CHAIN, route)
            other, held_blocks = lax.optimization_barrier((other, held_blocks))
            correction, keep, send = kernel_call(
                last_body,
                ends,
                [SMEM] + [VMEM] * 3,
                [pltpu.VMEM(residual.shape, bf16)],
                flops=level_flops(residual, 2),
            )(place, residual, other, in_vmem(matrices))
            break
        body = functools.partial(load_body, level, 0 if level == 2 else 3)
        matrices = load(body, place, residual, level_lower, level_upper, packed)
        below, above = along(residual if level > 2 else lifted, CHAIN, step), along(residual, CHAIN, -step)
        if level == 2:
            count = own_count * rows
            lower_table = below[count : count + slab_count, : table.shape[1]].astype(jnp.int32)
            theirs = pack(levels[3:], place, matrices, level_lower, level_upper, level_final)
            theirs, below, above = lax.optimization_barrier((theirs, below, above))
            packed = swapped(theirs)
        if level == 3:
            late_blocks, below, above = lax.optimization_barrier((blocks, below, above))
            others = swapped(late_blocks)
        residual = kernel_call(
            level_body if level > 2 else third_body,
            struct(residual.shape),
            [SMEM] + [VMEM] * 4,
            flops=level_flops(residual, 2),
        )(place, residual, below, above, in_vmem(matrices))
    if not one_partner:
        correction, keep, send = kernel_call(
            final_body,
            ends,
            [SMEM, VMEM, ANY, ANY],
            [pltpu.VMEM((2, own_count, width, half), bf16), pltpu.SemaphoreType.DMA((2,))],
            flops=level_flops(residual, 1),
        )(place, residual, in_hbm(level_final), packed)
    held_blocks, others = in_vmem(held_blocks), in_vmem(others)

    far, near = along(correction, CHAIN, 2), along(correction, CHAIN, 1)
    received = swapped(send)
    result = jnp.where(core == 0, jnp.concatenate([keep, received], 0), jnp.concatenate([received, keep], 0))
    tables = jnp.concatenate([lower_table, table], 0)
    flops = level_flops(image, 7)
    sums = (5 * rows // 2, 2 * rows)
    begun, part, shift = kernel_call(
        own_pairs_body,
        (struct(image.shape, f32), struct(sums, f32), struct((8, 2 * rows), f32)),
        [SMEM] * 4 + [VMEM] * 5,
        flops=flops,
    )(place, tables, shift_levels, shift_index, extended, image, correction, held_blocks, others)
    share = struct((sums[0] // 2, sums[1]), f32)
    keep, send = kernel_call(
        cross_pairs_body,
        (share, share),
        [SMEM] * 2 + [VMEM] * 8,
        [
            pltpu.VMEM((3 * own_count, rows, width), bf16),
            pltpu.VMEM((3 * own_count, rows, width), f32),
            pltpu.VMEM(sums, f32),
        ],
        flops=flops,
    )(place, tables, extended, correction, near, far, held_blocks, others, begun, part)
    share = slab_total(keep + swapped(send))
    square = struct((2 * rows, 2 * rows), f32)
    gram, pencil = kernel_call(
        functools.partial(assemble_body, 1.0 / rows_total),
        (square, square),
        [SMEM] + [VMEM] * 4,
        [pltpu.VMEM(sums, f32)],
    )(place, shift, moments, share, swapped(share))
    return (result, gram, pencil)


def solution(mesh):
    in_specs = (
        P(("groups", "slab"), None, "vec"),
        P("groups", None, "vec"),
        P(("groups", "slab"), None),
        P(("groups", "slab"), None),
        P(("groups", "slab"), None),
        P(None, ("groups", "slab"), None, "vec"),
        P(None, ("groups", "slab"), None, "vec"),
        P(("groups", "slab"), None, "vec"),
        P("groups"),
        P("groups"),
    )
    out_specs = (P(("groups", "slab"), None, "vec"), P("groups", None), P("groups", None))
    return jax.shard_map(
        on_device, mesh=mesh, in_specs=in_specs, out_specs=out_specs, check_vma=False
    )
```

```python
import functools

import jax
import jax.numpy as jnp
from jax import lax
from jax.experimental import pallas as pl
from jax.experimental.pallas import tpu as pltpu
from jax.sharding import PartitionSpec as P

f32, bf16 = jnp.float32, jnp.bfloat16
CHAIN = ("slab", "vec")
ANY = pl.BlockSpec(memory_space=pl.ANY)
VMEM = pl.BlockSpec(memory_space=pltpu.VMEM)
SMEM = pl.BlockSpec(memory_space=pltpu.SMEM)
SWAP = [(0, 1), (1, 0)]
MIB = 1024 * 1024


def kernel_call(body, out_shape, in_specs, scratch=(), vmem=16 * MIB, flops=0, size=0):
    return pl.pallas_call(
        body,
        out_shape=out_shape,
        in_specs=in_specs,
        out_specs=jax.tree.map(lambda _: VMEM, out_shape),
        scratch_shapes=list(scratch),
        compiler_params=pltpu.CompilerParams(vmem_limit_bytes=vmem),
        cost_estimate=pl.CostEstimate(flops=flops, bytes_accessed=size, transcendentals=0),
    )


def struct(shape, dtype=bf16):
    return jax.ShapeDtypeStruct(shape, dtype)


def dot(rows, matrix):
    return jnp.dot(rows, matrix, preferred_element_type=f32)


def dot_t(left, right):
    return lax.dot_general(left, right, (((1,), (1,)), ((), ())), preferred_element_type=f32)


def columns(index, width):
    return pl.ds(pl.multiple_of(index * width, width), width)


def in_vmem(operand):
    return pltpu.with_memory_space_constraint(operand, pltpu.VMEM)


def in_hbm(operand):
    return pltpu.with_memory_space_constraint(operand, pltpu.HBM)


def run(copies):
    for copy in copies:
        copy.start()
    for copy in copies:
        copy.wait()


def pack_body(levels, place, token, lower, upper, *rest):
    *final, out, held, sem = rest
    count = out.shape[1]
    slabs = pl.ds((1 - place[0]) * count, count)
    parts = [ref.at[level, slabs] for level in levels for ref in (lower, upper)]
    parts += [ref.at[slabs] for ref in final]
    ins = [pltpu.make_async_copy(part, held.at[k], sem.at[0, k]) for k, part in enumerate(parts)]
    outs = [pltpu.make_async_copy(held.at[k], out.at[k], sem.at[1, k]) for k in range(len(parts))]
    for copy in ins:
        copy.start()
    for copy, following in zip(ins, outs):
        copy.wait()
        following.start()
    for copy in outs:
        copy.wait()


def pack(levels, place, token, *operands):
    _, slabs, rows, half = operands[0].shape
    count = 2 * len(levels) + len(operands) - 2
    shape = (count, slabs // 2, rows, half)
    return pl.pallas_call(
        functools.partial(pack_body, levels),
        out_shape=pltpu.HBM(shape, bf16),
        in_specs=[SMEM] + [ANY] * (1 + len(operands)),
        out_specs=ANY,
        scratch_shapes=[pltpu.VMEM(shape, bf16), pltpu.SemaphoreType.DMA((2, count))],
        compiler_params=pltpu.CompilerParams(vmem_limit_bytes=6 * MIB),
        cost_estimate=pl.CostEstimate(
            flops=0, bytes_accessed=4 * count * (slabs // 2) * rows * half, transcendentals=0
        ),
    )(place, token, *[in_hbm(x) for x in operands])


def load_body(level, first, place, token, lower, upper, packed, weights, sem):
    count = weights.shape[2]
    slabs = pl.ds(place[0] * count, count)
    copies = []
    for side, ref in enumerate((lower, upper)):
        sources = (ref.at[level, slabs], packed.at[2 * (level - first) + side])
        for part, source in enumerate(sources):
            copies.append(pltpu.make_async_copy(source, weights.at[side, part], sem.at[side, part]))
    run(copies)


def load_last_body(level, first, place, token, lower, upper, packed, final, weights, sem):
    count = weights.shape[2]
    slabs = pl.ds(place[0] * count, count)
    above = 1 - place[1 + level]

    def copy(source, side, part):
        return pltpu.make_async_copy(source, weights.at[side, part], sem.at[side, part])

    pl.when(above == 1)(lambda: copy(upper.at[level, slabs], 0, 0).start())
    pl.when(above == 0)(lambda: copy(lower.at[level, slabs], 0, 0).start())
    others = [
        copy(packed.at[2 * (level - first) + above], 0, 1),
        copy(final.at[slabs], 1, 0),
        copy(packed.at[packed.shape[0] - 1], 1, 1),
    ]
    for each in others:
        each.start()
    copy(lower.at[level, slabs], 0, 0).wait()
    for each in others:
        each.wait()


def load(body, place, token, lower, upper, packed, *finals):
    _, slabs, rows, half = lower.shape
    shape = (2, 2, slabs // 2, rows, half)
    operands = [in_hbm(lower), in_hbm(upper), packed] + [in_hbm(x) for x in finals]
    return pl.pallas_call(
        body,
        out_shape=pltpu.VMEM(shape, bf16),
        in_specs=[SMEM] + [ANY] * (1 + len(operands)),
        out_specs=VMEM,
        scratch_shapes=[pltpu.SemaphoreType.DMA((2, 2))],
        compiler_params=pltpu.CompilerParams(vmem_limit_bytes=4 * MIB),
        cost_estimate=pl.CostEstimate(flops=0, bytes_accessed=8 * slabs * rows * half, transcendentals=0),
    )(place, token, *operands)


def load_whole_body(place, token, source, target, sem):
    run([pltpu.make_async_copy(source, target, sem.at[0])])


def load_whole(place, token, array):
    return pl.pallas_call(
        load_whole_body,
        out_shape=pltpu.VMEM(array.shape, array.dtype),
        in_specs=[SMEM, ANY, ANY],
        out_specs=VMEM,
        scratch_shapes=[pltpu.SemaphoreType.DMA((1,))],
        compiler_params=pltpu.CompilerParams(vmem_limit_bytes=6 * MIB),
        cost_estimate=pl.CostEstimate(flops=0, bytes_accessed=2 * array.size, transcendentals=0),
    )(place, token, in_hbm(array))


def image_body(place, table, extended, vectors, blocks, keep, send, moments, image):
    slabs, count, _ = vectors.shape
    reach = table.shape[1] // 2
    quotient, old = jnp.zeros((count, count), f32), jnp.zeros((count, count), f32)
    for slab in range(slabs):
        summed = None
        for entry in range(reach):
            rows = extended[table[slab, entry] + (slab + slabs)]
            term = dot(rows, blocks[table[slab, reach + entry]])
            summed = term if summed is None else summed + term
        rounded = summed.astype(bf16)
        image[slab] = rounded
        quotient = quotient + dot_t(vectors[slab], rounded)
        old = old + dot_t(vectors[slab], vectors[slab])
    moments[:, 0:count] = quotient
    moments[:, count : 2 * count] = old
    mine = slabs // 2
    keep[...] = image[pl.ds(place[0] * mine, mine)]
    send[...] = image[pl.ds((1 - place[0]) * mine, mine)]


def image_halves(place, table, extended, vectors, blocks):
    slabs, rows, half = vectors.shape
    part = struct((slabs // 2, rows, half))
    return kernel_call(
        image_body,
        (part, part, struct((rows, 2 * rows), f32)),
        [SMEM, SMEM, VMEM, VMEM, VMEM],
        [pltpu.VMEM((slabs, rows, half), bf16)],
        flops=14 * slabs * rows * 2 * half * half,
        size=2 * blocks.size,
    )(place, table, extended, vectors, blocks)


def both_parts(place, half):
    return columns(place[0], half), columns(1 - place[0], half)


def first_vectors_body(place, extended, weights, out):
    count, half = out.shape[0], weights.shape[-1]
    first = extended.shape[0] // 3 + count * place[0]
    for part, cols in enumerate(both_parts(place, half)):
        for slab in range(count):
            own = first + slab
            summed = dot(extended[own - 1], weights[0, part, slab])
            summed = summed + dot(extended[own + 1], weights[1, part, slab])
            out[slab, :, cols] = (extended[own, :, cols].astype(f32) - summed).astype(bf16)


def first_body(place, image, inner, outer, vectors, weights, out):
    count, rows, _ = image.shape
    half = weights.shape[-1]
    odd = place[0] == 1
    below = [jnp.where(odd, inner[0], outer[0])] + [image[slab] for slab in range(count - 1)]
    above = [image[slab] for slab in range(1, count)] + [jnp.where(odd, outer[0], inner[0])]
    for slab in range(count):
        out[slab, rows : 2 * rows] = vectors[slab]
    for part, cols in enumerate(both_parts(place, half)):
        for slab in range(count):
            summed = dot(below[slab], weights[0, part, slab]) + dot(above[slab], weights[1, part, slab])
            out[slab, 0:rows, cols] = (image[slab, :, cols].astype(f32) - summed).astype(bf16)


def reduce_rows(place, own, partners, sides, weights, out):
    for part, cols in enumerate(both_parts(place, weights.shape[-1])):
        for slab in range(own.shape[0]):
            summed = None
            for side, rows in zip(sides, partners):
                term = dot(rows[slab], weights[side, part, slab])
                summed = term if summed is None else summed + term
            out[slab, :, cols] = (own[slab, :, cols].astype(f32) - summed).astype(bf16)


def second_body(place, own, inner, outer, weights, moments, note, out, lifted):
    count, rows, _ = out.shape
    lifted[count * rows :] = note[...]
    high = moments[:, 0:rows].astype(bf16)
    low = (moments[:, 0:rows] - high.astype(f32)).astype(bf16)
    factors = (high.T, low.T)
    for part, cols in enumerate(both_parts(place, weights.shape[-1])):
        for slab in range(count):
            summed = dot(inner[slab], weights[1 - place[0], part, slab])
            summed = summed + dot(outer[slab], weights[place[0], part, slab])
            both = own[slab, :, cols].astype(f32) - summed
            image, vectors = both[:rows], both[rows:].astype(bf16)
            for factor in factors:
                image = image - dot(factor, vectors)
            out[slab, :, cols] = image.astype(bf16)
            lifted[slab * rows : (slab + 1) * rows, cols] = image.astype(bf16)


def level_body(place, own, below, above, weights, out):
    reduce_rows(place, own, (below, above), (0, 1), weights, out)


def third_body(place, own, lifted, above, weights, out):
    count, rows, _ = own.shape
    below = [lifted[slab * rows : (slab + 1) * rows] for slab in range(count)]
    reduce_rows(place, own, (below, above), (0, 1), weights, out)


def product(place, rows, weights, whole, targets):
    for part, cols in enumerate(both_parts(place, weights.shape[-1])):
        for slab in range(whole.shape[0]):
            result = dot(rows[slab], weights[part, slab]).astype(bf16)
            targets[part][slab] = result
            whole[slab, :, cols] = result


def last_body(place, own, other, weights, whole, keep, send, rows):
    reduce_rows(place, own, (other,), (0,), weights, rows)
    product(place, rows, weights.at[1], whole, (keep, send))


def final_body(place, own, final, packed, whole, keep, send, weights, sem):
    count = own.shape[0]
    sources = (final.at[pl.ds(place[0] * count, count)], packed.at[packed.shape[0] - 1])
    run([
        pltpu.make_async_copy(source, weights.at[part], sem.at[part])
        for part, source in enumerate(sources)
    ])
    product(place, own, weights, whole, (keep, send))


def level_flops(operand, products):
    return 2 * products * operand.size * operand.shape[-1]


def add_pairs(place, table, targets, inside, window, blocks, others, summed):
    half = blocks.shape[-1]
    reach = table.shape[1] // 2
    first = place[0] * 2
    mine, theirs = columns(place[0], half), columns(1 - place[0], half)
    for target in targets:

        @pl.loop(0, reach)
        def _(entry):
            source = target + table[first + target, entry]

            @pl.when(inside(source))
            def _():
                block = table[first + target, reach + entry]
                vectors = window(source)
                summed[target, :, mine] += dot(vectors, blocks[block])
                summed[target, :, theirs] += dot(vectors, others[block])


def own_pairs_body(place, table, levels, index, extended, image, correction, blocks, others, summed, out, shift):
    own, rows, _ = image.shape
    below = extended.shape[0] // 3
    first = place[0] * own
    shift[...] = jnp.full(shift.shape, levels[index[0]], f32)
    summed[...] = jnp.zeros(summed.shape, f32)
    add_pairs(
        place, table, range(below + own),
        lambda source: jnp.logical_and(source >= below, source < below + own),
        lambda source: correction[source - below], blocks, others, summed,
    )
    overlap = jnp.zeros((2 * rows, rows), f32)
    mixed = jnp.zeros((rows, rows), f32)
    for slab in range(own):
        vectors, fixed = extended[first + below + slab], correction[slab]
        overlap = overlap + dot_t(jnp.concatenate([vectors, fixed], 0), fixed)
        mixed = mixed + dot_t(fixed, image[slab])
    out[0 : 2 * rows, 0:rows] = jnp.zeros((2 * rows, rows), f32)
    out[0 : 2 * rows, rows : 2 * rows] = overlap
    out[2 * rows :, 0:rows] = mixed[: rows // 2]
    out[2 * rows :, rows : 2 * rows] = mixed[rows // 2 :]


def cross_pairs_body(
    place, table, extended, correction, near, far, blocks, others, begun, part, keep, send, window, summed, out
):
    own, rows, _ = correction.shape
    below = window.shape[0]
    first = place[0] * own
    window[0:own] = far[...]
    window[own : 2 * own] = near[...]
    summed[below : below + own] = begun[below : below + own]
    add_pairs(
        place, table, range(below, below + own),
        lambda source: jnp.logical_and(source >= 0, source < below),
        lambda source: window[source], blocks, others, summed,
    )
    pencil = jnp.zeros((2 * rows, rows), f32)
    for slab in range(below + own):
        fixed = window[slab] if slab < below else correction[slab - below]
        terms = begun[slab] if slab < below else summed[slab]
        basis = jnp.concatenate([extended[first + slab], fixed], 0)
        pencil = pencil + dot_t(basis, terms.astype(bf16))
    out[...] = part[...]
    out[0 : 2 * rows, 0:rows] = pencil
    keep[...] = out[row_half(place[0], keep)]
    send[...] = out[row_half(1 - place[0], keep)]


def row_half(index, part):
    return pl.ds(pl.multiple_of(index * part.shape[0], 8), part.shape[0])


def assemble_body(scale, place, shift, moments, keep, received, first, second, gram, pencil, result, whole):
    rows = moments.shape[0]
    own = keep.shape[0]
    result[pl.ds(place[0] * own, own)] = keep[...]
    result[pl.ds((1 - place[0]) * own, own)] = received[...]
    whole[row_half(place[0], first)] = first[...] * scale
    whole[row_half(1 - place[0], first)] = second[...] * scale
    top, bottom = whole[0 : 2 * rows], whole[2 * rows :]
    overlap = top[:, rows:]
    mixed = jnp.concatenate([bottom[:, :rows], bottom[:, rows:]], 0)
    left = jnp.concatenate([moments[:, rows:], overlap[:rows].T], 0)
    product = jnp.concatenate([left, overlap], 1)
    gram[...] = product
    projected = jnp.concatenate([jnp.concatenate([moments[:, :rows], mixed], 0), top[:, :rows]], 1)
    pencil[...] = projected - shift[0:1] * product


def swapped(operand):
    return lax.ppermute(operand, "vec", SWAP)


def along(operand, axis, distance):
    count = lax.axis_size("slab") * (2 if axis == CHAIN else 1)
    route = [(i, i + distance) for i in range(count) if 0 <= i + distance < count]
    return lax.ppermute(operand, axis, route)


def pair_routes(distance):
    chain = 2 * lax.axis_size("slab")
    routes = []
    for bit in range(2):
        ups = [(i, i + distance) for i in range(chain - distance) if i // distance % 2 == bit]
        routes.append(ups + [(j, i) for i, j in ups])
    return [route for route in routes if route]


def summed_up(parts):
    while len(parts) > 1:
        parts = [a + b for a, b in zip(parts[::2], parts[1::2])]
    return parts[0]


def slab_total(part):
    slabs = lax.axis_size("slab")
    reach = 1
    while reach < slabs:
        radix = min(4, slabs // reach)
        routes = [[(i, i ^ (offset * reach)) for i in range(slabs)] for offset in range(1, radix)]
        part = summed_up([part] + [lax.ppermute(part, "slab", route) for route in routes])
        reach *= radix
    return part


def on_device(
    vectors,
    blocks,
    slab_blocks,
    far_source,
    far_block,
    level_lower,
    level_upper,
    level_final,
    shift_levels,
    shift_index,
):
    slab_count, rows, half = vectors.shape
    own_count = slab_count // 2
    slabs = lax.axis_size("slab")
    chain = 2 * slabs
    width = blocks.shape[1]
    rows_total = slab_count * slabs * width
    levels = [l for l in range(level_lower.shape[0]) if 2**l < slab_count * slabs]
    slab, core = lax.axis_index("slab"), lax.axis_index("vec")
    link = 2 * slab + core
    steps = [max(2**l // own_count, 1) for l in levels]
    place = jnp.stack([core] + [link // step % 2 for step in steps]).astype(jnp.int32)

    below, above = along(vectors, "slab", 1), along(vectors, "slab", -1)
    slab_ids = slab * slab_count + jnp.arange(slab_count, dtype=jnp.int32)[:, None]
    near = jnp.broadcast_to(jnp.arange(-1, 2, dtype=jnp.int32), (slab_count, 3))
    table = jnp.concatenate([near, far_source - slab_ids, slab_blocks, far_block], 1)
    note = jnp.pad(table.astype(bf16), ((0, 16 - slab_count), (0, width - table.shape[1])))
    held_blocks = load_whole(place, place, blocks)
    theirs = pack(levels[:3], place, held_blocks, level_lower, level_upper)
    extended = lax.all_gather(jnp.concatenate([below, vectors, above], 0), "vec", axis=2, tiled=True)
    theirs, extended = lax.optimization_barrier((theirs, extended))
    keep, send, moments = image_halves(place, table, extended, vectors, in_vmem(held_blocks))
    received, moments = swapped(send), moments + swapped(moments)
    image = jnp.where(core == 0, jnp.concatenate([keep, received], 2), jnp.concatenate([received, keep], 2))
    image, moments, theirs = lax.optimization_barrier((image, moments, theirs))
    packed = swapped(theirs)

    inner_route, outer_route = pair_routes(1)
    outer = lax.ppermute(lax.dynamic_slice_in_dim(image, (own_count - 1) * core, 1), CHAIN, outer_route)
    inner = swapped(lax.dynamic_slice_in_dim(image, (own_count - 1) * (1 - core), 1))
    flips = [[(i, i ^ 2**bit) for i in range(slabs)] for bit in range((slabs - 1).bit_length())]
    received = lax.ppermute(moments, "slab", flips[0])
    body = functools.partial(load_body, 0, 0)
    matrices = in_vmem(load(body, place, image, level_lower, level_upper, packed))
    vectors_1 = kernel_call(
        first_vectors_body,
        struct(image.shape),
        [SMEM] + [VMEM] * 2,
        flops=level_flops(image, 2),
    )(place, extended, matrices)
    both = kernel_call(
        first_body,
        struct((own_count, 2 * rows, width)),
        [SMEM] + [VMEM] * 5,
        flops=level_flops(image, 2),
    )(place, image, inner, outer, vectors_1, matrices)
    both, received = lax.optimization_barrier((both, received))
    outer, inner = lax.ppermute(both, CHAIN, outer_route), swapped(both)
    for flip in flips[1:]:
        moments = moments + received
        received = lax.ppermute(moments, "slab", flip)
    moments = (moments + received) / rows_total
    body = functools.partial(load_body, 1, 0)
    matrices = in_vmem(load(body, place, both, level_lower, level_upper, packed))
    theirs = pack(levels[3:], place, matrices, level_lower, level_upper, level_final)
    theirs, inner, outer, moments = lax.optimization_barrier((theirs, inner, outer, moments))
    following = swapped(theirs)
    residual, lifted = kernel_call(
        second_body,
        (struct(image.shape), struct((own_count * rows + 16, width))),
        [SMEM] + [VMEM] * 6,
        flops=level_flops(both, 2),
    )(place, both, inner, outer, matrices, moments, note)

    part = struct((own_count, rows, half))
    ends = (struct(residual.shape), part, part)
    one_partner = chain == 2 * steps[-1]
    for level, step in zip(levels[2:], steps[2:]):
        last = level == levels[-1]
        if last:
            held_blocks = load_whole(place, residual, blocks)
        if last and one_partner:
            body = functools.partial(load_last_body, level, 3)
            matrices = load(body, place, residual, level_lower, level_upper, packed, level_final)
            (route,) = pair_routes(step)
            other = lax.ppermute(residual, CHAIN, route)
            other, held_blocks = lax.optimization_barrier((other, held_blocks))
            correction, keep, send = kernel_call(
                last_body,
                ends,
                [SMEM] + [VMEM] * 3,
                [pltpu.VMEM(residual.shape, bf16)],
                flops=level_flops(residual, 2),
            )(place, residual, other, in_vmem(matrices))
            break
        body = functools.partial(load_body, level, 0 if level == 2 else 3)
        matrices = load(body, place, residual, level_lower, level_upper, packed)
        below, above = along(residual if level > 2 else lifted, CHAIN, step), along(residual, CHAIN, -step)
        if level == 2:
            count = own_count * rows
            lower_table = below[count : count + slab_count, : table.shape[1]].astype(jnp.int32)
            packed, below, above = lax.optimization_barrier((following, below, above))
        if level == 3:
            late_blocks, below, above, matrices = lax.optimization_barrier((blocks, below, above, matrices))
            others = swapped(late_blocks)
        residual = kernel_call(
            level_body if level > 2 else third_body,
            struct(residual.shape),
            [SMEM] + [VMEM] * 4,
            flops=level_flops(residual, 2),
        )(place, residual, below, above, in_vmem(matrices))
    if not one_partner:
        correction, keep, send = kernel_call(
            final_body,
            ends,
            [SMEM, VMEM, ANY, ANY],
            [pltpu.VMEM((2, own_count, width, half), bf16), pltpu.SemaphoreType.DMA((2,))],
            flops=level_flops(residual, 1),
        )(place, residual, in_hbm(level_final), packed)
    held_blocks, others = in_vmem(held_blocks), in_vmem(others)

    far, near = along(correction, CHAIN, 2), along(correction, CHAIN, 1)
    received = swapped(send)
    result_parts = (keep, received)
    tables = jnp.concatenate([lower_table, table], 0)
    flops = level_flops(image, 7)
    sums = (5 * rows // 2, 2 * rows)
    begun, part, shift = kernel_call(
        own_pairs_body,
        (struct((3 * own_count, rows, width), f32), struct(sums, f32), struct((8, 2 * rows), f32)),
        [SMEM] * 4 + [VMEM] * 5,
        flops=flops,
    )(place, tables, shift_levels, shift_index, extended, image, correction, held_blocks, others)
    share = struct((sums[0] // 2, sums[1]), f32)
    keep, send = kernel_call(
        cross_pairs_body,
        (share, share),
        [SMEM] * 2 + [VMEM] * 8,
        [
            pltpu.VMEM((2 * own_count, rows, width), bf16),
            pltpu.VMEM((3 * own_count, rows, width), f32),
            pltpu.VMEM(sums, f32),
        ],
        flops=flops,
    )(place, tables, extended, correction, near, far, held_blocks, others, begun, part)
    share = slab_total(keep + swapped(send))
    square = struct((2 * rows, 2 * rows), f32)
    gram, pencil, result = kernel_call(
        functools.partial(assemble_body, 1.0 / rows_total),
        (square, square, struct(vectors.shape)),
        [SMEM] + [VMEM] * 6,
        [pltpu.VMEM(sums, f32)],
    )(place, shift, moments, *result_parts, share, swapped(share))
    return (result, gram, pencil)


def solution(mesh):
    in_specs = (
        P(("groups", "slab"), None, "vec"),
        P("groups", None, "vec"),
        P(("groups", "slab"), None),
        P(("groups", "slab"), None),
        P(("groups", "slab"), None),
        P(None, ("groups", "slab"), None, "vec"),
        P(None, ("groups", "slab"), None, "vec"),
        P(("groups", "slab"), None, "vec"),
        P("groups"),
        P("groups"),
    )
    out_specs = (P(("groups", "slab"), None, "vec"), P("groups", None), P("groups", None))
    return jax.shard_map(
        on_device, mesh=mesh, in_specs=in_specs, out_specs=out_specs, check_vma=False
    )
```

```python
import functools

import jax
import jax.numpy as jnp
from jax import lax
from jax.experimental import pallas as pl
from jax.experimental.pallas import tpu as pltpu
from jax.sharding import PartitionSpec as P

f32, bf16 = jnp.float32, jnp.bfloat16
CHAIN = ("slab", "vec")
ANY = pl.BlockSpec(memory_space=pl.ANY)
VMEM = pl.BlockSpec(memory_space=pltpu.VMEM)
SMEM = pl.BlockSpec(memory_space=pltpu.SMEM)
SWAP = [(0, 1), (1, 0)]
MIB = 1024 * 1024


def kernel_call(body, out_shape, in_specs, scratch=(), vmem=16 * MIB, flops=0, size=0):
    return pl.pallas_call(
        body,
        out_shape=out_shape,
        in_specs=in_specs,
        out_specs=jax.tree.map(lambda _: VMEM, out_shape),
        scratch_shapes=list(scratch),
        compiler_params=pltpu.CompilerParams(vmem_limit_bytes=vmem),
        cost_estimate=pl.CostEstimate(flops=flops, bytes_accessed=size, transcendentals=0),
    )


def struct(shape, dtype=bf16):
    return jax.ShapeDtypeStruct(shape, dtype)


def dot(rows, matrix):
    return jnp.dot(rows, matrix, preferred_element_type=f32)


def dot_t(left, right):
    return lax.dot_general(left, right, (((1,), (1,)), ((), ())), preferred_element_type=f32)


def columns(index, width):
    return pl.ds(pl.multiple_of(index * width, width), width)


def in_vmem(operand):
    return pltpu.with_memory_space_constraint(operand, pltpu.VMEM)


def in_hbm(operand):
    return pltpu.with_memory_space_constraint(operand, pltpu.HBM)


def run(copies):
    for copy in copies:
        copy.start()
    for copy in copies:
        copy.wait()


def through(parts, held, outs, sem):
    ins = [pltpu.make_async_copy(part, held.at[k], sem.at[0, k]) for k, part in enumerate(parts)]
    outs = [pltpu.make_async_copy(held.at[k], out, sem.at[1, k]) for k, out in enumerate(outs)]
    return ins, outs


def finish(ins, outs, others):
    for copy, following in zip(ins, outs):
        copy.wait()
        following.start()
    for copy in others + outs:
        copy.wait()


def prepare_body(place, lower, upper, blocks, held_blocks, first, second, held, sem, block_sem):
    count = held.shape[1]
    slabs = pl.ds((1 - place[0]) * count, count)
    parts = [ref.at[level, slabs] for level in range(3) for ref in (lower, upper)]
    outs = [first.at[k] for k in range(2)] + [second.at[k] for k in range(4)]
    ins, outs = through(parts, held, outs, sem)
    whole = pltpu.make_async_copy(blocks, held_blocks, block_sem.at[0])
    for copy in ins + [whole]:
        copy.start()
    finish(ins, outs, [whole])


def prepare(place, lower, upper, blocks):
    _, slabs, rows, half = lower.shape
    shape = (slabs // 2, rows, half)
    size = 2 * slabs * rows * half
    return pl.pallas_call(
        prepare_body,
        out_shape=[
            pltpu.VMEM(blocks.shape, bf16),
            pltpu.HBM((2,) + shape, bf16),
            pltpu.HBM((4,) + shape, bf16),
        ],
        in_specs=[SMEM] + [ANY] * 3,
        out_specs=[VMEM, ANY, ANY],
        scratch_shapes=[
            pltpu.VMEM((6,) + shape, bf16),
            pltpu.SemaphoreType.DMA((2, 6)),
            pltpu.SemaphoreType.DMA((1,)),
        ],
        compiler_params=pltpu.CompilerParams(vmem_limit_bytes=10 * MIB),
        cost_estimate=pl.CostEstimate(
            flops=0, bytes_accessed=2 * blocks.size + 6 * size, transcendentals=0
        ),
    )(place, *[in_hbm(x) for x in (lower, upper, blocks)])


def load_and_pack_body(level, first, later, place, token, lower, upper, final, packed, weights, out, held, sem, pack_sem):
    count = weights.shape[2]
    slabs = pl.ds((1 - place[0]) * count, count)
    parts = [ref.at[each, slabs] for each in later for ref in (lower, upper)] + [final.at[slabs]]
    ins, outs = through(parts, held, [out.at[k] for k in range(len(parts))], pack_sem)
    loads = level_copies(level, first, place, lower, upper, packed, weights, sem)
    for copy in ins + loads:
        copy.start()
    finish(ins, outs, loads)


def load_and_pack(level, first, later, place, token, lower, upper, final, packed):
    _, slabs, rows, half = lower.shape
    shape = (2, 2, slabs // 2, rows, half)
    count = 2 * len(later) + 1
    later_shape = (count,) + shape[2:]
    return pl.pallas_call(
        functools.partial(load_and_pack_body, level, first, later),
        out_shape=[pltpu.VMEM(shape, bf16), pltpu.HBM(later_shape, bf16)],
        in_specs=[SMEM] + [ANY] * 5,
        out_specs=[VMEM, ANY],
        scratch_shapes=[
            pltpu.VMEM(later_shape, bf16),
            pltpu.SemaphoreType.DMA((2, 2)),
            pltpu.SemaphoreType.DMA((2, count)),
        ],
        compiler_params=pltpu.CompilerParams(vmem_limit_bytes=8 * MIB),
        cost_estimate=pl.CostEstimate(
            flops=0, bytes_accessed=(8 + 4 * count) * slabs * rows * half // 2, transcendentals=0
        ),
    )(place, token, *[in_hbm(x) for x in (lower, upper, final)], packed)


def level_copies(level, first, place, lower, upper, packed, weights, sem):
    count = weights.shape[2]
    slabs = pl.ds(place[0] * count, count)
    copies = []
    for side, ref in enumerate((lower, upper)):
        sources = (ref.at[level, slabs], packed.at[2 * (level - first) + side])
        for part, source in enumerate(sources):
            copies.append(pltpu.make_async_copy(source, weights.at[side, part], sem.at[side, part]))
    return copies


def load_body(level, first, place, token, lower, upper, packed, weights, sem):
    run(level_copies(level, first, place, lower, upper, packed, weights, sem))


def load_last_body(level, first, place, token, lower, upper, packed, final, weights, sem):
    count = weights.shape[2]
    slabs = pl.ds(place[0] * count, count)
    above = 1 - place[1 + level]

    def copy(source, side, part):
        return pltpu.make_async_copy(source, weights.at[side, part], sem.at[side, part])

    pl.when(above == 1)(lambda: copy(upper.at[level, slabs], 0, 0).start())
    pl.when(above == 0)(lambda: copy(lower.at[level, slabs], 0, 0).start())
    others = [
        copy(packed.at[2 * (level - first) + above], 0, 1),
        copy(final.at[slabs], 1, 0),
        copy(packed.at[packed.shape[0] - 1], 1, 1),
    ]
    for each in others:
        each.start()
    copy(lower.at[level, slabs], 0, 0).wait()
    for each in others:
        each.wait()


def load(body, place, token, lower, upper, packed, *finals):
    _, slabs, rows, half = lower.shape
    shape = (2, 2, slabs // 2, rows, half)
    operands = [in_hbm(lower), in_hbm(upper), packed] + [in_hbm(x) for x in finals]
    return pl.pallas_call(
        body,
        out_shape=pltpu.VMEM(shape, bf16),
        in_specs=[SMEM] + [ANY] * (1 + len(operands)),
        out_specs=VMEM,
        scratch_shapes=[pltpu.SemaphoreType.DMA((2, 2))],
        compiler_params=pltpu.CompilerParams(vmem_limit_bytes=4 * MIB),
        cost_estimate=pl.CostEstimate(flops=0, bytes_accessed=8 * slabs * rows * half, transcendentals=0),
    )(place, token, *operands)


def load_whole_body(place, token, source, target, sem):
    run([pltpu.make_async_copy(source, target, sem.at[0])])


def load_whole(place, token, array):
    return pl.pallas_call(
        load_whole_body,
        out_shape=pltpu.VMEM(array.shape, array.dtype),
        in_specs=[SMEM, ANY, ANY],
        out_specs=VMEM,
        scratch_shapes=[pltpu.SemaphoreType.DMA((1,))],
        compiler_params=pltpu.CompilerParams(vmem_limit_bytes=6 * MIB),
        cost_estimate=pl.CostEstimate(flops=0, bytes_accessed=2 * array.size, transcendentals=0),
    )(place, token, in_hbm(array))


def image_body(place, table, extended, vectors, blocks, keep, send, moments, image):
    slabs, count, _ = vectors.shape
    reach = table.shape[1] // 2
    quotient, old = jnp.zeros((count, count), f32), jnp.zeros((count, count), f32)
    for slab in range(slabs):
        summed = None
        for entry in range(reach):
            rows = extended[table[slab, entry] + (slab + slabs)]
            term = dot(rows, blocks[table[slab, reach + entry]])
            summed = term if summed is None else summed + term
        rounded = summed.astype(bf16)
        image[slab] = rounded
        quotient = quotient + dot_t(vectors[slab], rounded)
        old = old + dot_t(vectors[slab], vectors[slab])
    moments[:, 0:count] = quotient
    moments[:, count : 2 * count] = old
    mine = slabs // 2
    keep[...] = image[pl.ds(place[0] * mine, mine)]
    send[...] = image[pl.ds((1 - place[0]) * mine, mine)]


def image_halves(place, table, extended, vectors, blocks):
    slabs, rows, half = vectors.shape
    part = struct((slabs // 2, rows, half))
    return kernel_call(
        image_body,
        (part, part, struct((rows, 2 * rows), f32)),
        [SMEM, SMEM, VMEM, VMEM, VMEM],
        [pltpu.VMEM((slabs, rows, half), bf16)],
        flops=14 * slabs * rows * 2 * half * half,
        size=2 * blocks.size,
    )(place, table, extended, vectors, blocks)


def both_parts(place, half):
    return columns(place[0], half), columns(1 - place[0], half)


def first_vectors_body(place, extended, weights, out):
    count, half = out.shape[0], weights.shape[-1]
    first = extended.shape[0] // 3 + count * place[0]
    for part, cols in enumerate(both_parts(place, half)):
        for slab in range(count):
            own = first + slab
            summed = dot(extended[own - 1], weights[0, part, slab])
            summed = summed + dot(extended[own + 1], weights[1, part, slab])
            out[slab, :, cols] = (extended[own, :, cols].astype(f32) - summed).astype(bf16)


def first_body(place, image, inner, outer, vectors, weights, out):
    count, rows, _ = image.shape
    half = weights.shape[-1]
    odd = place[0] == 1
    below = [jnp.where(odd, inner[0], outer[0])] + [image[slab] for slab in range(count - 1)]
    above = [image[slab] for slab in range(1, count)] + [jnp.where(odd, outer[0], inner[0])]
    for slab in range(count):
        out[slab, rows : 2 * rows] = vectors[slab]
    for part, cols in enumerate(both_parts(place, half)):
        for slab in range(count):
            summed = dot(below[slab], weights[0, part, slab]) + dot(above[slab], weights[1, part, slab])
            out[slab, 0:rows, cols] = (image[slab, :, cols].astype(f32) - summed).astype(bf16)


def reduce_rows(place, own, partners, sides, weights, out):
    for part, cols in enumerate(both_parts(place, weights.shape[-1])):
        for slab in range(own.shape[0]):
            summed = None
            for side, rows in zip(sides, partners):
                term = dot(rows[slab], weights[side, part, slab])
                summed = term if summed is None else summed + term
            out[slab, :, cols] = (own[slab, :, cols].astype(f32) - summed).astype(bf16)


def second_body(place, own, inner, outer, weights, moments, note, out, lifted):
    count, rows, _ = out.shape
    lifted[count * rows :] = note[...]
    high = moments[:, 0:rows].astype(bf16)
    low = (moments[:, 0:rows] - high.astype(f32)).astype(bf16)
    factors = (high.T, low.T)
    for part, cols in enumerate(both_parts(place, weights.shape[-1])):
        for slab in range(count):
            summed = dot(inner[slab], weights[1 - place[0], part, slab])
            summed = summed + dot(outer[slab], weights[place[0], part, slab])
            both = own[slab, :, cols].astype(f32) - summed
            image, vectors = both[:rows], both[rows:].astype(bf16)
            for factor in factors:
                image = image - dot(factor, vectors)
            out[slab, :, cols] = image.astype(bf16)
            lifted[slab * rows : (slab + 1) * rows, cols] = image.astype(bf16)


def level_body(place, own, below, above, weights, out):
    reduce_rows(place, own, (below, above), (0, 1), weights, out)


def third_body(place, own, lifted, above, weights, out):
    count, rows, _ = own.shape
    below = [lifted[slab * rows : (slab + 1) * rows] for slab in range(count)]
    reduce_rows(place, own, (below, above), (0, 1), weights, out)


def product(place, rows, weights, whole, targets):
    for part, cols in enumerate(both_parts(place, weights.shape[-1])):
        for slab in range(whole.shape[0]):
            result = dot(rows[slab], weights[part, slab]).astype(bf16)
            targets[part][slab] = result
            whole[slab, :, cols] = result


def last_body(place, own, other, weights, whole, keep, send, rows):
    reduce_rows(place, own, (other,), (0,), weights, rows)
    product(place, rows, weights.at[1], whole, (keep, send))


def final_body(place, own, final, packed, whole, keep, send, weights, sem):
    count = own.shape[0]
    sources = (final.at[pl.ds(place[0] * count, count)], packed.at[packed.shape[0] - 1])
    run([
        pltpu.make_async_copy(source, weights.at[part], sem.at[part])
        for part, source in enumerate(sources)
    ])
    product(place, own, weights, whole, (keep, send))


def level_flops(operand, products):
    return 2 * products * operand.size * operand.shape[-1]


def add_pairs(place, table, targets, inside, window, blocks, others, summed):
    half = blocks.shape[-1]
    reach = table.shape[1] // 2
    first = place[0] * 2
    mine, theirs = columns(place[0], half), columns(1 - place[0], half)
    for target in targets:

        @pl.loop(0, reach)
        def _(entry):
            source = target + table[first + target, entry]

            @pl.when(inside(source))
            def _():
                block = table[first + target, reach + entry]
                vectors = window(source)
                summed[target, :, mine] += dot(vectors, blocks[block])
                summed[target, :, theirs] += dot(vectors, others[block])


def own_pairs_body(place, table, levels, index, extended, image, correction, blocks, others, summed, out, shift):
    own, rows, _ = image.shape
    below = extended.shape[0] // 3
    first = place[0] * own
    shift[...] = jnp.full(shift.shape, levels[index[0]], f32)
    summed[...] = jnp.zeros(summed.shape, f32)
    add_pairs(
        place, table, range(below + own),
        lambda source: jnp.logical_and(source >= below, source < below + own),
        lambda source: correction[source - below], blocks, others, summed,
    )
    overlap = jnp.zeros((2 * rows, rows), f32)
    mixed = jnp.zeros((rows, rows), f32)
    for slab in range(own):
        vectors, fixed = extended[first + below + slab], correction[slab]
        overlap = overlap + dot_t(jnp.concatenate([vectors, fixed], 0), fixed)
        mixed = mixed + dot_t(fixed, image[slab])
    out[0 : 2 * rows, 0:rows] = jnp.zeros((2 * rows, rows), f32)
    out[0 : 2 * rows, rows : 2 * rows] = overlap
    out[2 * rows :, 0:rows] = mixed[: rows // 2]
    out[2 * rows :, rows : 2 * rows] = mixed[rows // 2 :]


def cross_pairs_body(
    place, table, extended, correction, near, far, blocks, others, begun, part, keep, send, window, summed, out
):
    own, rows, _ = correction.shape
    below = window.shape[0]
    first = place[0] * own
    window[0:own] = far[...]
    window[own : 2 * own] = near[...]
    summed[below : below + own] = begun[below : below + own]
    add_pairs(
        place, table, range(below, below + own),
        lambda source: jnp.logical_and(source >= 0, source < below),
        lambda source: window[source], blocks, others, summed,
    )
    pencil = jnp.zeros((2 * rows, rows), f32)
    for slab in range(below + own):
        fixed = window[slab] if slab < below else correction[slab - below]
        terms = begun[slab] if slab < below else summed[slab]
        basis = jnp.concatenate([extended[first + slab], fixed], 0)
        pencil = pencil + dot_t(basis, terms.astype(bf16))
    out[...] = part[...]
    out[0 : 2 * rows, 0:rows] = pencil
    keep[...] = out[row_half(place[0], keep)]
    send[...] = out[row_half(1 - place[0], keep)]


def row_half(index, part):
    return pl.ds(pl.multiple_of(index * part.shape[0], 8), part.shape[0])


def assemble_body(scale, place, shift, moments, keep, received, first, second, gram, pencil, result, whole):
    rows = moments.shape[0]
    own = keep.shape[0]
    result[pl.ds(place[0] * own, own)] = keep[...]
    result[pl.ds((1 - place[0]) * own, own)] = received[...]
    whole[row_half(place[0], first)] = first[...] * scale
    whole[row_half(1 - place[0], first)] = second[...] * scale
    top, bottom = whole[0 : 2 * rows], whole[2 * rows :]
    overlap = top[:, rows:]
    mixed = jnp.concatenate([bottom[:, :rows], bottom[:, rows:]], 0)
    left = jnp.concatenate([moments[:, rows:], overlap[:rows].T], 0)
    product = jnp.concatenate([left, overlap], 1)
    gram[...] = product
    projected = jnp.concatenate([jnp.concatenate([moments[:, :rows], mixed], 0), top[:, :rows]], 1)
    pencil[...] = projected - shift[0:1] * product


def swapped(operand):
    return lax.ppermute(operand, "vec", SWAP)


def along(operand, axis, distance):
    count = lax.axis_size("slab") * (2 if axis == CHAIN else 1)
    route = [(i, i + distance) for i in range(count) if 0 <= i + distance < count]
    return lax.ppermute(operand, axis, route)


def pair_routes(distance):
    chain = 2 * lax.axis_size("slab")
    routes = []
    for bit in range(2):
        ups = [(i, i + distance) for i in range(chain - distance) if i // distance % 2 == bit]
        routes.append(ups + [(j, i) for i, j in ups])
    return [route for route in routes if route]


def summed_up(parts):
    while len(parts) > 1:
        parts = [a + b for a, b in zip(parts[::2], parts[1::2])]
    return parts[0]


def slab_total(part):
    slabs = lax.axis_size("slab")
    reach = 1
    while reach < slabs:
        radix = min(4, slabs // reach)
        routes = [[(i, i ^ (offset * reach)) for i in range(slabs)] for offset in range(1, radix)]
        part = summed_up([part] + [lax.ppermute(part, "slab", route) for route in routes])
        reach *= radix
    return part


def on_device(
    vectors,
    blocks,
    slab_blocks,
    far_source,
    far_block,
    level_lower,
    level_upper,
    level_final,
    shift_levels,
    shift_index,
):
    slab_count, rows, half = vectors.shape
    own_count = slab_count // 2
    slabs = lax.axis_size("slab")
    chain = 2 * slabs
    width = blocks.shape[1]
    rows_total = slab_count * slabs * width
    levels = [l for l in range(level_lower.shape[0]) if 2**l < slab_count * slabs]
    slab, core = lax.axis_index("slab"), lax.axis_index("vec")
    link = 2 * slab + core
    steps = [max(2**l // own_count, 1) for l in levels]
    place = jnp.stack([core] + [link // step % 2 for step in steps]).astype(jnp.int32)

    below, above = along(vectors, "slab", 1), along(vectors, "slab", -1)
    slab_ids = slab * slab_count + jnp.arange(slab_count, dtype=jnp.int32)[:, None]
    near = jnp.broadcast_to(jnp.arange(-1, 2, dtype=jnp.int32), (slab_count, 3))
    table = jnp.concatenate([near, far_source - slab_ids, slab_blocks, far_block], 1)
    note = jnp.pad(table.astype(bf16), ((0, 16 - slab_count), (0, width - table.shape[1])))
    held_blocks, theirs_0, theirs = prepare(place, level_lower, level_upper, blocks)
    extended = lax.all_gather(jnp.concatenate([below, vectors, above], 0), "vec", axis=2, tiled=True)
    theirs_0, extended = lax.optimization_barrier((theirs_0, extended))
    packed_0 = swapped(theirs_0)
    keep, send, moments = image_halves(place, table, extended, vectors, in_vmem(held_blocks))
    received, moments = swapped(send), moments + swapped(moments)
    image = jnp.where(core == 0, jnp.concatenate([keep, received], 2), jnp.concatenate([received, keep], 2))
    image, moments, theirs = lax.optimization_barrier((image, moments, theirs))
    packed = swapped(theirs)

    inner_route, outer_route = pair_routes(1)
    outer = lax.ppermute(lax.dynamic_slice_in_dim(image, (own_count - 1) * core, 1), CHAIN, outer_route)
    inner = swapped(lax.dynamic_slice_in_dim(image, (own_count - 1) * (1 - core), 1))
    flips = [[(i, i ^ 2**bit) for i in range(slabs)] for bit in range((slabs - 1).bit_length())]
    received = lax.ppermute(moments, "slab", flips[0])
    body = functools.partial(load_body, 0, 0)
    matrices = in_vmem(load(body, place, keep, level_lower, level_upper, packed_0))
    vectors_1 = kernel_call(
        first_vectors_body,
        struct(image.shape),
        [SMEM] + [VMEM] * 2,
        flops=level_flops(image, 2),
    )(place, extended, matrices)
    both = kernel_call(
        first_body,
        struct((own_count, 2 * rows, width)),
        [SMEM] + [VMEM] * 5,
        flops=level_flops(image, 2),
    )(place, image, inner, outer, vectors_1, matrices)
    both, received, late_blocks, packed = lax.optimization_barrier((both, received, blocks, packed))
    others = swapped(late_blocks)
    outer, inner = lax.ppermute(both, CHAIN, outer_route), swapped(both)
    for flip in flips[1:]:
        moments = moments + received
        received = lax.ppermute(moments, "slab", flip)
    moments = (moments + received) / rows_total
    matrices, theirs = load_and_pack(
        1, 1, levels[3:], place, both, level_lower, level_upper, level_final, packed
    )
    matrices = in_vmem(matrices)
    theirs, inner, outer, moments = lax.optimization_barrier((theirs, inner, outer, moments))
    following = swapped(theirs)
    residual, lifted = kernel_call(
        second_body,
        (struct(image.shape), struct((own_count * rows + 16, width))),
        [SMEM] + [VMEM] * 6,
        flops=level_flops(both, 2),
    )(place, both, inner, outer, matrices, moments, note)

    part = struct((own_count, rows, half))
    ends = (struct(residual.shape), part, part)
    one_partner = chain == 2 * steps[-1]
    for level, step in zip(levels[2:], steps[2:]):
        last = level == levels[-1]
        if last:
            held_blocks = load_whole(place, residual, blocks)
        if last and one_partner:
            body = functools.partial(load_last_body, level, 3)
            matrices = load(body, place, residual, level_lower, level_upper, packed, level_final)
            (route,) = pair_routes(step)
            other = lax.ppermute(residual, CHAIN, route)
            other, held_blocks = lax.optimization_barrier((other, held_blocks))
            correction, keep, send = kernel_call(
                last_body,
                ends,
                [SMEM] + [VMEM] * 3,
                [pltpu.VMEM(residual.shape, bf16)],
                flops=level_flops(residual, 2),
            )(place, residual, other, in_vmem(matrices))
            break
        body = functools.partial(load_body, level, 1 if level == 2 else 3)
        matrices = load(body, place, residual, level_lower, level_upper, packed)
        below, above = along(residual if level > 2 else lifted, CHAIN, step), along(residual, CHAIN, -step)
        if level == 2:
            count = own_count * rows
            lower_table = below[count : count + slab_count, : table.shape[1]].astype(jnp.int32)
            packed, below, above = lax.optimization_barrier((following, below, above))
        if level == 3:
            below, above, matrices = lax.optimization_barrier((below, above, matrices))
        residual = kernel_call(
            level_body if level > 2 else third_body,
            struct(residual.shape),
            [SMEM] + [VMEM] * 4,
            flops=level_flops(residual, 2),
        )(place, residual, below, above, in_vmem(matrices))
    if not one_partner:
        correction, keep, send = kernel_call(
            final_body,
            ends,
            [SMEM, VMEM, ANY, ANY],
            [pltpu.VMEM((2, own_count, width, half), bf16), pltpu.SemaphoreType.DMA((2,))],
            flops=level_flops(residual, 1),
        )(place, residual, in_hbm(level_final), packed)
    held_blocks, others = in_vmem(held_blocks), in_vmem(others)

    far, near = along(correction, CHAIN, 2), along(correction, CHAIN, 1)
    received = swapped(send)
    result_parts = (keep, received)
    tables = jnp.concatenate([lower_table, table], 0)
    flops = level_flops(image, 7)
    sums = (5 * rows // 2, 2 * rows)
    begun, part, shift = kernel_call(
        own_pairs_body,
        (struct((3 * own_count, rows, width), f32), struct(sums, f32), struct((8, 2 * rows), f32)),
        [SMEM] * 4 + [VMEM] * 5,
        flops=flops,
    )(place, tables, shift_levels, shift_index, extended, image, correction, held_blocks, others)
    share = struct((sums[0] // 2, sums[1]), f32)
    keep, send = kernel_call(
        cross_pairs_body,
        (share, share),
        [SMEM] * 2 + [VMEM] * 8,
        [
            pltpu.VMEM((2 * own_count, rows, width), bf16),
            pltpu.VMEM((3 * own_count, rows, width), f32),
            pltpu.VMEM(sums, f32),
        ],
        flops=flops,
    )(place, tables, extended, correction, near, far, held_blocks, others, begun, part)
    share = slab_total(keep + swapped(send))
    square = struct((2 * rows, 2 * rows), f32)
    gram, pencil, result = kernel_call(
        functools.partial(assemble_body, 1.0 / rows_total),
        (square, square, struct(vectors.shape)),
        [SMEM] + [VMEM] * 6,
        [pltpu.VMEM(sums, f32)],
    )(place, shift, moments, *result_parts, share, swapped(share))
    return (result, gram, pencil)


def solution(mesh):
    in_specs = (
        P(("groups", "slab"), None, "vec"),
        P("groups", None, "vec"),
        P(("groups", "slab"), None),
        P(("groups", "slab"), None),
        P(("groups", "slab"), None),
        P(None, ("groups", "slab"), None, "vec"),
        P(None, ("groups", "slab"), None, "vec"),
        P(("groups", "slab"), None, "vec"),
        P("groups"),
        P("groups"),
    )
    out_specs = (P(("groups", "slab"), None, "vec"), P("groups", None), P("groups", None))
    return jax.shard_map(
        on_device, mesh=mesh, in_specs=in_specs, out_specs=out_specs, check_vma=False
    )
```

```python
import functools

import jax
import jax.numpy as jnp
from jax import lax
from jax.experimental import pallas as pl
from jax.experimental.pallas import tpu as pltpu
from jax.sharding import PartitionSpec as P

f32, bf16 = jnp.float32, jnp.bfloat16
CHAIN = ("slab", "vec")
ANY = pl.BlockSpec(memory_space=pl.ANY)
VMEM = pl.BlockSpec(memory_space=pltpu.VMEM)
SMEM = pl.BlockSpec(memory_space=pltpu.SMEM)
SWAP = [(0, 1), (1, 0)]
MIB = 1024 * 1024


def kernel_call(body, out_shape, in_specs, scratch=(), vmem=16 * MIB, flops=0, size=0):
    return pl.pallas_call(
        body,
        out_shape=out_shape,
        in_specs=in_specs,
        out_specs=jax.tree.map(lambda _: VMEM, out_shape),
        scratch_shapes=list(scratch),
        compiler_params=pltpu.CompilerParams(vmem_limit_bytes=vmem),
        cost_estimate=pl.CostEstimate(flops=flops, bytes_accessed=size, transcendentals=0),
    )


def struct(shape, dtype=bf16):
    return jax.ShapeDtypeStruct(shape, dtype)


def dot(rows, matrix):
    return jnp.dot(rows, matrix, preferred_element_type=f32)


def dot_t(left, right):
    return lax.dot_general(left, right, (((1,), (1,)), ((), ())), preferred_element_type=f32)


def columns(index, width):
    return pl.ds(pl.multiple_of(index * width, width), width)


def in_vmem(operand):
    return pltpu.with_memory_space_constraint(operand, pltpu.VMEM)


def in_hbm(operand):
    return pltpu.with_memory_space_constraint(operand, pltpu.HBM)


def run(copies):
    for copy in copies:
        copy.start()
    for copy in copies:
        copy.wait()


def through(parts, held, outs, sem):
    ins = [pltpu.make_async_copy(part, held.at[k], sem.at[0, k]) for k, part in enumerate(parts)]
    outs = [pltpu.make_async_copy(held.at[k], out, sem.at[1, k]) for k, out in enumerate(outs)]
    return ins, outs


def finish(ins, outs, others):
    for copy, following in zip(ins, outs):
        copy.wait()
        following.start()
    for copy in others + outs:
        copy.wait()


def prepare_body(place, lower, upper, blocks, held_blocks, first, second, held, sem, block_sem):
    count = held.shape[1]
    slabs = pl.ds((1 - place[0]) * count, count)
    parts = [ref.at[level, slabs] for level in range(3) for ref in (lower, upper)]
    outs = [first.at[k] for k in range(2)] + [second.at[k] for k in range(4)]
    ins, outs = through(parts, held, outs, sem)
    whole = pltpu.make_async_copy(blocks, held_blocks, block_sem.at[0])
    for copy in ins + [whole]:
        copy.start()
    finish(ins, outs, [whole])


def prepare(place, lower, upper, blocks):
    _, slabs, rows, half = lower.shape
    shape = (slabs // 2, rows, half)
    size = 2 * slabs * rows * half
    return pl.pallas_call(
        prepare_body,
        out_shape=[
            pltpu.VMEM(blocks.shape, bf16),
            pltpu.HBM((2,) + shape, bf16),
            pltpu.HBM((4,) + shape, bf16),
        ],
        in_specs=[SMEM] + [ANY] * 3,
        out_specs=[VMEM, ANY, ANY],
        scratch_shapes=[
            pltpu.VMEM((6,) + shape, bf16),
            pltpu.SemaphoreType.DMA((2, 6)),
            pltpu.SemaphoreType.DMA((1,)),
        ],
        compiler_params=pltpu.CompilerParams(vmem_limit_bytes=10 * MIB),
        cost_estimate=pl.CostEstimate(
            flops=0, bytes_accessed=2 * blocks.size + 6 * size, transcendentals=0
        ),
    )(place, *[in_hbm(x) for x in (lower, upper, blocks)])


def load_and_pack_body(level, first, later, place, token, lower, upper, final, packed, weights, out, held, sem, pack_sem):
    count = weights.shape[2]
    slabs = pl.ds((1 - place[0]) * count, count)
    parts = [ref.at[each, slabs] for each in later for ref in (lower, upper)] + [final.at[slabs]]
    ins, outs = through(parts, held, [out.at[k] for k in range(len(parts))], pack_sem)
    loads = level_copies(level, first, place, lower, upper, packed, weights, sem)
    for copy in ins + loads:
        copy.start()
    finish(ins, outs, loads)


def load_and_pack(level, first, later, place, token, lower, upper, final, packed):
    _, slabs, rows, half = lower.shape
    shape = (2, 2, slabs // 2, rows, half)
    count = 2 * len(later) + 1
    later_shape = (count,) + shape[2:]
    return pl.pallas_call(
        functools.partial(load_and_pack_body, level, first, later),
        out_shape=[pltpu.VMEM(shape, bf16), pltpu.HBM(later_shape, bf16)],
        in_specs=[SMEM] + [ANY] * 5,
        out_specs=[VMEM, ANY],
        scratch_shapes=[
            pltpu.VMEM(later_shape, bf16),
            pltpu.SemaphoreType.DMA((2, 2)),
            pltpu.SemaphoreType.DMA((2, count)),
        ],
        compiler_params=pltpu.CompilerParams(vmem_limit_bytes=8 * MIB),
        cost_estimate=pl.CostEstimate(
            flops=0, bytes_accessed=(8 + 4 * count) * slabs * rows * half // 2, transcendentals=0
        ),
    )(place, token, *[in_hbm(x) for x in (lower, upper, final)], packed)


def level_copies(level, first, place, lower, upper, packed, weights, sem):
    count = weights.shape[2]
    slabs = pl.ds(place[0] * count, count)
    copies = []
    for side, ref in enumerate((lower, upper)):
        sources = (ref.at[level, slabs], packed.at[2 * (level - first) + side])
        for part, source in enumerate(sources):
            copies.append(pltpu.make_async_copy(source, weights.at[side, part], sem.at[side, part]))
    return copies


def load_body(level, first, place, token, lower, upper, packed, weights, sem):
    run(level_copies(level, first, place, lower, upper, packed, weights, sem))


def load_last_body(level, first, place, token, lower, upper, packed, final, weights, sem):
    count = weights.shape[2]
    slabs = pl.ds(place[0] * count, count)
    above = 1 - place[1 + level]

    def copy(source, side, part):
        return pltpu.make_async_copy(source, weights.at[side, part], sem.at[side, part])

    pl.when(above == 1)(lambda: copy(upper.at[level, slabs], 0, 0).start())
    pl.when(above == 0)(lambda: copy(lower.at[level, slabs], 0, 0).start())
    others = [
        copy(packed.at[2 * (level - first) + above], 0, 1),
        copy(final.at[slabs], 1, 0),
        copy(packed.at[packed.shape[0] - 1], 1, 1),
    ]
    for each in others:
        each.start()
    copy(lower.at[level, slabs], 0, 0).wait()
    for each in others:
        each.wait()


def load(body, place, token, lower, upper, packed, *finals):
    _, slabs, rows, half = lower.shape
    shape = (2, 2, slabs // 2, rows, half)
    operands = [in_hbm(lower), in_hbm(upper), packed] + [in_hbm(x) for x in finals]
    return pl.pallas_call(
        body,
        out_shape=pltpu.VMEM(shape, bf16),
        in_specs=[SMEM] + [ANY] * (1 + len(operands)),
        out_specs=VMEM,
        scratch_shapes=[pltpu.SemaphoreType.DMA((2, 2))],
        compiler_params=pltpu.CompilerParams(vmem_limit_bytes=4 * MIB),
        cost_estimate=pl.CostEstimate(flops=0, bytes_accessed=8 * slabs * rows * half, transcendentals=0),
    )(place, token, *operands)


def load_whole_body(place, token, source, target, sem):
    run([pltpu.make_async_copy(source, target, sem.at[0])])


def load_whole(place, token, array):
    return pl.pallas_call(
        load_whole_body,
        out_shape=pltpu.VMEM(array.shape, array.dtype),
        in_specs=[SMEM, ANY, ANY],
        out_specs=VMEM,
        scratch_shapes=[pltpu.SemaphoreType.DMA((1,))],
        compiler_params=pltpu.CompilerParams(vmem_limit_bytes=6 * MIB),
        cost_estimate=pl.CostEstimate(flops=0, bytes_accessed=2 * array.size, transcendentals=0),
    )(place, token, in_hbm(array))


def image_body(place, table, extended, vectors, blocks, keep, send, moments, image):
    slabs, count, _ = vectors.shape
    reach = table.shape[1] // 2
    quotient, old = jnp.zeros((count, count), f32), jnp.zeros((count, count), f32)
    for slab in range(slabs):
        summed = None
        for entry in range(reach):
            rows = extended[table[slab, entry] + (slab + slabs)]
            term = dot(rows, blocks[table[slab, reach + entry]])
            summed = term if summed is None else summed + term
        rounded = summed.astype(bf16)
        image[slab] = rounded
        quotient = quotient + dot_t(vectors[slab], rounded)
        old = old + dot_t(vectors[slab], vectors[slab])
    moments[:, 0:count] = quotient
    moments[:, count : 2 * count] = old
    mine = slabs // 2
    keep[...] = image[pl.ds(place[0] * mine, mine)]
    send[...] = image[pl.ds((1 - place[0]) * mine, mine)]


def image_halves(place, table, extended, vectors, blocks):
    slabs, rows, half = vectors.shape
    part = struct((slabs // 2, rows, half))
    return kernel_call(
        image_body,
        (part, part, struct((rows, 2 * rows), f32)),
        [SMEM, SMEM, VMEM, VMEM, VMEM],
        [pltpu.VMEM((slabs, rows, half), bf16)],
        flops=14 * slabs * rows * 2 * half * half,
        size=2 * blocks.size,
    )(place, table, extended, vectors, blocks)


def both_parts(place, half):
    return columns(place[0], half), columns(1 - place[0], half)


def first_vectors_body(place, extended, weights, out):
    count, half = out.shape[0], weights.shape[-1]
    first = extended.shape[0] // 3 + count * place[0]
    for part, cols in enumerate(both_parts(place, half)):
        for slab in range(count):
            own = first + slab
            summed = dot(extended[own - 1], weights[0, part, slab])
            summed = summed + dot(extended[own + 1], weights[1, part, slab])
            out[slab, :, cols] = (extended[own, :, cols].astype(f32) - summed).astype(bf16)


def first_body(place, image, inner, outer, vectors, weights, out):
    count, rows, _ = image.shape
    half = weights.shape[-1]
    odd = place[0] == 1
    below = [jnp.where(odd, inner[0], outer[0])] + [image[slab] for slab in range(count - 1)]
    above = [image[slab] for slab in range(1, count)] + [jnp.where(odd, outer[0], inner[0])]
    for slab in range(count):
        out[slab, rows : 2 * rows] = vectors[slab]
    for part, cols in enumerate(both_parts(place, half)):
        for slab in range(count):
            summed = dot(below[slab], weights[0, part, slab]) + dot(above[slab], weights[1, part, slab])
            out[slab, 0:rows, cols] = (image[slab, :, cols].astype(f32) - summed).astype(bf16)


def reduce_rows(place, own, partners, sides, weights, out):
    for part, cols in enumerate(both_parts(place, weights.shape[-1])):
        for slab in range(own.shape[0]):
            summed = None
            for side, rows in zip(sides, partners):
                term = dot(rows[slab], weights[side, part, slab])
                summed = term if summed is None else summed + term
            out[slab, :, cols] = (own[slab, :, cols].astype(f32) - summed).astype(bf16)


def second_body(place, own, inner, outer, weights, moments, note, out, lifted):
    count, rows, _ = out.shape
    lifted[count * rows :] = note[...]
    high = moments[:, 0:rows].astype(bf16)
    low = (moments[:, 0:rows] - high.astype(f32)).astype(bf16)
    factors = (high.T, low.T)
    for part, cols in enumerate(both_parts(place, weights.shape[-1])):
        for slab in range(count):
            summed = dot(inner[slab], weights[1 - place[0], part, slab])
            summed = summed + dot(outer[slab], weights[place[0], part, slab])
            both = own[slab, :, cols].astype(f32) - summed
            image, vectors = both[:rows], both[rows:].astype(bf16)
            for factor in factors:
                image = image - dot(factor, vectors)
            out[slab, :, cols] = image.astype(bf16)
            lifted[slab * rows : (slab + 1) * rows, cols] = image.astype(bf16)


def level_body(place, own, below, above, weights, out):
    reduce_rows(place, own, (below, above), (0, 1), weights, out)


def third_body(place, own, lifted, above, weights, out):
    count, rows, _ = own.shape
    below = [lifted[slab * rows : (slab + 1) * rows] for slab in range(count)]
    reduce_rows(place, own, (below, above), (0, 1), weights, out)


def product(place, rows, weights, whole, targets):
    for part, cols in enumerate(both_parts(place, weights.shape[-1])):
        for slab in range(whole.shape[0]):
            result = dot(rows[slab], weights[part, slab]).astype(bf16)
            targets[part][slab] = result
            whole[slab, :, cols] = result


def last_body(place, own, other, weights, whole, keep, send, rows):
    reduce_rows(place, own, (other,), (0,), weights, rows)
    product(place, rows, weights.at[1], whole, (keep, send))


def final_body(place, own, final, packed, whole, keep, send, weights, sem):
    count = own.shape[0]
    sources = (final.at[pl.ds(place[0] * count, count)], packed.at[packed.shape[0] - 1])
    run([
        pltpu.make_async_copy(source, weights.at[part], sem.at[part])
        for part, source in enumerate(sources)
    ])
    product(place, own, weights, whole, (keep, send))


def level_flops(operand, products):
    return 2 * products * operand.size * operand.shape[-1]


def add_pairs(place, table, targets, inside, window, blocks, others, summed):
    half = blocks.shape[-1]
    reach = table.shape[1] // 2
    first = place[0] * 2
    mine, theirs = columns(place[0], half), columns(1 - place[0], half)
    for target in targets:

        @pl.loop(0, reach)
        def _(entry):
            source = target + table[first + target, entry]

            @pl.when(inside(source))
            def _():
                block = table[first + target, reach + entry]
                vectors = window(source)
                summed[target, :, mine] += dot(vectors, blocks[block])
                summed[target, :, theirs] += dot(vectors, others[block])


def own_pairs_body(place, table, levels, index, extended, image, correction, blocks, others, summed, out, shift):
    own, rows, _ = image.shape
    below = extended.shape[0] // 3
    first = place[0] * own
    shift[...] = jnp.full(shift.shape, levels[index[0]], f32)
    summed[...] = jnp.zeros(summed.shape, f32)
    add_pairs(
        place, table, range(below + own),
        lambda source: jnp.logical_and(source >= below, source < below + own),
        lambda source: correction[source - below], blocks, others, summed,
    )
    overlap = jnp.zeros((2 * rows, rows), f32)
    mixed = jnp.zeros((rows, rows), f32)
    for slab in range(own):
        vectors, fixed = extended[first + below + slab], correction[slab]
        overlap = overlap + dot_t(jnp.concatenate([vectors, fixed], 0), fixed)
        mixed = mixed + dot_t(fixed, image[slab])
    out[0 : 2 * rows, 0:rows] = jnp.zeros((2 * rows, rows), f32)
    out[0 : 2 * rows, rows : 2 * rows] = overlap
    out[2 * rows :, 0:rows] = mixed[: rows // 2]
    out[2 * rows :, rows : 2 * rows] = mixed[rows // 2 :]


def cross_pairs_body(
    place, table, extended, correction, near, far, blocks, others, begun, part, keep, send, window, summed, out
):
    own, rows, _ = correction.shape
    below = window.shape[0]
    first = place[0] * own
    window[0:own] = far[...]
    window[own : 2 * own] = near[...]
    summed[below : below + own] = begun[below : below + own]
    add_pairs(
        place, table, range(below, below + own),
        lambda source: jnp.logical_and(source >= 0, source < below),
        lambda source: window[source], blocks, others, summed,
    )
    pencil = jnp.zeros((2 * rows, rows), f32)
    for slab in range(below + own):
        fixed = window[slab] if slab < below else correction[slab - below]
        terms = begun[slab] if slab < below else summed[slab]
        basis = jnp.concatenate([extended[first + slab], fixed], 0)
        pencil = pencil + dot_t(basis, terms.astype(bf16))
    out[...] = part[...]
    out[0 : 2 * rows, 0:rows] = pencil
    keep[...] = out[row_half(place[0], keep)]
    send[...] = out[row_half(1 - place[0], keep)]


def row_half(index, part):
    return pl.ds(pl.multiple_of(index * part.shape[0], 8), part.shape[0])


def assemble_body(scale, place, shift, moments, keep, received, first, second, gram, pencil, result, whole):
    rows = moments.shape[0]
    own = keep.shape[0]
    result[pl.ds(place[0] * own, own)] = keep[...]
    result[pl.ds((1 - place[0]) * own, own)] = received[...]
    whole[row_half(place[0], first)] = first[...] * scale
    whole[row_half(1 - place[0], first)] = second[...] * scale
    top, bottom = whole[0 : 2 * rows], whole[2 * rows :]
    overlap = top[:, rows:]
    mixed = jnp.concatenate([bottom[:, :rows], bottom[:, rows:]], 0)
    left = jnp.concatenate([moments[:, rows:], overlap[:rows].T], 0)
    product = jnp.concatenate([left, overlap], 1)
    gram[...] = product
    projected = jnp.concatenate([jnp.concatenate([moments[:, :rows], mixed], 0), top[:, :rows]], 1)
    pencil[...] = projected - shift[0:1] * product


def swapped(operand):
    return lax.ppermute(operand, "vec", SWAP)


def along(operand, axis, distance):
    count = lax.axis_size("slab") * (2 if axis == CHAIN else 1)
    route = [(i, i + distance) for i in range(count) if 0 <= i + distance < count]
    return lax.ppermute(operand, axis, route)


def pair_routes(distance):
    chain = 2 * lax.axis_size("slab")
    routes = []
    for bit in range(2):
        ups = [(i, i + distance) for i in range(chain - distance) if i // distance % 2 == bit]
        routes.append(ups + [(j, i) for i, j in ups])
    return [route for route in routes if route]


def summed_up(parts):
    while len(parts) > 1:
        parts = [a + b for a, b in zip(parts[::2], parts[1::2])]
    return parts[0]


def slab_total(part):
    slabs = lax.axis_size("slab")
    reach = 1
    while reach < slabs:
        radix = min(4, slabs // reach)
        routes = [[(i, i ^ (offset * reach)) for i in range(slabs)] for offset in range(1, radix)]
        part = summed_up([part] + [lax.ppermute(part, "slab", route) for route in routes])
        reach *= radix
    return part


def on_device(
    vectors,
    blocks,
    slab_blocks,
    far_source,
    far_block,
    level_lower,
    level_upper,
    level_final,
    shift_levels,
    shift_index,
):
    slab_count, rows, half = vectors.shape
    own_count = slab_count // 2
    slabs = lax.axis_size("slab")
    chain = 2 * slabs
    width = blocks.shape[1]
    rows_total = slab_count * slabs * width
    levels = [l for l in range(level_lower.shape[0]) if 2**l < slab_count * slabs]
    slab, core = lax.axis_index("slab"), lax.axis_index("vec")
    link = 2 * slab + core
    steps = [max(2**l // own_count, 1) for l in levels]
    place = jnp.stack([core] + [link // step % 2 for step in steps]).astype(jnp.int32)

    below, above = along(vectors, "slab", 1), along(vectors, "slab", -1)
    slab_ids = slab * slab_count + jnp.arange(slab_count, dtype=jnp.int32)[:, None]
    near = jnp.broadcast_to(jnp.arange(-1, 2, dtype=jnp.int32), (slab_count, 3))
    table = jnp.concatenate([near, far_source - slab_ids, slab_blocks, far_block], 1)
    note = jnp.pad(table.astype(bf16), ((0, 16 - slab_count), (0, width - table.shape[1])))
    held_blocks, theirs_0, theirs = prepare(place, level_lower, level_upper, blocks)
    extended = lax.all_gather(jnp.concatenate([below, vectors, above], 0), "vec", axis=2, tiled=True)
    theirs_0, extended = lax.optimization_barrier((theirs_0, extended))
    packed_0 = swapped(theirs_0)
    keep, send, moments = image_halves(place, table, extended, vectors, in_vmem(held_blocks))
    send, moments, packed_0 = lax.optimization_barrier((send, moments, packed_0))
    body = functools.partial(load_body, 0, 0)
    matrices = load(body, place, keep, level_lower, level_upper, packed_0)
    received, moments = swapped(send), moments + swapped(moments)
    image = jnp.where(core == 0, jnp.concatenate([keep, received], 2), jnp.concatenate([received, keep], 2))
    image, moments, theirs, matrices = lax.optimization_barrier((image, moments, theirs, matrices))
    matrices = in_vmem(matrices)
    packed = swapped(theirs)

    inner_route, outer_route = pair_routes(1)
    outer = lax.ppermute(lax.dynamic_slice_in_dim(image, (own_count - 1) * core, 1), CHAIN, outer_route)
    inner = swapped(lax.dynamic_slice_in_dim(image, (own_count - 1) * (1 - core), 1))
    flips = [[(i, i ^ 2**bit) for i in range(slabs)] for bit in range((slabs - 1).bit_length())]
    received = lax.ppermute(moments, "slab", flips[0])
    vectors_1 = kernel_call(
        first_vectors_body,
        struct(image.shape),
        [SMEM] + [VMEM] * 2,
        flops=level_flops(image, 2),
    )(place, extended, matrices)
    both = kernel_call(
        first_body,
        struct((own_count, 2 * rows, width)),
        [SMEM] + [VMEM] * 5,
        flops=level_flops(image, 2),
    )(place, image, inner, outer, vectors_1, matrices)
    both, received, late_blocks, packed = lax.optimization_barrier((both, received, blocks, packed))
    others = swapped(late_blocks)
    outer, inner = lax.ppermute(both, CHAIN, outer_route), swapped(both)
    for flip in flips[1:]:
        moments = moments + received
        received = lax.ppermute(moments, "slab", flip)
    moments = (moments + received) / rows_total
    matrices, theirs = load_and_pack(
        1, 1, levels[3:], place, both, level_lower, level_upper, level_final, packed
    )
    matrices = in_vmem(matrices)
    theirs, inner, outer, moments = lax.optimization_barrier((theirs, inner, outer, moments))
    following = swapped(theirs)
    residual, lifted = kernel_call(
        second_body,
        (struct(image.shape), struct((own_count * rows + 16, width))),
        [SMEM] + [VMEM] * 6,
        flops=level_flops(both, 2),
    )(place, both, inner, outer, matrices, moments, note)

    part = struct((own_count, rows, half))
    ends = (struct(residual.shape), part, part)
    one_partner = chain == 2 * steps[-1]
    for level, step in zip(levels[2:], steps[2:]):
        last = level == levels[-1]
        if last:
            held_blocks = load_whole(place, residual, blocks)
        if last and one_partner:
            body = functools.partial(load_last_body, level, 3)
            matrices = load(body, place, residual, level_lower, level_upper, packed, level_final)
            (route,) = pair_routes(step)
            other = lax.ppermute(residual, CHAIN, route)
            other, held_blocks = lax.optimization_barrier((other, held_blocks))
            correction, keep, send = kernel_call(
                last_body,
                ends,
                [SMEM] + [VMEM] * 3,
                [pltpu.VMEM(residual.shape, bf16)],
                flops=level_flops(residual, 2),
            )(place, residual, other, in_vmem(matrices))
            break
        body = functools.partial(load_body, level, 1 if level == 2 else 3)
        matrices = load(body, place, residual, level_lower, level_upper, packed)
        below, above = along(residual if level > 2 else lifted, CHAIN, step), along(residual, CHAIN, -step)
        if level == 2:
            count = own_count * rows
            lower_table = below[count : count + slab_count, : table.shape[1]].astype(jnp.int32)
            packed, below, above = lax.optimization_barrier((following, below, above))
        if level == 3:
            below, above, matrices = lax.optimization_barrier((below, above, matrices))
        residual = kernel_call(
            level_body if level > 2 else third_body,
            struct(residual.shape),
            [SMEM] + [VMEM] * 4,
            flops=level_flops(residual, 2),
        )(place, residual, below, above, in_vmem(matrices))
    if not one_partner:
        correction, keep, send = kernel_call(
            final_body,
            ends,
            [SMEM, VMEM, ANY, ANY],
            [pltpu.VMEM((2, own_count, width, half), bf16), pltpu.SemaphoreType.DMA((2,))],
            flops=level_flops(residual, 1),
        )(place, residual, in_hbm(level_final), packed)
    held_blocks, others = in_vmem(held_blocks), in_vmem(others)

    far, near = along(correction, CHAIN, 2), along(correction, CHAIN, 1)
    received = swapped(send)
    result_parts = (keep, received)
    tables = jnp.concatenate([lower_table, table], 0)
    flops = level_flops(image, 7)
    sums = (5 * rows // 2, 2 * rows)
    begun, part, shift = kernel_call(
        own_pairs_body,
        (struct((3 * own_count, rows, width), f32), struct(sums, f32), struct((8, 2 * rows), f32)),
        [SMEM] * 4 + [VMEM] * 5,
        flops=flops,
    )(place, tables, shift_levels, shift_index, extended, image, correction, held_blocks, others)
    share = struct((sums[0] // 2, sums[1]), f32)
    keep, send = kernel_call(
        cross_pairs_body,
        (share, share),
        [SMEM] * 2 + [VMEM] * 8,
        [
            pltpu.VMEM((2 * own_count, rows, width), bf16),
            pltpu.VMEM((3 * own_count, rows, width), f32),
            pltpu.VMEM(sums, f32),
        ],
        flops=flops,
    )(place, tables, extended, correction, near, far, held_blocks, others, begun, part)
    share = slab_total(keep + swapped(send))
    square = struct((2 * rows, 2 * rows), f32)
    gram, pencil, result = kernel_call(
        functools.partial(assemble_body, 1.0 / rows_total),
        (square, square, struct(vectors.shape)),
        [SMEM] + [VMEM] * 6,
        [pltpu.VMEM(sums, f32)],
    )(place, shift, moments, *result_parts, share, swapped(share))
    return (result, gram, pencil)


def solution(mesh):
    in_specs = (
        P(("groups", "slab"), None, "vec"),
        P("groups", None, "vec"),
        P(("groups", "slab"), None),
        P(("groups", "slab"), None),
        P(("groups", "slab"), None),
        P(None, ("groups", "slab"), None, "vec"),
        P(None, ("groups", "slab"), None, "vec"),
        P(("groups", "slab"), None, "vec"),
        P("groups"),
        P("groups"),
    )
    out_specs = (P(("groups", "slab"), None, "vec"), P("groups", None), P("groups", None))
    return jax.shard_map(
        on_device, mesh=mesh, in_specs=in_specs, out_specs=out_specs, check_vma=False
    )
```

```python
import functools

import jax
import jax.numpy as jnp
from jax import lax
from jax.experimental import pallas as pl
from jax.experimental.pallas import tpu as pltpu
from jax.sharding import PartitionSpec as P

f32, bf16 = jnp.float32, jnp.bfloat16
CHAIN = ("slab", "vec")
ANY = pl.BlockSpec(memory_space=pl.ANY)
VMEM = pl.BlockSpec(memory_space=pltpu.VMEM)
SMEM = pl.BlockSpec(memory_space=pltpu.SMEM)
SWAP = [(0, 1), (1, 0)]
MIB = 1024 * 1024


def kernel_call(body, out_shape, in_specs, scratch=(), vmem=16 * MIB, flops=0, size=0):
    return pl.pallas_call(
        body,
        out_shape=out_shape,
        in_specs=in_specs,
        out_specs=jax.tree.map(lambda _: VMEM, out_shape),
        scratch_shapes=list(scratch),
        compiler_params=pltpu.CompilerParams(vmem_limit_bytes=vmem),
        cost_estimate=pl.CostEstimate(flops=flops, bytes_accessed=size, transcendentals=0),
    )


def struct(shape, dtype=bf16):
    return jax.ShapeDtypeStruct(shape, dtype)


def dot(rows, matrix):
    return jnp.dot(rows, matrix, preferred_element_type=f32)


def dot_t(left, right):
    return lax.dot_general(left, right, (((1,), (1,)), ((), ())), preferred_element_type=f32)


def columns(index, width):
    return pl.ds(pl.multiple_of(index * width, width), width)


def in_vmem(operand):
    return pltpu.with_memory_space_constraint(operand, pltpu.VMEM)


def in_hbm(operand):
    return pltpu.with_memory_space_constraint(operand, pltpu.HBM)


def run(copies):
    for copy in copies:
        copy.start()
    for copy in copies:
        copy.wait()


def through(parts, held, outs, sem):
    ins = [pltpu.make_async_copy(part, held.at[k], sem.at[0, k]) for k, part in enumerate(parts)]
    outs = [pltpu.make_async_copy(held.at[k], out, sem.at[1, k]) for k, out in enumerate(outs)]
    return ins, outs


def finish(ins, outs, others):
    for copy, following in zip(ins, outs):
        copy.wait()
        following.start()
    for copy in others + outs:
        copy.wait()


def prepare_body(place, lower, upper, blocks, held_blocks, first, second, held, sem, block_sem):
    count = held.shape[1]
    slabs = pl.ds((1 - place[0]) * count, count)
    parts = [ref.at[level, slabs] for level in range(3) for ref in (lower, upper)]
    outs = [first.at[k] for k in range(2)] + [second.at[k] for k in range(4)]
    ins, outs = through(parts, held, outs, sem)
    whole = pltpu.make_async_copy(blocks, held_blocks, block_sem.at[0])
    for copy in ins + [whole]:
        copy.start()
    finish(ins, outs, [whole])


def prepare(place, lower, upper, blocks):
    _, slabs, rows, half = lower.shape
    shape = (slabs // 2, rows, half)
    size = 2 * slabs * rows * half
    return pl.pallas_call(
        prepare_body,
        out_shape=[
            pltpu.VMEM(blocks.shape, bf16),
            pltpu.HBM((2,) + shape, bf16),
            pltpu.HBM((4,) + shape, bf16),
        ],
        in_specs=[SMEM] + [ANY] * 3,
        out_specs=[VMEM, ANY, ANY],
        scratch_shapes=[
            pltpu.VMEM((6,) + shape, bf16),
            pltpu.SemaphoreType.DMA((2, 6)),
            pltpu.SemaphoreType.DMA((1,)),
        ],
        compiler_params=pltpu.CompilerParams(vmem_limit_bytes=10 * MIB),
        cost_estimate=pl.CostEstimate(
            flops=0, bytes_accessed=2 * blocks.size + 6 * size, transcendentals=0
        ),
    )(place, *[in_hbm(x) for x in (lower, upper, blocks)])


def load_and_pack_body(level, first, later, place, token, lower, upper, final, packed, weights, out, held, sem, pack_sem):
    count = weights.shape[2]
    slabs = pl.ds((1 - place[0]) * count, count)
    parts = [ref.at[each, slabs] for each in later for ref in (lower, upper)] + [final.at[slabs]]
    ins, outs = through(parts, held, [out.at[k] for k in range(len(parts))], pack_sem)
    loads = level_copies(level, first, place, lower, upper, packed, weights, sem)
    for copy in ins + loads:
        copy.start()
    finish(ins, outs, loads)


def load_and_pack(level, first, later, place, token, lower, upper, final, packed):
    _, slabs, rows, half = lower.shape
    shape = (2, 2, slabs // 2, rows, half)
    count = 2 * len(later) + 1
    later_shape = (count,) + shape[2:]
    return pl.pallas_call(
        functools.partial(load_and_pack_body, level, first, later),
        out_shape=[pltpu.VMEM(shape, bf16), pltpu.HBM(later_shape, bf16)],
        in_specs=[SMEM] + [ANY] * 5,
        out_specs=[VMEM, ANY],
        scratch_shapes=[
            pltpu.VMEM(later_shape, bf16),
            pltpu.SemaphoreType.DMA((2, 2)),
            pltpu.SemaphoreType.DMA((2, count)),
        ],
        compiler_params=pltpu.CompilerParams(vmem_limit_bytes=8 * MIB),
        cost_estimate=pl.CostEstimate(
            flops=0, bytes_accessed=(8 + 4 * count) * slabs * rows * half // 2, transcendentals=0
        ),
    )(place, token, *[in_hbm(x) for x in (lower, upper, final)], packed)


def level_copies(level, first, place, lower, upper, packed, weights, sem):
    count = weights.shape[2]
    slabs = pl.ds(place[0] * count, count)
    copies = []
    for side, ref in enumerate((lower, upper)):
        sources = (ref.at[level, slabs], packed.at[2 * (level - first) + side])
        for part, source in enumerate(sources):
            copies.append(pltpu.make_async_copy(source, weights.at[side, part], sem.at[side, part]))
    return copies


def load_body(level, first, place, token, lower, upper, packed, weights, sem):
    run(level_copies(level, first, place, lower, upper, packed, weights, sem))


def load_last_body(level, first, place, token, lower, upper, packed, final, weights, sem):
    count = weights.shape[2]
    slabs = pl.ds(place[0] * count, count)
    above = 1 - place[1 + level]

    def copy(source, side, part):
        return pltpu.make_async_copy(source, weights.at[side, part], sem.at[side, part])

    pl.when(above == 1)(lambda: copy(upper.at[level, slabs], 0, 0).start())
    pl.when(above == 0)(lambda: copy(lower.at[level, slabs], 0, 0).start())
    others = [
        copy(packed.at[2 * (level - first) + above], 0, 1),
        copy(final.at[slabs], 1, 0),
        copy(packed.at[packed.shape[0] - 1], 1, 1),
    ]
    for each in others:
        each.start()
    copy(lower.at[level, slabs], 0, 0).wait()
    for each in others:
        each.wait()


def load(body, place, token, lower, upper, packed, *finals):
    _, slabs, rows, half = lower.shape
    shape = (2, 2, slabs // 2, rows, half)
    operands = [in_hbm(lower), in_hbm(upper), packed] + [in_hbm(x) for x in finals]
    return pl.pallas_call(
        body,
        out_shape=pltpu.VMEM(shape, bf16),
        in_specs=[SMEM] + [ANY] * (1 + len(operands)),
        out_specs=VMEM,
        scratch_shapes=[pltpu.SemaphoreType.DMA((2, 2))],
        compiler_params=pltpu.CompilerParams(vmem_limit_bytes=4 * MIB),
        cost_estimate=pl.CostEstimate(flops=0, bytes_accessed=8 * slabs * rows * half, transcendentals=0),
    )(place, token, *operands)


def load_whole_body(place, token, source, target, sem):
    run([pltpu.make_async_copy(source, target, sem.at[0])])


def load_whole(place, token, array):
    return pl.pallas_call(
        load_whole_body,
        out_shape=pltpu.VMEM(array.shape, array.dtype),
        in_specs=[SMEM, ANY, ANY],
        out_specs=VMEM,
        scratch_shapes=[pltpu.SemaphoreType.DMA((1,))],
        compiler_params=pltpu.CompilerParams(vmem_limit_bytes=6 * MIB),
        cost_estimate=pl.CostEstimate(flops=0, bytes_accessed=2 * array.size, transcendentals=0),
    )(place, token, in_hbm(array))


def image_body(place, table, extended, vectors, blocks, keep, send, moments, image):
    slabs, count, _ = vectors.shape
    reach = table.shape[1] // 2
    quotient, old = jnp.zeros((count, count), f32), jnp.zeros((count, count), f32)
    for slab in range(slabs):
        summed = None
        for entry in range(reach):
            rows = extended[table[slab, entry] + (slab + slabs)]
            term = dot(rows, blocks[table[slab, reach + entry]])
            summed = term if summed is None else summed + term
        rounded = summed.astype(bf16)
        image[slab] = rounded
        quotient = quotient + dot_t(vectors[slab], rounded)
        old = old + dot_t(vectors[slab], vectors[slab])
    moments[:, 0:count] = quotient
    moments[:, count : 2 * count] = old
    mine = slabs // 2
    keep[...] = image[pl.ds(place[0] * mine, mine)]
    send[...] = image[pl.ds((1 - place[0]) * mine, mine)]


def image_halves(place, table, extended, vectors, blocks):
    slabs, rows, half = vectors.shape
    part = struct((slabs // 2, rows, half))
    return kernel_call(
        image_body,
        (part, part, struct((rows, 2 * rows), f32)),
        [SMEM, SMEM, VMEM, VMEM, VMEM],
        [pltpu.VMEM((slabs, rows, half), bf16)],
        flops=14 * slabs * rows * 2 * half * half,
        size=2 * blocks.size,
    )(place, table, extended, vectors, blocks)


def both_parts(place, half):
    return columns(place[0], half), columns(1 - place[0], half)


def first_vectors_body(place, extended, weights, out):
    count, half = out.shape[0], weights.shape[-1]
    first = extended.shape[0] // 3 + count * place[0]
    for part, cols in enumerate(both_parts(place, half)):
        for slab in range(count):
            own = first + slab
            summed = dot(extended[own - 1], weights[0, part, slab])
            summed = summed + dot(extended[own + 1], weights[1, part, slab])
            out[slab, :, cols] = (extended[own, :, cols].astype(f32) - summed).astype(bf16)


def first_body(place, image, inner, outer, vectors, weights, out):
    count, rows, _ = image.shape
    half = weights.shape[-1]
    odd = place[0] == 1
    below = [jnp.where(odd, inner[0], outer[0])] + [image[slab] for slab in range(count - 1)]
    above = [image[slab] for slab in range(1, count)] + [jnp.where(odd, outer[0], inner[0])]
    for slab in range(count):
        out[slab, rows : 2 * rows] = vectors[slab]
    for part, cols in enumerate(both_parts(place, half)):
        for slab in range(count):
            summed = dot(below[slab], weights[0, part, slab]) + dot(above[slab], weights[1, part, slab])
            out[slab, 0:rows, cols] = (image[slab, :, cols].astype(f32) - summed).astype(bf16)


def reduce_rows(place, own, partners, sides, weights, out):
    for part, cols in enumerate(both_parts(place, weights.shape[-1])):
        for slab in range(own.shape[0]):
            summed = None
            for side, rows in zip(sides, partners):
                term = dot(rows[slab], weights[side, part, slab])
                summed = term if summed is None else summed + term
            out[slab, :, cols] = (own[slab, :, cols].astype(f32) - summed).astype(bf16)


def second_body(place, own, inner, outer, weights, moments, note, out, lifted):
    count, rows, _ = out.shape
    lifted[count * rows :] = note[...]
    high = moments[:, 0:rows].astype(bf16)
    low = (moments[:, 0:rows] - high.astype(f32)).astype(bf16)
    factors = (high.T, low.T)
    for part, cols in enumerate(both_parts(place, weights.shape[-1])):
        for slab in range(count):
            summed = dot(inner[slab], weights[1 - place[0], part, slab])
            summed = summed + dot(outer[slab], weights[place[0], part, slab])
            both = own[slab, :, cols].astype(f32) - summed
            image, vectors = both[:rows], both[rows:].astype(bf16)
            for factor in factors:
                image = image - dot(factor, vectors)
            out[slab, :, cols] = image.astype(bf16)
            lifted[slab * rows : (slab + 1) * rows, cols] = image.astype(bf16)


def level_body(place, own, below, above, weights, out):
    reduce_rows(place, own, (below, above), (0, 1), weights, out)


def third_body(place, own, lifted, above, weights, out):
    count, rows, _ = own.shape
    below = [lifted[slab * rows : (slab + 1) * rows] for slab in range(count)]
    reduce_rows(place, own, (below, above), (0, 1), weights, out)


def product(place, rows, weights, whole, targets):
    for part, cols in enumerate(both_parts(place, weights.shape[-1])):
        for slab in range(whole.shape[0]):
            result = dot(rows[slab], weights[part, slab]).astype(bf16)
            targets[part][slab] = result
            whole[slab, :, cols] = result


def last_body(place, own, other, weights, whole, keep, send, rows):
    reduce_rows(place, own, (other,), (0,), weights, rows)
    product(place, rows, weights.at[1], whole, (keep, send))


def final_body(place, own, final, packed, whole, keep, send, weights, sem):
    count = own.shape[0]
    sources = (final.at[pl.ds(place[0] * count, count)], packed.at[packed.shape[0] - 1])
    run([
        pltpu.make_async_copy(source, weights.at[part], sem.at[part])
        for part, source in enumerate(sources)
    ])
    product(place, own, weights, whole, (keep, send))


def level_flops(operand, products):
    return 2 * products * operand.size * operand.shape[-1]


def add_pairs(place, table, targets, inside, window, blocks, others, summed):
    half = blocks.shape[-1]
    reach = table.shape[1] // 2
    first = place[0] * 2
    mine, theirs = columns(place[0], half), columns(1 - place[0], half)
    for target in targets:

        @pl.loop(0, reach)
        def _(entry):
            source = target + table[first + target, entry]

            @pl.when(inside(source))
            def _():
                block = table[first + target, reach + entry]
                vectors = window(source)
                summed[target, :, mine] += dot(vectors, blocks[block])
                summed[target, :, theirs] += dot(vectors, others[block])


def own_pairs_body(place, table, levels, index, extended, image, correction, blocks, others, summed, out, shift):
    own, rows, _ = image.shape
    below = extended.shape[0] // 3
    first = place[0] * own
    shift[...] = jnp.full(shift.shape, levels[index[0]], f32)
    summed[...] = jnp.zeros(summed.shape, f32)
    add_pairs(
        place, table, range(below + own),
        lambda source: jnp.logical_and(source >= below, source < below + own),
        lambda source: correction[source - below], blocks, others, summed,
    )
    overlap = jnp.zeros((2 * rows, rows), f32)
    mixed = jnp.zeros((rows, rows), f32)
    for slab in range(own):
        vectors, fixed = extended[first + below + slab], correction[slab]
        overlap = overlap + dot_t(jnp.concatenate([vectors, fixed], 0), fixed)
        mixed = mixed + dot_t(fixed, image[slab])
    out[0 : 2 * rows, 0:rows] = jnp.zeros((2 * rows, rows), f32)
    out[0 : 2 * rows, rows : 2 * rows] = overlap
    out[2 * rows :, 0:rows] = mixed[: rows // 2]
    out[2 * rows :, rows : 2 * rows] = mixed[rows // 2 :]


def cross_pairs_body(
    place, table, extended, correction, near, far, blocks, others, begun, part, keep, send, window, summed, out
):
    own, rows, _ = correction.shape
    below = window.shape[0]
    first = place[0] * own
    window[0:own] = far[...]
    window[own : 2 * own] = near[...]
    summed[below : below + own] = begun[below : below + own]
    add_pairs(
        place, table, range(below, below + own),
        lambda source: jnp.logical_and(source >= 0, source < below),
        lambda source: window[source], blocks, others, summed,
    )
    pencil = jnp.zeros((2 * rows, rows), f32)
    for slab in range(below + own):
        fixed = window[slab] if slab < below else correction[slab - below]
        terms = begun[slab] if slab < below else summed[slab]
        basis = jnp.concatenate([extended[first + slab], fixed], 0)
        pencil = pencil + dot_t(basis, terms.astype(bf16))
    out[...] = part[...]
    out[0 : 2 * rows, 0:rows] = pencil
    keep[...] = out[row_half(place[0], keep)]
    send[...] = out[row_half(1 - place[0], keep)]


def row_half(index, part):
    return pl.ds(pl.multiple_of(index * part.shape[0], 8), part.shape[0])


def assemble_body(scale, place, shift, moments, keep, received, first, second, gram, pencil, result, whole):
    rows = moments.shape[0]
    own = keep.shape[0]
    result[pl.ds(place[0] * own, own)] = keep[...]
    result[pl.ds((1 - place[0]) * own, own)] = received[...]
    whole[row_half(place[0], first)] = first[...] * scale
    whole[row_half(1 - place[0], first)] = second[...] * scale
    top, bottom = whole[0 : 2 * rows], whole[2 * rows :]
    overlap = top[:, rows:]
    mixed = jnp.concatenate([bottom[:, :rows], bottom[:, rows:]], 0)
    left = jnp.concatenate([moments[:, rows:], overlap[:rows].T], 0)
    product = jnp.concatenate([left, overlap], 1)
    gram[...] = product
    projected = jnp.concatenate([jnp.concatenate([moments[:, :rows], mixed], 0), top[:, :rows]], 1)
    pencil[...] = projected - shift[0:1] * product


def swapped(operand):
    return lax.ppermute(operand, "vec", SWAP)


def along(operand, axis, distance):
    count = lax.axis_size("slab") * (2 if axis == CHAIN else 1)
    route = [(i, i + distance) for i in range(count) if 0 <= i + distance < count]
    return lax.ppermute(operand, axis, route)


def pair_routes(distance):
    chain = 2 * lax.axis_size("slab")
    routes = []
    for bit in range(2):
        ups = [(i, i + distance) for i in range(chain - distance) if i // distance % 2 == bit]
        routes.append(ups + [(j, i) for i, j in ups])
    return [route for route in routes if route]


def summed_up(parts):
    while len(parts) > 1:
        parts = [a + b for a, b in zip(parts[::2], parts[1::2])]
    return parts[0]


def slab_total(part):
    slabs = lax.axis_size("slab")
    reach = 1
    while reach < slabs:
        radix = min(4, slabs // reach)
        routes = [[(i, i ^ (offset * reach)) for i in range(slabs)] for offset in range(1, radix)]
        part = summed_up([part] + [lax.ppermute(part, "slab", route) for route in routes])
        reach *= radix
    return part


def on_device(
    vectors,
    blocks,
    slab_blocks,
    far_source,
    far_block,
    level_lower,
    level_upper,
    level_final,
    shift_levels,
    shift_index,
):
    slab_count, rows, half = vectors.shape
    own_count = slab_count // 2
    slabs = lax.axis_size("slab")
    chain = 2 * slabs
    width = blocks.shape[1]
    rows_total = slab_count * slabs * width
    levels = [l for l in range(level_lower.shape[0]) if 2**l < slab_count * slabs]
    slab, core = lax.axis_index("slab"), lax.axis_index("vec")
    link = 2 * slab + core
    steps = [max(2**l // own_count, 1) for l in levels]
    place = jnp.stack([core] + [link // step % 2 for step in steps]).astype(jnp.int32)

    below, above = along(vectors, "slab", 1), along(vectors, "slab", -1)
    slab_ids = slab * slab_count + jnp.arange(slab_count, dtype=jnp.int32)[:, None]
    near = jnp.broadcast_to(jnp.arange(-1, 2, dtype=jnp.int32), (slab_count, 3))
    table = jnp.concatenate([near, far_source - slab_ids, slab_blocks, far_block], 1)
    note = jnp.pad(table.astype(bf16), ((0, 16 - slab_count), (0, width - table.shape[1])))
    held_blocks, theirs_0, theirs = prepare(place, level_lower, level_upper, blocks)
    extended = lax.all_gather(jnp.concatenate([below, vectors, above], 0), "vec", axis=2, tiled=True)
    theirs_0, extended = lax.optimization_barrier((theirs_0, extended))
    packed_0 = swapped(theirs_0)
    keep, send, moments = image_halves(place, table, extended, vectors, in_vmem(held_blocks))
    received, moments = swapped(send), moments + swapped(moments)
    image = jnp.where(core == 0, jnp.concatenate([keep, received], 2), jnp.concatenate([received, keep], 2))
    image, moments = lax.optimization_barrier((image, moments))
    theirs, packed_0 = lax.optimization_barrier((theirs, packed_0))
    packed = swapped(theirs)

    inner_route, outer_route = pair_routes(1)
    outer = lax.ppermute(lax.dynamic_slice_in_dim(image, (own_count - 1) * core, 1), CHAIN, outer_route)
    inner = swapped(lax.dynamic_slice_in_dim(image, (own_count - 1) * (1 - core), 1))
    flips = [[(i, i ^ 2**bit) for i in range(slabs)] for bit in range((slabs - 1).bit_length())]
    received = lax.ppermute(moments, "slab", flips[0])
    body = functools.partial(load_body, 0, 0)
    matrices = in_vmem(load(body, place, keep, level_lower, level_upper, packed_0))
    vectors_1 = kernel_call(
        first_vectors_body,
        struct(image.shape),
        [SMEM] + [VMEM] * 2,
        flops=level_flops(image, 2),
    )(place, extended, matrices)
    both = kernel_call(
        first_body,
        struct((own_count, 2 * rows, width)),
        [SMEM] + [VMEM] * 5,
        flops=level_flops(image, 2),
    )(place, image, inner, outer, vectors_1, matrices)
    both, received, late_blocks, packed = lax.optimization_barrier((both, received, blocks, packed))
    others = swapped(late_blocks)
    outer, inner = lax.ppermute(both, CHAIN, outer_route), swapped(both)
    for flip in flips[1:]:
        moments = moments + received
        received = lax.ppermute(moments, "slab", flip)
    moments = (moments + received) / rows_total
    matrices, theirs = load_and_pack(
        1, 1, levels[3:], place, both, level_lower, level_upper, level_final, packed
    )
    matrices = in_vmem(matrices)
    theirs, inner, outer, moments = lax.optimization_barrier((theirs, inner, outer, moments))
    following = swapped(theirs)
    residual, lifted = kernel_call(
        second_body,
        (struct(image.shape), struct((own_count * rows + 16, width))),
        [SMEM] + [VMEM] * 6,
        flops=level_flops(both, 2),
    )(place, both, inner, outer, matrices, moments, note)

    part = struct((own_count, rows, half))
    ends = (struct(residual.shape), part, part)
    one_partner = chain == 2 * steps[-1]
    for level, step in zip(levels[2:], steps[2:]):
        last = level == levels[-1]
        if last:
            held_blocks = load_whole(place, residual, blocks)
        if last and one_partner:
            body = functools.partial(load_last_body, level, 3)
            matrices = load(body, place, residual, level_lower, level_upper, packed, level_final)
            (route,) = pair_routes(step)
            other = lax.ppermute(residual, CHAIN, route)
            other, held_blocks = lax.optimization_barrier((other, held_blocks))
            correction, keep, send = kernel_call(
                last_body,
                ends,
                [SMEM] + [VMEM] * 3,
                [pltpu.VMEM(residual.shape, bf16)],
                flops=level_flops(residual, 2),
            )(place, residual, other, in_vmem(matrices))
            break
        body = functools.partial(load_body, level, 1 if level == 2 else 3)
        matrices = load(body, place, residual, level_lower, level_upper, packed)
        below, above = along(residual if level > 2 else lifted, CHAIN, step), along(residual, CHAIN, -step)
        if level == 2:
            count = own_count * rows
            lower_table = below[count : count + slab_count, : table.shape[1]].astype(jnp.int32)
            packed, below, above = lax.optimization_barrier((following, below, above))
        if level == 3:
            below, above, matrices = lax.optimization_barrier((below, above, matrices))
        residual = kernel_call(
            level_body if level > 2 else third_body,
            struct(residual.shape),
            [SMEM] + [VMEM] * 4,
            flops=level_flops(residual, 2),
        )(place, residual, below, above, in_vmem(matrices))
    if not one_partner:
        correction, keep, send = kernel_call(
            final_body,
            ends,
            [SMEM, VMEM, ANY, ANY],
            [pltpu.VMEM((2, own_count, width, half), bf16), pltpu.SemaphoreType.DMA((2,))],
            flops=level_flops(residual, 1),
        )(place, residual, in_hbm(level_final), packed)
    held_blocks, others = in_vmem(held_blocks), in_vmem(others)

    far, near = along(correction, CHAIN, 2), along(correction, CHAIN, 1)
    received = swapped(send)
    result_parts = (keep, received)
    tables = jnp.concatenate([lower_table, table], 0)
    flops = level_flops(image, 7)
    sums = (5 * rows // 2, 2 * rows)
    begun, part, shift = kernel_call(
        own_pairs_body,
        (struct((3 * own_count, rows, width), f32), struct(sums, f32), struct((8, 2 * rows), f32)),
        [SMEM] * 4 + [VMEM] * 5,
        flops=flops,
    )(place, tables, shift_levels, shift_index, extended, image, correction, held_blocks, others)
    share = struct((sums[0] // 2, sums[1]), f32)
    keep, send = kernel_call(
        cross_pairs_body,
        (share, share),
        [SMEM] * 2 + [VMEM] * 8,
        [
            pltpu.VMEM((2 * own_count, rows, width), bf16),
            pltpu.VMEM((3 * own_count, rows, width), f32),
            pltpu.VMEM(sums, f32),
        ],
        flops=flops,
    )(place, tables, extended, correction, near, far, held_blocks, others, begun, part)
    share = slab_total(keep + swapped(send))
    square = struct((2 * rows, 2 * rows), f32)
    gram, pencil, result = kernel_call(
        functools.partial(assemble_body, 1.0 / rows_total),
        (square, square, struct(vectors.shape)),
        [SMEM] + [VMEM] * 6,
        [pltpu.VMEM(sums, f32)],
    )(place, shift, moments, *result_parts, share, swapped(share))
    return (result, gram, pencil)


def solution(mesh):
    in_specs = (
        P(("groups", "slab"), None, "vec"),
        P("groups", None, "vec"),
        P(("groups", "slab"), None),
        P(("groups", "slab"), None),
        P(("groups", "slab"), None),
        P(None, ("groups", "slab"), None, "vec"),
        P(None, ("groups", "slab"), None, "vec"),
        P(("groups", "slab"), None, "vec"),
        P("groups"),
        P("groups"),
    )
    out_specs = (P(("groups", "slab"), None, "vec"), P("groups", None), P("groups", None))
    return jax.shard_map(
        on_device, mesh=mesh, in_specs=in_specs, out_specs=out_specs, check_vma=False
    )
```

```python
import functools

import jax
import jax.numpy as jnp
from jax import lax
from jax.experimental import pallas as pl
from jax.experimental.pallas import tpu as pltpu
from jax.sharding import PartitionSpec as P

f32, bf16 = jnp.float32, jnp.bfloat16
CHAIN = ("slab", "vec")
ANY = pl.BlockSpec(memory_space=pl.ANY)
VMEM = pl.BlockSpec(memory_space=pltpu.VMEM)
SMEM = pl.BlockSpec(memory_space=pltpu.SMEM)
SWAP = [(0, 1), (1, 0)]
MIB = 1024 * 1024


def kernel_call(body, out_shape, in_specs, scratch=(), vmem=16 * MIB, flops=0, size=0):
    return pl.pallas_call(
        body,
        out_shape=out_shape,
        in_specs=in_specs,
        out_specs=jax.tree.map(lambda _: VMEM, out_shape),
        scratch_shapes=list(scratch),
        compiler_params=pltpu.CompilerParams(vmem_limit_bytes=vmem),
        cost_estimate=pl.CostEstimate(flops=flops, bytes_accessed=size, transcendentals=0),
    )


def struct(shape, dtype=bf16):
    return jax.ShapeDtypeStruct(shape, dtype)


def dot(rows, matrix):
    return jnp.dot(rows, matrix, preferred_element_type=f32)


def dot_t(left, right):
    return lax.dot_general(left, right, (((1,), (1,)), ((), ())), preferred_element_type=f32)


def columns(index, width):
    return pl.ds(pl.multiple_of(index * width, width), width)


def in_vmem(operand):
    return pltpu.with_memory_space_constraint(operand, pltpu.VMEM)


def in_hbm(operand):
    return pltpu.with_memory_space_constraint(operand, pltpu.HBM)


def run(copies):
    for copy in copies:
        copy.start()
    for copy in copies:
        copy.wait()


def through(parts, held, outs, sem):
    ins = [pltpu.make_async_copy(part, held.at[k], sem.at[0, k]) for k, part in enumerate(parts)]
    outs = [pltpu.make_async_copy(held.at[k], out, sem.at[1, k]) for k, out in enumerate(outs)]
    return ins, outs


def finish(ins, outs, others):
    for copy, following in zip(ins, outs):
        copy.wait()
        following.start()
    for copy in others + outs:
        copy.wait()


def prepare_body(place, lower, upper, blocks, held_blocks, first, second, held, sem, block_sem):
    count = held.shape[1]
    slabs = pl.ds((1 - place[0]) * count, count)
    parts = [ref.at[level, slabs] for level in range(3) for ref in (lower, upper)]
    outs = [first.at[k] for k in range(2)] + [second.at[k] for k in range(4)]
    ins, outs = through(parts, held, outs, sem)
    whole = pltpu.make_async_copy(blocks, held_blocks, block_sem.at[0])
    for copy in ins + [whole]:
        copy.start()
    finish(ins, outs, [whole])


def prepare(place, lower, upper, blocks):
    _, slabs, rows, half = lower.shape
    shape = (slabs // 2, rows, half)
    size = 2 * slabs * rows * half
    return pl.pallas_call(
        prepare_body,
        out_shape=[
            pltpu.VMEM(blocks.shape, bf16),
            pltpu.HBM((2,) + shape, bf16),
            pltpu.HBM((4,) + shape, bf16),
        ],
        in_specs=[SMEM] + [ANY] * 3,
        out_specs=[VMEM, ANY, ANY],
        scratch_shapes=[
            pltpu.VMEM((6,) + shape, bf16),
            pltpu.SemaphoreType.DMA((2, 6)),
            pltpu.SemaphoreType.DMA((1,)),
        ],
        compiler_params=pltpu.CompilerParams(vmem_limit_bytes=10 * MIB),
        cost_estimate=pl.CostEstimate(
            flops=0, bytes_accessed=2 * blocks.size + 6 * size, transcendentals=0
        ),
    )(place, *[in_hbm(x) for x in (lower, upper, blocks)])


def load_and_pack_body(level, first, later, place, token, lower, upper, final, packed, weights, out, held, sem, pack_sem):
    count = weights.shape[2]
    slabs = pl.ds((1 - place[0]) * count, count)
    parts = [ref.at[each, slabs] for each in later for ref in (lower, upper)] + [final.at[slabs]]
    ins, outs = through(parts, held, [out.at[k] for k in range(len(parts))], pack_sem)
    loads = level_copies(level, first, place, lower, upper, packed, weights, sem)
    for copy in ins + loads:
        copy.start()
    finish(ins, outs, loads)


def load_and_pack(level, first, later, place, token, lower, upper, final, packed):
    _, slabs, rows, half = lower.shape
    shape = (2, 2, slabs // 2, rows, half)
    count = 2 * len(later) + 1
    later_shape = (count,) + shape[2:]
    return pl.pallas_call(
        functools.partial(load_and_pack_body, level, first, later),
        out_shape=[pltpu.VMEM(shape, bf16), pltpu.HBM(later_shape, bf16)],
        in_specs=[SMEM] + [ANY] * 5,
        out_specs=[VMEM, ANY],
        scratch_shapes=[
            pltpu.VMEM(later_shape, bf16),
            pltpu.SemaphoreType.DMA((2, 2)),
            pltpu.SemaphoreType.DMA((2, count)),
        ],
        compiler_params=pltpu.CompilerParams(vmem_limit_bytes=8 * MIB),
        cost_estimate=pl.CostEstimate(
            flops=0, bytes_accessed=(8 + 4 * count) * slabs * rows * half // 2, transcendentals=0
        ),
    )(place, token, *[in_hbm(x) for x in (lower, upper, final)], packed)


def level_copies(level, first, place, lower, upper, packed, weights, sem):
    count = weights.shape[2]
    slabs = pl.ds(place[0] * count, count)
    copies = []
    for side, ref in enumerate((lower, upper)):
        sources = (ref.at[level, slabs], packed.at[2 * (level - first) + side])
        for part, source in enumerate(sources):
            copies.append(pltpu.make_async_copy(source, weights.at[side, part], sem.at[side, part]))
    return copies


def load_body(level, first, place, token, lower, upper, packed, weights, sem):
    run(level_copies(level, first, place, lower, upper, packed, weights, sem))


def load_last_body(level, first, place, token, lower, upper, packed, final, weights, sem):
    count = weights.shape[2]
    slabs = pl.ds(place[0] * count, count)
    above = 1 - place[1 + level]

    def copy(source, side, part):
        return pltpu.make_async_copy(source, weights.at[side, part], sem.at[side, part])

    pl.when(above == 1)(lambda: copy(upper.at[level, slabs], 0, 0).start())
    pl.when(above == 0)(lambda: copy(lower.at[level, slabs], 0, 0).start())
    others = [
        copy(packed.at[2 * (level - first) + above], 0, 1),
        copy(final.at[slabs], 1, 0),
        copy(packed.at[packed.shape[0] - 1], 1, 1),
    ]
    for each in others:
        each.start()
    copy(lower.at[level, slabs], 0, 0).wait()
    for each in others:
        each.wait()


def load(body, place, token, lower, upper, packed, *finals):
    _, slabs, rows, half = lower.shape
    shape = (2, 2, slabs // 2, rows, half)
    operands = [in_hbm(lower), in_hbm(upper), packed] + [in_hbm(x) for x in finals]
    return pl.pallas_call(
        body,
        out_shape=pltpu.VMEM(shape, bf16),
        in_specs=[SMEM] + [ANY] * (1 + len(operands)),
        out_specs=VMEM,
        scratch_shapes=[pltpu.SemaphoreType.DMA((2, 2))],
        compiler_params=pltpu.CompilerParams(vmem_limit_bytes=4 * MIB),
        cost_estimate=pl.CostEstimate(flops=0, bytes_accessed=8 * slabs * rows * half, transcendentals=0),
    )(place, token, *operands)


def load_whole_body(place, token, source, target, sem):
    run([pltpu.make_async_copy(source, target, sem.at[0])])


def load_whole(place, token, array):
    return pl.pallas_call(
        load_whole_body,
        out_shape=pltpu.VMEM(array.shape, array.dtype),
        in_specs=[SMEM, ANY, ANY],
        out_specs=VMEM,
        scratch_shapes=[pltpu.SemaphoreType.DMA((1,))],
        compiler_params=pltpu.CompilerParams(vmem_limit_bytes=6 * MIB),
        cost_estimate=pl.CostEstimate(flops=0, bytes_accessed=2 * array.size, transcendentals=0),
    )(place, token, in_hbm(array))


def image_body(place, table, extended, vectors, blocks, keep, send, moments, image):
    slabs, count, _ = vectors.shape
    reach = table.shape[1] // 2
    quotient, old = jnp.zeros((count, count), f32), jnp.zeros((count, count), f32)
    for slab in range(slabs):
        summed = None
        for entry in range(reach):
            rows = extended[table[slab, entry] + (slab + slabs)]
            term = dot(rows, blocks[table[slab, reach + entry]])
            summed = term if summed is None else summed + term
        rounded = summed.astype(bf16)
        image[slab] = rounded
        quotient = quotient + dot_t(vectors[slab], rounded)
        old = old + dot_t(vectors[slab], vectors[slab])
    moments[:, 0:count] = quotient
    moments[:, count : 2 * count] = old
    mine = slabs // 2
    keep[...] = image[pl.ds(place[0] * mine, mine)]
    send[...] = image[pl.ds((1 - place[0]) * mine, mine)]


def image_halves(place, table, extended, vectors, blocks):
    slabs, rows, half = vectors.shape
    part = struct((slabs // 2, rows, half))
    return kernel_call(
        image_body,
        (part, part, struct((rows, 2 * rows), f32)),
        [SMEM, SMEM, VMEM, VMEM, VMEM],
        [pltpu.VMEM((slabs, rows, half), bf16)],
        flops=14 * slabs * rows * 2 * half * half,
        size=2 * blocks.size,
    )(place, table, extended, vectors, blocks)


def both_parts(place, half):
    return columns(place[0], half), columns(1 - place[0], half)


def first_vectors_body(place, extended, weights, out):
    count, half = out.shape[0], weights.shape[-1]
    first = extended.shape[0] // 3 + count * place[0]
    for part, cols in enumerate(both_parts(place, half)):
        for slab in range(count):
            own = first + slab
            summed = dot(extended[own - 1], weights[0, part, slab])
            summed = summed + dot(extended[own + 1], weights[1, part, slab])
            out[slab, :, cols] = (extended[own, :, cols].astype(f32) - summed).astype(bf16)


def first_body(place, image, inner, outer, vectors, weights, out):
    count, rows, _ = image.shape
    half = weights.shape[-1]
    odd = place[0] == 1
    below = [jnp.where(odd, inner[0], outer[0])] + [image[slab] for slab in range(count - 1)]
    above = [image[slab] for slab in range(1, count)] + [jnp.where(odd, outer[0], inner[0])]
    for slab in range(count):
        out[slab, rows : 2 * rows] = vectors[slab]
    for part, cols in enumerate(both_parts(place, half)):
        for slab in range(count):
            summed = dot(below[slab], weights[0, part, slab]) + dot(above[slab], weights[1, part, slab])
            out[slab, 0:rows, cols] = (image[slab, :, cols].astype(f32) - summed).astype(bf16)


def reduce_rows(place, own, partners, sides, weights, out):
    for part, cols in enumerate(both_parts(place, weights.shape[-1])):
        for slab in range(own.shape[0]):
            summed = None
            for side, rows in zip(sides, partners):
                term = dot(rows[slab], weights[side, part, slab])
                summed = term if summed is None else summed + term
            out[slab, :, cols] = (own[slab, :, cols].astype(f32) - summed).astype(bf16)


def second_body(place, own, inner, outer, weights, moments, note, out, lifted):
    count, rows, _ = out.shape
    lifted[count * rows :] = note[...]
    high = moments[:, 0:rows].astype(bf16)
    low = (moments[:, 0:rows] - high.astype(f32)).astype(bf16)
    factors = (high.T, low.T)
    for part, cols in enumerate(both_parts(place, weights.shape[-1])):
        for slab in range(count):
            summed = dot(inner[slab], weights[1 - place[0], part, slab])
            summed = summed + dot(outer[slab], weights[place[0], part, slab])
            both = own[slab, :, cols].astype(f32) - summed
            image, vectors = both[:rows], both[rows:].astype(bf16)
            for factor in factors:
                image = image - dot(factor, vectors)
            out[slab, :, cols] = image.astype(bf16)
            lifted[slab * rows : (slab + 1) * rows, cols] = image.astype(bf16)


def level_body(place, own, below, above, weights, out):
    reduce_rows(place, own, (below, above), (0, 1), weights, out)


def third_body(place, own, lifted, above, weights, out):
    count, rows, _ = own.shape
    below = [lifted[slab * rows : (slab + 1) * rows] for slab in range(count)]
    reduce_rows(place, own, (below, above), (0, 1), weights, out)


def product(place, rows, weights, whole, targets):
    for part, cols in enumerate(both_parts(place, weights.shape[-1])):
        for slab in range(whole.shape[0]):
            result = dot(rows[slab], weights[part, slab]).astype(bf16)
            targets[part][slab] = result
            whole[slab, :, cols] = result


def last_body(place, own, other, weights, whole, keep, send, rows):
    reduce_rows(place, own, (other,), (0,), weights, rows)
    product(place, rows, weights.at[1], whole, (keep, send))


def final_body(place, own, final, packed, whole, keep, send, weights, sem):
    count = own.shape[0]
    sources = (final.at[pl.ds(place[0] * count, count)], packed.at[packed.shape[0] - 1])
    run([
        pltpu.make_async_copy(source, weights.at[part], sem.at[part])
        for part, source in enumerate(sources)
    ])
    product(place, own, weights, whole, (keep, send))


def level_flops(operand, products):
    return 2 * products * operand.size * operand.shape[-1]


def add_pairs(place, table, targets, inside, window, blocks, others, summed):
    half = blocks.shape[-1]
    reach = table.shape[1] // 2
    first = place[0] * 2
    mine, theirs = columns(place[0], half), columns(1 - place[0], half)
    for target in targets:

        @pl.loop(0, reach)
        def _(entry):
            source = target + table[first + target, entry]

            @pl.when(inside(source))
            def _():
                block = table[first + target, reach + entry]
                vectors = window(source)
                summed[target, :, mine] += dot(vectors, blocks[block])
                summed[target, :, theirs] += dot(vectors, others[block])


def own_pairs_body(place, table, levels, index, extended, image, correction, blocks, others, summed, out, shift):
    own, rows, _ = image.shape
    below = extended.shape[0] // 3
    first = place[0] * own
    shift[...] = jnp.full(shift.shape, levels[index[0]], f32)
    summed[...] = jnp.zeros(summed.shape, f32)
    add_pairs(
        place, table, range(below + own),
        lambda source: jnp.logical_and(source >= below, source < below + own),
        lambda source: correction[source - below], blocks, others, summed,
    )
    overlap = jnp.zeros((2 * rows, rows), f32)
    mixed = jnp.zeros((rows, rows), f32)
    for slab in range(own):
        vectors, fixed = extended[first + below + slab], correction[slab]
        overlap = overlap + dot_t(jnp.concatenate([vectors, fixed], 0), fixed)
        mixed = mixed + dot_t(fixed, image[slab])
    out[0 : 2 * rows, 0:rows] = jnp.zeros((2 * rows, rows), f32)
    out[0 : 2 * rows, rows : 2 * rows] = overlap
    out[2 * rows :, 0:rows] = mixed[: rows // 2]
    out[2 * rows :, rows : 2 * rows] = mixed[rows // 2 :]


def cross_pairs_body(
    place, table, extended, correction, near, far, blocks, others, begun, part, keep, send, window, summed, out
):
    own, rows, _ = correction.shape
    below = window.shape[0]
    first = place[0] * own
    window[0:own] = far[...]
    window[own : 2 * own] = near[...]
    summed[below : below + own] = begun[below : below + own]
    add_pairs(
        place, table, range(below, below + own),
        lambda source: jnp.logical_and(source >= 0, source < below),
        lambda source: window[source], blocks, others, summed,
    )
    pencil = jnp.zeros((2 * rows, rows), f32)
    for slab in range(below + own):
        fixed = window[slab] if slab < below else correction[slab - below]
        terms = begun[slab] if slab < below else summed[slab]
        basis = jnp.concatenate([extended[first + slab], fixed], 0)
        pencil = pencil + dot_t(basis, terms.astype(bf16))
    out[...] = part[...]
    out[0 : 2 * rows, 0:rows] = pencil
    keep[...] = out[row_half(place[0], keep)]
    send[...] = out[row_half(1 - place[0], keep)]


def row_half(index, part):
    return pl.ds(pl.multiple_of(index * part.shape[0], 8), part.shape[0])


def assemble_body(scale, place, shift, moments, keep, received, first, second, gram, pencil, result, whole):
    rows = moments.shape[0]
    own = keep.shape[0]
    result[pl.ds(place[0] * own, own)] = keep[...]
    result[pl.ds((1 - place[0]) * own, own)] = received[...]
    whole[row_half(place[0], first)] = first[...] * scale
    whole[row_half(1 - place[0], first)] = second[...] * scale
    top, bottom = whole[0 : 2 * rows], whole[2 * rows :]
    overlap = top[:, rows:]
    mixed = jnp.concatenate([bottom[:, :rows], bottom[:, rows:]], 0)
    left = jnp.concatenate([moments[:, rows:], overlap[:rows].T], 0)
    product = jnp.concatenate([left, overlap], 1)
    gram[...] = product
    projected = jnp.concatenate([jnp.concatenate([moments[:, :rows], mixed], 0), top[:, :rows]], 1)
    pencil[...] = projected - shift[0:1] * product


def swapped(operand):
    return lax.ppermute(operand, "vec", SWAP)


def along(operand, axis, distance):
    count = lax.axis_size("slab") * (2 if axis == CHAIN else 1)
    route = [(i, i + distance) for i in range(count) if 0 <= i + distance < count]
    return lax.ppermute(operand, axis, route)


def pair_routes(distance):
    chain = 2 * lax.axis_size("slab")
    routes = []
    for bit in range(2):
        ups = [(i, i + distance) for i in range(chain - distance) if i // distance % 2 == bit]
        routes.append(ups + [(j, i) for i, j in ups])
    return [route for route in routes if route]


def summed_up(parts):
    while len(parts) > 1:
        parts = [a + b for a, b in zip(parts[::2], parts[1::2])]
    return parts[0]


def slab_total(part):
    slabs = lax.axis_size("slab")
    reach = 1
    while reach < slabs:
        radix = min(8, slabs // reach)
        routes = [[(i, i ^ (offset * reach)) for i in range(slabs)] for offset in range(1, radix)]
        part = summed_up([part] + [lax.ppermute(part, "slab", route) for route in routes])
        reach *= radix
    return part


def on_device(
    vectors,
    blocks,
    slab_blocks,
    far_source,
    far_block,
    level_lower,
    level_upper,
    level_final,
    shift_levels,
    shift_index,
):
    slab_count, rows, half = vectors.shape
    own_count = slab_count // 2
    slabs = lax.axis_size("slab")
    chain = 2 * slabs
    width = blocks.shape[1]
    rows_total = slab_count * slabs * width
    levels = [l for l in range(level_lower.shape[0]) if 2**l < slab_count * slabs]
    slab, core = lax.axis_index("slab"), lax.axis_index("vec")
    link = 2 * slab + core
    steps = [max(2**l // own_count, 1) for l in levels]
    place = jnp.stack([core] + [link // step % 2 for step in steps]).astype(jnp.int32)

    below, above = along(vectors, "slab", 1), along(vectors, "slab", -1)
    slab_ids = slab * slab_count + jnp.arange(slab_count, dtype=jnp.int32)[:, None]
    near = jnp.broadcast_to(jnp.arange(-1, 2, dtype=jnp.int32), (slab_count, 3))
    table = jnp.concatenate([near, far_source - slab_ids, slab_blocks, far_block], 1)
    note = jnp.pad(table.astype(bf16), ((0, 16 - slab_count), (0, width - table.shape[1])))
    held_blocks, theirs_0, theirs = prepare(place, level_lower, level_upper, blocks)
    extended = lax.all_gather(jnp.concatenate([below, vectors, above], 0), "vec", axis=2, tiled=True)
    theirs_0, extended = lax.optimization_barrier((theirs_0, extended))
    packed_0 = swapped(theirs_0)
    keep, send, moments = image_halves(place, table, extended, vectors, in_vmem(held_blocks))
    received, moments = swapped(send), moments + swapped(moments)
    image = jnp.where(core == 0, jnp.concatenate([keep, received], 2), jnp.concatenate([received, keep], 2))
    image, moments, theirs = lax.optimization_barrier((image, moments, theirs))
    packed = swapped(theirs)

    inner_route, outer_route = pair_routes(1)
    outer = lax.ppermute(lax.dynamic_slice_in_dim(image, (own_count - 1) * core, 1), CHAIN, outer_route)
    inner = swapped(lax.dynamic_slice_in_dim(image, (own_count - 1) * (1 - core), 1))
    flips = [[(i, i ^ 2**bit) for i in range(slabs)] for bit in range((slabs - 1).bit_length())]
    received = lax.ppermute(moments, "slab", flips[0])
    body = functools.partial(load_body, 0, 0)
    matrices = in_vmem(load(body, place, keep, level_lower, level_upper, packed_0))
    vectors_1 = kernel_call(
        first_vectors_body,
        struct(image.shape),
        [SMEM] + [VMEM] * 2,
        flops=level_flops(image, 2),
    )(place, extended, matrices)
    both = kernel_call(
        first_body,
        struct((own_count, 2 * rows, width)),
        [SMEM] + [VMEM] * 5,
        flops=level_flops(image, 2),
    )(place, image, inner, outer, vectors_1, matrices)
    both, received, late_blocks, packed = lax.optimization_barrier((both, received, blocks, packed))
    others = swapped(late_blocks)
    outer, inner = lax.ppermute(both, CHAIN, outer_route), swapped(both)
    for flip in flips[1:]:
        moments = moments + received
        received = lax.ppermute(moments, "slab", flip)
    moments = (moments + received) / rows_total
    matrices, theirs = load_and_pack(
        1, 1, levels[3:], place, both, level_lower, level_upper, level_final, packed
    )
    matrices = in_vmem(matrices)
    theirs, inner, outer, moments = lax.optimization_barrier((theirs, inner, outer, moments))
    following = swapped(theirs)
    residual, lifted = kernel_call(
        second_body,
        (struct(image.shape), struct((own_count * rows + 16, width))),
        [SMEM] + [VMEM] * 6,
        flops=level_flops(both, 2),
    )(place, both, inner, outer, matrices, moments, note)

    part = struct((own_count, rows, half))
    ends = (struct(residual.shape), part, part)
    one_partner = chain == 2 * steps[-1]
    for level, step in zip(levels[2:], steps[2:]):
        last = level == levels[-1]
        if last:
            held_blocks = load_whole(place, residual, blocks)
        if last and one_partner:
            body = functools.partial(load_last_body, level, 3)
            matrices = load(body, place, residual, level_lower, level_upper, packed, level_final)
            (route,) = pair_routes(step)
            other = lax.ppermute(residual, CHAIN, route)
            other, held_blocks = lax.optimization_barrier((other, held_blocks))
            correction, keep, send = kernel_call(
                last_body,
                ends,
                [SMEM] + [VMEM] * 3,
                [pltpu.VMEM(residual.shape, bf16)],
                flops=level_flops(residual, 2),
            )(place, residual, other, in_vmem(matrices))
            break
        body = functools.partial(load_body, level, 1 if level == 2 else 3)
        matrices = load(body, place, residual, level_lower, level_upper, packed)
        below, above = along(residual if level > 2 else lifted, CHAIN, step), along(residual, CHAIN, -step)
        if level == 2:
            count = own_count * rows
            lower_table = below[count : count + slab_count, : table.shape[1]].astype(jnp.int32)
            packed, below, above = lax.optimization_barrier((following, below, above))
        if level == 3:
            below, above, matrices = lax.optimization_barrier((below, above, matrices))
        residual = kernel_call(
            level_body if level > 2 else third_body,
            struct(residual.shape),
            [SMEM] + [VMEM] * 4,
            flops=level_flops(residual, 2),
        )(place, residual, below, above, in_vmem(matrices))
    if not one_partner:
        correction, keep, send = kernel_call(
            final_body,
            ends,
            [SMEM, VMEM, ANY, ANY],
            [pltpu.VMEM((2, own_count, width, half), bf16), pltpu.SemaphoreType.DMA((2,))],
            flops=level_flops(residual, 1),
        )(place, residual, in_hbm(level_final), packed)
    held_blocks, others = in_vmem(held_blocks), in_vmem(others)

    far, near = along(correction, CHAIN, 2), along(correction, CHAIN, 1)
    received = swapped(send)
    result_parts = (keep, received)
    tables = jnp.concatenate([lower_table, table], 0)
    flops = level_flops(image, 7)
    sums = (5 * rows // 2, 2 * rows)
    begun, part, shift = kernel_call(
        own_pairs_body,
        (struct((3 * own_count, rows, width), f32), struct(sums, f32), struct((8, 2 * rows), f32)),
        [SMEM] * 4 + [VMEM] * 5,
        flops=flops,
    )(place, tables, shift_levels, shift_index, extended, image, correction, held_blocks, others)
    share = struct((sums[0] // 2, sums[1]), f32)
    keep, send = kernel_call(
        cross_pairs_body,
        (share, share),
        [SMEM] * 2 + [VMEM] * 8,
        [
            pltpu.VMEM((2 * own_count, rows, width), bf16),
            pltpu.VMEM((3 * own_count, rows, width), f32),
            pltpu.VMEM(sums, f32),
        ],
        flops=flops,
    )(place, tables, extended, correction, near, far, held_blocks, others, begun, part)
    share = slab_total(keep + swapped(send))
    square = struct((2 * rows, 2 * rows), f32)
    gram, pencil, result = kernel_call(
        functools.partial(assemble_body, 1.0 / rows_total),
        (square, square, struct(vectors.shape)),
        [SMEM] + [VMEM] * 6,
        [pltpu.VMEM(sums, f32)],
    )(place, shift, moments, *result_parts, share, swapped(share))
    return (result, gram, pencil)


def solution(mesh):
    in_specs = (
        P(("groups", "slab"), None, "vec"),
        P("groups", None, "vec"),
        P(("groups", "slab"), None),
        P(("groups", "slab"), None),
        P(("groups", "slab"), None),
        P(None, ("groups", "slab"), None, "vec"),
        P(None, ("groups", "slab"), None, "vec"),
        P(("groups", "slab"), None, "vec"),
        P("groups"),
        P("groups"),
    )
    out_specs = (P(("groups", "slab"), None, "vec"), P("groups", None), P("groups", None))
    return jax.shard_map(
        on_device, mesh=mesh, in_specs=in_specs, out_specs=out_specs, check_vma=False
    )
```

```python
import functools

import jax
import jax.numpy as jnp
from jax import lax
from jax.experimental import pallas as pl
from jax.experimental.pallas import tpu as pltpu
from jax.sharding import PartitionSpec as P

f32, bf16 = jnp.float32, jnp.bfloat16
CHAIN = ("slab", "vec")
ANY = pl.BlockSpec(memory_space=pl.ANY)
VMEM = pl.BlockSpec(memory_space=pltpu.VMEM)
SMEM = pl.BlockSpec(memory_space=pltpu.SMEM)
SWAP = [(0, 1), (1, 0)]
MIB = 1024 * 1024


def kernel_call(body, out_shape, in_specs, scratch=(), vmem=16 * MIB, flops=0, size=0):
    return pl.pallas_call(
        body,
        out_shape=out_shape,
        in_specs=in_specs,
        out_specs=jax.tree.map(lambda _: VMEM, out_shape),
        scratch_shapes=list(scratch),
        compiler_params=pltpu.CompilerParams(vmem_limit_bytes=vmem),
        cost_estimate=pl.CostEstimate(flops=flops, bytes_accessed=size, transcendentals=0),
    )


def struct(shape, dtype=bf16):
    return jax.ShapeDtypeStruct(shape, dtype)


def dot(rows, matrix):
    return jnp.dot(rows, matrix, preferred_element_type=f32)


def dot_t(left, right):
    return lax.dot_general(left, right, (((1,), (1,)), ((), ())), preferred_element_type=f32)


def columns(index, width):
    return pl.ds(pl.multiple_of(index * width, width), width)


def in_vmem(operand):
    return pltpu.with_memory_space_constraint(operand, pltpu.VMEM)


def in_hbm(operand):
    return pltpu.with_memory_space_constraint(operand, pltpu.HBM)


def run(copies):
    for copy in copies:
        copy.start()
    for copy in copies:
        copy.wait()


def through(parts, held, outs, sem):
    ins = [pltpu.make_async_copy(part, held.at[k], sem.at[0, k]) for k, part in enumerate(parts)]
    outs = [pltpu.make_async_copy(held.at[k], out, sem.at[1, k]) for k, out in enumerate(outs)]
    return ins, outs


def finish(ins, outs, others):
    for copy, following in zip(ins, outs):
        copy.wait()
        following.start()
    for copy in others + outs:
        copy.wait()


def prepare_body(place, lower, upper, blocks, held_blocks, first, second, held, sem, block_sem):
    count = held.shape[1]
    slabs = pl.ds((1 - place[0]) * count, count)
    parts = [ref.at[level, slabs] for level in range(3) for ref in (lower, upper)]
    outs = [first.at[k] for k in range(2)] + [second.at[k] for k in range(4)]
    ins, outs = through(parts, held, outs, sem)
    whole = pltpu.make_async_copy(blocks, held_blocks, block_sem.at[0])
    for copy in ins + [whole]:
        copy.start()
    finish(ins, outs, [whole])


def prepare(place, lower, upper, blocks):
    _, slabs, rows, half = lower.shape
    shape = (slabs // 2, rows, half)
    size = 2 * slabs * rows * half
    return pl.pallas_call(
        prepare_body,
        out_shape=[
            pltpu.VMEM(blocks.shape, bf16),
            pltpu.HBM((2,) + shape, bf16),
            pltpu.HBM((4,) + shape, bf16),
        ],
        in_specs=[SMEM] + [ANY] * 3,
        out_specs=[VMEM, ANY, ANY],
        scratch_shapes=[
            pltpu.VMEM((6,) + shape, bf16),
            pltpu.SemaphoreType.DMA((2, 6)),
            pltpu.SemaphoreType.DMA((1,)),
        ],
        compiler_params=pltpu.CompilerParams(vmem_limit_bytes=10 * MIB),
        cost_estimate=pl.CostEstimate(
            flops=0, bytes_accessed=2 * blocks.size + 6 * size, transcendentals=0
        ),
    )(place, *[in_hbm(x) for x in (lower, upper, blocks)])


def load_and_pack_body(level, first, later, place, token, lower, upper, final, packed, weights, out, held, sem, pack_sem):
    count = weights.shape[2]
    slabs = pl.ds((1 - place[0]) * count, count)
    parts = [ref.at[each, slabs] for each in later for ref in (lower, upper)] + [final.at[slabs]]
    ins, outs = through(parts, held, [out.at[k] for k in range(len(parts))], pack_sem)
    loads = level_copies(level, first, place, lower, upper, packed, weights, sem)
    for copy in ins + loads:
        copy.start()
    finish(ins, outs, loads)


def load_and_pack(level, first, later, place, token, lower, upper, final, packed):
    _, slabs, rows, half = lower.shape
    shape = (2, 2, slabs // 2, rows, half)
    count = 2 * len(later) + 1
    later_shape = (count,) + shape[2:]
    return pl.pallas_call(
        functools.partial(load_and_pack_body, level, first, later),
        out_shape=[pltpu.VMEM(shape, bf16), pltpu.HBM(later_shape, bf16)],
        in_specs=[SMEM] + [ANY] * 5,
        out_specs=[VMEM, ANY],
        scratch_shapes=[
            pltpu.VMEM(later_shape, bf16),
            pltpu.SemaphoreType.DMA((2, 2)),
            pltpu.SemaphoreType.DMA((2, count)),
        ],
        compiler_params=pltpu.CompilerParams(vmem_limit_bytes=8 * MIB),
        cost_estimate=pl.CostEstimate(
            flops=0, bytes_accessed=(8 + 4 * count) * slabs * rows * half // 2, transcendentals=0
        ),
    )(place, token, *[in_hbm(x) for x in (lower, upper, final)], packed)


def level_copies(level, first, place, lower, upper, packed, weights, sem):
    count = weights.shape[2]
    slabs = pl.ds(place[0] * count, count)
    copies = []
    for side, ref in enumerate((lower, upper)):
        sources = (ref.at[level, slabs], packed.at[2 * (level - first) + side])
        for part, source in enumerate(sources):
            copies.append(pltpu.make_async_copy(source, weights.at[side, part], sem.at[side, part]))
    return copies


def load_body(level, first, place, token, lower, upper, packed, weights, sem):
    run(level_copies(level, first, place, lower, upper, packed, weights, sem))


def load_last_body(level, first, place, token, lower, upper, packed, final, weights, sem):
    count = weights.shape[2]
    slabs = pl.ds(place[0] * count, count)
    above = 1 - place[1 + level]

    def copy(source, side, part):
        return pltpu.make_async_copy(source, weights.at[side, part], sem.at[side, part])

    pl.when(above == 1)(lambda: copy(upper.at[level, slabs], 0, 0).start())
    pl.when(above == 0)(lambda: copy(lower.at[level, slabs], 0, 0).start())
    others = [
        copy(packed.at[2 * (level - first) + above], 0, 1),
        copy(final.at[slabs], 1, 0),
        copy(packed.at[packed.shape[0] - 1], 1, 1),
    ]
    for each in others:
        each.start()
    copy(lower.at[level, slabs], 0, 0).wait()
    for each in others:
        each.wait()


def load(body, place, token, lower, upper, packed, *finals):
    _, slabs, rows, half = lower.shape
    shape = (2, 2, slabs // 2, rows, half)
    operands = [in_hbm(lower), in_hbm(upper), packed] + [in_hbm(x) for x in finals]
    return pl.pallas_call(
        body,
        out_shape=pltpu.VMEM(shape, bf16),
        in_specs=[SMEM] + [ANY] * (1 + len(operands)),
        out_specs=VMEM,
        scratch_shapes=[pltpu.SemaphoreType.DMA((2, 2))],
        compiler_params=pltpu.CompilerParams(vmem_limit_bytes=4 * MIB),
        cost_estimate=pl.CostEstimate(flops=0, bytes_accessed=8 * slabs * rows * half, transcendentals=0),
    )(place, token, *operands)


def load_whole_body(place, token, source, target, sem):
    run([pltpu.make_async_copy(source, target, sem.at[0])])


def load_whole(place, token, array):
    return pl.pallas_call(
        load_whole_body,
        out_shape=pltpu.VMEM(array.shape, array.dtype),
        in_specs=[SMEM, ANY, ANY],
        out_specs=VMEM,
        scratch_shapes=[pltpu.SemaphoreType.DMA((1,))],
        compiler_params=pltpu.CompilerParams(vmem_limit_bytes=6 * MIB),
        cost_estimate=pl.CostEstimate(flops=0, bytes_accessed=2 * array.size, transcendentals=0),
    )(place, token, in_hbm(array))


def image_body(place, table, extended, vectors, blocks, keep, send, moments, image):
    slabs, count, _ = vectors.shape
    reach = table.shape[1] // 2
    quotient, old = jnp.zeros((count, count), f32), jnp.zeros((count, count), f32)
    for slab in range(slabs):
        summed = None
        for entry in range(reach):
            rows = extended[table[slab, entry] + (slab + slabs)]
            term = dot(rows, blocks[table[slab, reach + entry]])
            summed = term if summed is None else summed + term
        rounded = summed.astype(bf16)
        image[slab] = rounded
        quotient = quotient + dot_t(vectors[slab], rounded)
        old = old + dot_t(vectors[slab], vectors[slab])
    moments[:, 0:count] = quotient
    moments[:, count : 2 * count] = old
    mine = slabs // 2
    keep[...] = image[pl.ds(place[0] * mine, mine)]
    send[...] = image[pl.ds((1 - place[0]) * mine, mine)]


def image_halves(place, table, extended, vectors, blocks):
    slabs, rows, half = vectors.shape
    part = struct((slabs // 2, rows, half))
    return kernel_call(
        image_body,
        (part, part, struct((rows, 2 * rows), f32)),
        [SMEM, SMEM, VMEM, VMEM, VMEM],
        [pltpu.VMEM((slabs, rows, half), bf16)],
        flops=14 * slabs * rows * 2 * half * half,
        size=2 * blocks.size,
    )(place, table, extended, vectors, blocks)


def both_parts(place, half):
    return columns(place[0], half), columns(1 - place[0], half)


def first_vectors_body(place, extended, weights, out):
    count, half = out.shape[0], weights.shape[-1]
    first = extended.shape[0] // 3 + count * place[0]
    for part, cols in enumerate(both_parts(place, half)):
        for slab in range(count):
            own = first + slab
            summed = dot(extended[own - 1], weights[0, part, slab])
            summed = summed + dot(extended[own + 1], weights[1, part, slab])
            out[slab, :, cols] = (extended[own, :, cols].astype(f32) - summed).astype(bf16)


def first_body(place, image, inner, outer, vectors, weights, out):
    count, rows, _ = image.shape
    half = weights.shape[-1]
    odd = place[0] == 1
    below = [jnp.where(odd, inner[0], outer[0])] + [image[slab] for slab in range(count - 1)]
    above = [image[slab] for slab in range(1, count)] + [jnp.where(odd, outer[0], inner[0])]
    for slab in range(count):
        out[slab, rows : 2 * rows] = vectors[slab]
    for part, cols in enumerate(both_parts(place, half)):
        for slab in range(count):
            summed = dot(below[slab], weights[0, part, slab]) + dot(above[slab], weights[1, part, slab])
            out[slab, 0:rows, cols] = (image[slab, :, cols].astype(f32) - summed).astype(bf16)


def reduce_rows(place, own, partners, sides, weights, out):
    for part, cols in enumerate(both_parts(place, weights.shape[-1])):
        for slab in range(own.shape[0]):
            summed = None
            for side, rows in zip(sides, partners):
                term = dot(rows[slab], weights[side, part, slab])
                summed = term if summed is None else summed + term
            out[slab, :, cols] = (own[slab, :, cols].astype(f32) - summed).astype(bf16)


def second_body(place, own, inner, outer, weights, moments, note, out, lifted):
    count, rows, _ = out.shape
    lifted[count * rows :] = note[...]
    high = moments[:, 0:rows].astype(bf16)
    low = (moments[:, 0:rows] - high.astype(f32)).astype(bf16)
    factors = (high.T, low.T)
    for part, cols in enumerate(both_parts(place, weights.shape[-1])):
        for slab in range(count):
            summed = dot(inner[slab], weights[1 - place[0], part, slab])
            summed = summed + dot(outer[slab], weights[place[0], part, slab])
            both = own[slab, :, cols].astype(f32) - summed
            image, vectors = both[:rows], both[rows:].astype(bf16)
            for factor in factors:
                image = image - dot(factor, vectors)
            out[slab, :, cols] = image.astype(bf16)
            lifted[slab * rows : (slab + 1) * rows, cols] = image.astype(bf16)


def level_body(place, own, below, above, weights, out):
    reduce_rows(place, own, (below, above), (0, 1), weights, out)


def third_body(place, own, lifted, above, weights, out):
    count, rows, _ = own.shape
    below = [lifted[slab * rows : (slab + 1) * rows] for slab in range(count)]
    reduce_rows(place, own, (below, above), (0, 1), weights, out)


def product(place, rows, weights, whole, targets):
    for part, cols in enumerate(both_parts(place, weights.shape[-1])):
        for slab in range(whole.shape[0]):
            result = dot(rows[slab], weights[part, slab]).astype(bf16)
            targets[part][slab] = result
            whole[slab, :, cols] = result


def last_body(place, own, other, weights, whole, keep, send, rows):
    reduce_rows(place, own, (other,), (0,), weights, rows)
    product(place, rows, weights.at[1], whole, (keep, send))


def final_body(place, own, final, packed, whole, keep, send, weights, sem):
    count = own.shape[0]
    sources = (final.at[pl.ds(place[0] * count, count)], packed.at[packed.shape[0] - 1])
    run([
        pltpu.make_async_copy(source, weights.at[part], sem.at[part])
        for part, source in enumerate(sources)
    ])
    product(place, own, weights, whole, (keep, send))


def level_flops(operand, products):
    return 2 * products * operand.size * operand.shape[-1]


def add_pairs(place, table, targets, inside, window, blocks, others, summed):
    half = blocks.shape[-1]
    reach = table.shape[1] // 2
    first = place[0] * 2
    mine, theirs = columns(place[0], half), columns(1 - place[0], half)
    for target in targets:

        @pl.loop(0, reach)
        def _(entry):
            source = target + table[first + target, entry]

            @pl.when(inside(source))
            def _():
                block = table[first + target, reach + entry]
                vectors = window(source)
                summed[target, :, mine] += dot(vectors, blocks[block])
                summed[target, :, theirs] += dot(vectors, others[block])


def own_pairs_body(place, table, levels, index, extended, image, correction, blocks, others, summed, out, shift):
    own, rows, _ = image.shape
    below = extended.shape[0] // 3
    first = place[0] * own
    shift[...] = jnp.full(shift.shape, levels[index[0]], f32)
    summed[...] = jnp.zeros(summed.shape, f32)
    add_pairs(
        place, table, range(below + own),
        lambda source: jnp.logical_and(source >= below, source < below + own),
        lambda source: correction[source - below], blocks, others, summed,
    )
    overlap = jnp.zeros((2 * rows, rows), f32)
    mixed = jnp.zeros((rows, rows), f32)
    for slab in range(own):
        vectors, fixed = extended[first + below + slab], correction[slab]
        overlap = overlap + dot_t(jnp.concatenate([vectors, fixed], 0), fixed)
        mixed = mixed + dot_t(fixed, image[slab])
    out[0 : 2 * rows, 0:rows] = jnp.zeros((2 * rows, rows), f32)
    out[0 : 2 * rows, rows : 2 * rows] = overlap
    out[2 * rows :, 0:rows] = mixed[: rows // 2]
    out[2 * rows :, rows : 2 * rows] = mixed[rows // 2 :]


def cross_pairs_body(
    place, table, extended, correction, near, far, blocks, others, begun, part, keep, send, window, summed, out
):
    own, rows, _ = correction.shape
    below = window.shape[0]
    first = place[0] * own
    window[0:own] = far[...]
    window[own : 2 * own] = near[...]
    summed[below : below + own] = begun[below : below + own]
    add_pairs(
        place, table, range(below, below + own),
        lambda source: jnp.logical_and(source >= 0, source < below),
        lambda source: window[source], blocks, others, summed,
    )
    pencil = jnp.zeros((2 * rows, rows), f32)
    for slab in range(below + own):
        fixed = window[slab] if slab < below else correction[slab - below]
        terms = begun[slab] if slab < below else summed[slab]
        basis = jnp.concatenate([extended[first + slab], fixed], 0)
        pencil = pencil + dot_t(basis, terms.astype(bf16))
    out[...] = part[...]
    out[0 : 2 * rows, 0:rows] = pencil
    keep[...] = out[row_half(place[0], keep)]
    send[...] = out[row_half(1 - place[0], keep)]


def row_half(index, part):
    return pl.ds(pl.multiple_of(index * part.shape[0], 8), part.shape[0])


def assemble_body(scale, place, shift, moments, keep, received, first, second, gram, pencil, result, whole):
    rows = moments.shape[0]
    own = keep.shape[0]
    result[pl.ds(place[0] * own, own)] = keep[...]
    result[pl.ds((1 - place[0]) * own, own)] = received[...]
    whole[row_half(place[0], first)] = first[...] * scale
    whole[row_half(1 - place[0], first)] = second[...] * scale
    top, bottom = whole[0 : 2 * rows], whole[2 * rows :]
    overlap = top[:, rows:]
    mixed = jnp.concatenate([bottom[:, :rows], bottom[:, rows:]], 0)
    left = jnp.concatenate([moments[:, rows:], overlap[:rows].T], 0)
    product = jnp.concatenate([left, overlap], 1)
    gram[...] = product
    projected = jnp.concatenate([jnp.concatenate([moments[:, :rows], mixed], 0), top[:, :rows]], 1)
    pencil[...] = projected - shift[0:1] * product


def swapped(operand):
    return lax.ppermute(operand, "vec", SWAP)


def along(operand, axis, distance):
    count = lax.axis_size("slab") * (2 if axis == CHAIN else 1)
    route = [(i, i + distance) for i in range(count) if 0 <= i + distance < count]
    return lax.ppermute(operand, axis, route)


def pair_routes(distance):
    chain = 2 * lax.axis_size("slab")
    routes = []
    for bit in range(2):
        ups = [(i, i + distance) for i in range(chain - distance) if i // distance % 2 == bit]
        routes.append(ups + [(j, i) for i, j in ups])
    return [route for route in routes if route]


def summed_up(parts):
    while len(parts) > 1:
        parts = [a + b for a, b in zip(parts[::2], parts[1::2])]
    return parts[0]


def slab_total(part):
    slabs = lax.axis_size("slab")
    reach = 1
    while reach < slabs:
        radix = min(2, slabs // reach)
        routes = [[(i, i ^ (offset * reach)) for i in range(slabs)] for offset in range(1, radix)]
        part = summed_up([part] + [lax.ppermute(part, "slab", route) for route in routes])
        reach *= radix
    return part


def on_device(
    vectors,
    blocks,
    slab_blocks,
    far_source,
    far_block,
    level_lower,
    level_upper,
    level_final,
    shift_levels,
    shift_index,
):
    slab_count, rows, half = vectors.shape
    own_count = slab_count // 2
    slabs = lax.axis_size("slab")
    chain = 2 * slabs
    width = blocks.shape[1]
    rows_total = slab_count * slabs * width
    levels = [l for l in range(level_lower.shape[0]) if 2**l < slab_count * slabs]
    slab, core = lax.axis_index("slab"), lax.axis_index("vec")
    link = 2 * slab + core
    steps = [max(2**l // own_count, 1) for l in levels]
    place = jnp.stack([core] + [link // step % 2 for step in steps]).astype(jnp.int32)

    below, above = along(vectors, "slab", 1), along(vectors, "slab", -1)
    slab_ids = slab * slab_count + jnp.arange(slab_count, dtype=jnp.int32)[:, None]
    near = jnp.broadcast_to(jnp.arange(-1, 2, dtype=jnp.int32), (slab_count, 3))
    table = jnp.concatenate([near, far_source - slab_ids, slab_blocks, far_block], 1)
    note = jnp.pad(table.astype(bf16), ((0, 16 - slab_count), (0, width - table.shape[1])))
    held_blocks, theirs_0, theirs = prepare(place, level_lower, level_upper, blocks)
    extended = lax.all_gather(jnp.concatenate([below, vectors, above], 0), "vec", axis=2, tiled=True)
    theirs_0, extended = lax.optimization_barrier((theirs_0, extended))
    packed_0 = swapped(theirs_0)
    keep, send, moments = image_halves(place, table, extended, vectors, in_vmem(held_blocks))
    received, moments = swapped(send), moments + swapped(moments)
    image = jnp.where(core == 0, jnp.concatenate([keep, received], 2), jnp.concatenate([received, keep], 2))
    image, moments, theirs = lax.optimization_barrier((image, moments, theirs))
    packed = swapped(theirs)

    inner_route, outer_route = pair_routes(1)
    outer = lax.ppermute(lax.dynamic_slice_in_dim(image, (own_count - 1) * core, 1), CHAIN, outer_route)
    inner = swapped(lax.dynamic_slice_in_dim(image, (own_count - 1) * (1 - core), 1))
    flips = [[(i, i ^ 2**bit) for i in range(slabs)] for bit in range((slabs - 1).bit_length())]
    received = lax.ppermute(moments, "slab", flips[0])
    body = functools.partial(load_body, 0, 0)
    matrices = in_vmem(load(body, place, keep, level_lower, level_upper, packed_0))
    vectors_1 = kernel_call(
        first_vectors_body,
        struct(image.shape),
        [SMEM] + [VMEM] * 2,
        flops=level_flops(image, 2),
    )(place, extended, matrices)
    both = kernel_call(
        first_body,
        struct((own_count, 2 * rows, width)),
        [SMEM] + [VMEM] * 5,
        flops=level_flops(image, 2),
    )(place, image, inner, outer, vectors_1, matrices)
    both, received, late_blocks, packed = lax.optimization_barrier((both, received, blocks, packed))
    others = swapped(late_blocks)
    outer, inner = lax.ppermute(both, CHAIN, outer_route), swapped(both)
    for flip in flips[1:]:
        moments = moments + received
        received = lax.ppermute(moments, "slab", flip)
    moments = (moments + received) / rows_total
    matrices, theirs = load_and_pack(
        1, 1, levels[3:], place, both, level_lower, level_upper, level_final, packed
    )
    matrices = in_vmem(matrices)
    theirs, inner, outer, moments = lax.optimization_barrier((theirs, inner, outer, moments))
    following = swapped(theirs)
    residual, lifted = kernel_call(
        second_body,
        (struct(image.shape), struct((own_count * rows + 16, width))),
        [SMEM] + [VMEM] * 6,
        flops=level_flops(both, 2),
    )(place, both, inner, outer, matrices, moments, note)

    part = struct((own_count, rows, half))
    ends = (struct(residual.shape), part, part)
    one_partner = chain == 2 * steps[-1]
    for level, step in zip(levels[2:], steps[2:]):
        last = level == levels[-1]
        if last:
            held_blocks = load_whole(place, residual, blocks)
        if last and one_partner:
            body = functools.partial(load_last_body, level, 3)
            matrices = load(body, place, residual, level_lower, level_upper, packed, level_final)
            (route,) = pair_routes(step)
            other = lax.ppermute(residual, CHAIN, route)
            other, held_blocks = lax.optimization_barrier((other, held_blocks))
            correction, keep, send = kernel_call(
                last_body,
                ends,
                [SMEM] + [VMEM] * 3,
                [pltpu.VMEM(residual.shape, bf16)],
                flops=level_flops(residual, 2),
            )(place, residual, other, in_vmem(matrices))
            break
        body = functools.partial(load_body, level, 1 if level == 2 else 3)
        matrices = load(body, place, residual, level_lower, level_upper, packed)
        below, above = along(residual if level > 2 else lifted, CHAIN, step), along(residual, CHAIN, -step)
        if level == 2:
            count = own_count * rows
            lower_table = below[count : count + slab_count, : table.shape[1]].astype(jnp.int32)
            packed, below, above = lax.optimization_barrier((following, below, above))
        if level == 3:
            below, above, matrices = lax.optimization_barrier((below, above, matrices))
        residual = kernel_call(
            level_body if level > 2 else third_body,
            struct(residual.shape),
            [SMEM] + [VMEM] * 4,
            flops=level_flops(residual, 2),
        )(place, residual, below, above, in_vmem(matrices))
    if not one_partner:
        correction, keep, send = kernel_call(
            final_body,
            ends,
            [SMEM, VMEM, ANY, ANY],
            [pltpu.VMEM((2, own_count, width, half), bf16), pltpu.SemaphoreType.DMA((2,))],
            flops=level_flops(residual, 1),
        )(place, residual, in_hbm(level_final), packed)
    held_blocks, others = in_vmem(held_blocks), in_vmem(others)

    far, near = along(correction, CHAIN, 2), along(correction, CHAIN, 1)
    received = swapped(send)
    result_parts = (keep, received)
    tables = jnp.concatenate([lower_table, table], 0)
    flops = level_flops(image, 7)
    sums = (5 * rows // 2, 2 * rows)
    begun, part, shift = kernel_call(
        own_pairs_body,
        (struct((3 * own_count, rows, width), f32), struct(sums, f32), struct((8, 2 * rows), f32)),
        [SMEM] * 4 + [VMEM] * 5,
        flops=flops,
    )(place, tables, shift_levels, shift_index, extended, image, correction, held_blocks, others)
    share = struct((sums[0] // 2, sums[1]), f32)
    keep, send = kernel_call(
        cross_pairs_body,
        (share, share),
        [SMEM] * 2 + [VMEM] * 8,
        [
            pltpu.VMEM((2 * own_count, rows, width), bf16),
            pltpu.VMEM((3 * own_count, rows, width), f32),
            pltpu.VMEM(sums, f32),
        ],
        flops=flops,
    )(place, tables, extended, correction, near, far, held_blocks, others, begun, part)
    share = slab_total(keep + swapped(send))
    square = struct((2 * rows, 2 * rows), f32)
    gram, pencil, result = kernel_call(
        functools.partial(assemble_body, 1.0 / rows_total),
        (square, square, struct(vectors.shape)),
        [SMEM] + [VMEM] * 6,
        [pltpu.VMEM(sums, f32)],
    )(place, shift, moments, *result_parts, share, swapped(share))
    return (result, gram, pencil)


def solution(mesh):
    in_specs = (
        P(("groups", "slab"), None, "vec"),
        P("groups", None, "vec"),
        P(("groups", "slab"), None),
        P(("groups", "slab"), None),
        P(("groups", "slab"), None),
        P(None, ("groups", "slab"), None, "vec"),
        P(None, ("groups", "slab"), None, "vec"),
        P(("groups", "slab"), None, "vec"),
        P("groups"),
        P("groups"),
    )
    out_specs = (P(("groups", "slab"), None, "vec"), P("groups", None), P("groups", None))
    return jax.shard_map(
        on_device, mesh=mesh, in_specs=in_specs, out_specs=out_specs, check_vma=False
    )
```
